32 devices in a mesh: dp: 4 (over x, core), tensor: 8 (over z, y).
Axes of the slice: x: 2, y: 2, z: 4, core: 2. Of those that a mesh axis runs over, the one named last changes fastest.
Arguments:
- hidden_in: bfloat16 [8192, 2048], P('dp'), may hold values from -6 to 6
- cotangent: bfloat16 [8192, 2048], P('dp'), may hold values from -6 to 6
- routes: int32 [8192, 8], P('dp'), may hold values from 0 to 15, all different within a row
- segments: int32 [8, 1024], P('dp'), may hold values from 0 to 3, never falling along the last dimension, each value on 1 to 512 neighbouring positions
- gain_in: bfloat16 [2048], replicated, may hold values from 0.25 to 1.75
- w_query: bfloat16 [2048, 2048], P(None, 'tensor'), may hold values from -0.125 to 0.125
- w_key: bfloat16 [2048, 2048], P(None, 'tensor'), may hold values from -0.125 to 0.125
- w_value: bfloat16 [2048, 2048], P(None, 'tensor'), may hold values from -0.125 to 0.125
- w_out: bfloat16 [2048, 2048], P(None, 'tensor'), may hold values from -2 to 2
- gain_query: bfloat16 [2048], P('tensor'), may hold values from 0.25 to 1.75
- gain_key: bfloat16 [2048], P('tensor'), may hold values from 0.25 to 1.75
- gain_mid: bfloat16 [2048], replicated, may hold values from 0.25 to 1.75
- w_router: bfloat16 [2048, 16], replicated, may hold values from -0.0625 to 0.0625
- w_gate: bfloat16 [16, 2048, 1024], P(None, None, 'tensor'), may hold values from -0.125 to 0.125
- w_up: bfloat16 [16, 2048, 1024], P(None, None, 'tensor'), may hold values from -0.125 to 0.125
- w_down: bfloat16 [16, 2048, 1024], P(None, None, 'tensor'), may hold values from -1.5 to 1.5
Outputs:
- output: bfloat16 [8192, 2048], P('dp', 'tensor')
- grad_input: bfloat16 [8192, 2048], P('dp', 'tensor')
- grad_w_query: float32 [2048, 2048], P('dp', 'tensor')
- grad_w_key: float32 [2048, 2048], P('dp', 'tensor')
- grad_w_value: float32 [2048, 2048], P('dp', 'tensor')
- grad_w_out: float32 [2048, 2048], P('dp', 'tensor')
- grad_gain_in: float32 [2048], P('tensor')
- grad_gain_query: float32 [2048], P('tensor')
- grad_gain_key: float32 [2048], P('tensor')
- grad_gain_mid: float32 [2048], P('dp')
- grad_w_router: float32 [2048, 16], P('dp')
- grad_w_gate: float32 [16, 2048, 1024], P('dp', None, 'tensor')
- grad_w_up: float32 [16, 2048, 1024], P('dp', None, 'tensor')
- grad_w_down: float32 [16, 2048, 1024], P('dp', None, 'tensor')
The draws below stay inside these ranges and needn't reach their ends.
Inputs may be any that keep to these rules, and one draw needn't show every extreme that they name: `routes`: each row names 8 different experts; every expert is named by some row. `segments`: numbers never fall along a row; each document holds 1 to 512 tokens, and some document holds exactly that many.
All inputs are finite; a program needn't handle non-finite values.
Results may differ from the reference program's by a relative error of at most 0.015.
The reference program's roundings to bfloat16 on the way count: a program that leaves them out, or rounds other values in their place, can miss the bound.
Values sent between devices are 32-bit elements; how exact they have to be, the bound alone decides.
No kernel may reach another device: no remote copies, remote signals or barrier semaphores. Data moves between devices by JAX's collectives and lax.ppermute only.
A program may use at most 448 MiB of HBM per device.

```python
import math
import jax
import jax.numpy as jnp
import numpy as np
from jax import lax

D = 2048
HEADS = 16
HEAD = 128
FF = 1024
TOPK = 8
EXPERTS = 16
LEN = 1024
WINDOW = 1024
SEQS = 8
TOKENS = 8192
CAP = 1280
N_DP = 4


def block_scale(stream_key, extent, shards, smallest, high):
    def one(dim, parts):
        draws = jax.random.uniform(jax.random.fold_in(jax.random.fold_in(stream_key, 6), dim), (parts,), jnp.float32, smallest / len(shards), high / len(shards))
        return jnp.repeat(jnp.exp(draws), extent[dim] // parts).reshape((-1,) + (1,) * (len(extent) - dim - 1))

    factor_of = one(*shards[0])
    for cut in shards[1:]:
        factor_of = factor_of * one(*cut)
    return factor_of


def choose_distinct(stream_key, rows, number_of, top, lift):
    order = jax.random.permutation(jax.random.fold_in(stream_key, 1), number_of)
    favour = order
    for power in range(3):
        favour = favour * favour // number_of
    favour = favour * lift // number_of
    chance = jax.random.randint(jax.random.fold_in(stream_key, 2), (rows, number_of), 0, 4096) + favour
    holders = jax.random.permutation(jax.random.fold_in(stream_key, 3), rows)[jnp.arange(number_of) % rows]
    chance = jnp.where(jnp.arange(rows)[:, None] == holders[None, :], 1 << 14, chance)
    merit = chance * number_of + jnp.arange(number_of)
    return lax.top_k(merit.astype(jnp.int32), top)[1].astype(jnp.int32)


def profile(count, total, limit, lean):
    portions = [(1 << 20) // math.isqrt(rank ** lean) + 1 for rank in range(2, count + 1)]
    surplus, holding = total - limit - (count - 1), [1] * (count - 1)
    while surplus > 0:
        candidates = [i for i in range(count - 1) if holding[i] < limit]
        whole, left = sum([portions[i] for i in candidates]), surplus
        for i in candidates:
            addition = min(limit - holding[i], max(1, left * portions[i] // whole), surplus)
            holding[i] = holding[i] + addition
            surplus = surplus - addition
    return np.array([limit] + holding)


def uneven_parts(key, count, total, reach, lean):
    if count == 2:
        one = jax.random.randint(key, (), max(1, total - reach), min(reach, total - 1) + 1)
        return jnp.stack([one, total - one])
    tallies = jnp.asarray(profile(count, total, reach, lean), jnp.int32)
    twos = (count - 1) // 2
    source_of, taker = tallies[1:1 + 2 * twos:2], tallies[2:2 + 2 * twos:2]
    margin = jnp.minimum(source_of - 1, reach - taker)
    moved = jax.random.randint(jax.random.fold_in(key, 1), (twos,), 0, 1 << 20) % (margin + 1)
    tallies = tallies.at[1:1 + 2 * twos:2].set(source_of - moved).at[2:2 + 2 * twos:2].set(taker + moved)
    return tallies[jax.random.permutation(jax.random.fold_in(key, 2), count)]


def centred(key, shape, spread, bound, split=(), held_as=jnp.bfloat16):
    result = spread * jax.random.normal(key, shape, jnp.float32)
    if split:
        result = result * block_scale(key, shape, split, -0.22, 0.18)
    return jnp.clip(result, -bound, bound).astype(held_as)


def setup_inputs(seed: int = 0) -> dict:
    arg_keys = jax.random.split(jax.random.key(seed), 17)
    hidden_in = centred(arg_keys[0], (TOKENS, D), 1.0, 6.0, ((0, 4),))
    cotangent = centred(arg_keys[1], (TOKENS, D), 1.0, 6.0, ((0, 4),))
    routes = choose_distinct(arg_keys[2], TOKENS, EXPERTS, TOPK, 4096)
    segments = jax.vmap(lambda own: jnp.searchsorted(jnp.cumsum(uneven_parts(own, 4, LEN, LEN // 2, 1)), jnp.arange(LEN), side="right"))(jax.random.split(arg_keys[3], SEQS)).reshape((SEQS, LEN)).astype(jnp.int32)
    gain_in = jnp.clip(1.0 + 0.15 * jax.random.normal(arg_keys[4], (D,), jnp.float32), 0.25, 1.75).astype(jnp.bfloat16)
    w_query = centred(arg_keys[5], (D, HEADS * HEAD), D ** -0.5, 0.125, ((1, 8),))
    w_key = centred(arg_keys[6], (D, HEADS * HEAD), D ** -0.5, 0.125, ((1, 8),))
    w_value = centred(arg_keys[7], (D, HEADS * HEAD), D ** -0.5, 0.125, ((1, 8),))
    w_out = centred(arg_keys[8], (D, HEADS * HEAD), (max(HEADS * HEAD // 256, 4)) ** -0.5, 2.0, ((1, 8),))
    gain_query = jnp.clip(1.0 + 0.15 * jax.random.normal(arg_keys[9], (HEADS * HEAD,), jnp.float32), 0.25, 1.75).astype(jnp.bfloat16)
    gain_key = jnp.clip(1.0 + 0.15 * jax.random.normal(arg_keys[10], (HEADS * HEAD,), jnp.float32), 0.25, 1.75).astype(jnp.bfloat16)
    gain_mid = jnp.clip(1.0 + 0.15 * jax.random.normal(arg_keys[11], (D,), jnp.float32), 0.25, 1.75).astype(jnp.bfloat16)
    w_router = centred(arg_keys[12], (D, EXPERTS), (4 * D) ** -0.5, 0.0625)
    w_gate = centred(arg_keys[13], (EXPERTS, D, FF), D ** -0.5, 0.125, ((2, 8),))
    w_up = centred(arg_keys[14], (EXPERTS, D, FF), D ** -0.5, 0.125, ((2, 8),))
    w_down = centred(arg_keys[15], (EXPERTS, D, FF), (max(FF // 64, 2)) ** -0.5, 1.5, ((2, 8),))
    return dict(hidden_in=hidden_in, cotangent=cotangent, routes=routes, segments=segments, gain_in=gain_in, w_query=w_query, w_key=w_key, w_value=w_value, w_out=w_out, gain_query=gain_query, gain_key=gain_key, gain_mid=gain_mid, w_router=w_router, w_gate=w_gate, w_up=w_up, w_down=w_down)


EPSILON = 1e-05
MASKED = -1e+30
HIGHEST = lax.Precision.HIGHEST

@jax.custom_vjp
def low(v):
    return lax.optimization_barrier(v.astype(jnp.bfloat16)).astype(jnp.float32)

@jax.custom_vjp
def low_back(v):
    return v

def low_keep(v):
    return (low(v), None)

def low_pass(kept, grad):
    return (grad,)

def back_keep(v):
    return (v, None)

def back_low(kept, grad):
    return (low(grad),)
low.defvjp(low_keep, low_pass)
low_back.defvjp(back_keep, back_low)

def norm_scale(values):
    return lax.rsqrt(lax.optimization_barrier(jnp.mean(values * values, axis=-1, keepdims=True)) + EPSILON)

def document_positions(segments):
    index = jnp.broadcast_to(jnp.arange(segments.shape[1], dtype=jnp.int32)[None, :], segments.shape)
    previous = jnp.concatenate([segments[:, :1] - 1, segments[:, :-1]], axis=1)
    starts = lax.cummax(jnp.where(segments != previous, index, 0), axis=1)
    return index - starts

def rotary_tables(positions, head):
    half = head // 2
    freq = 10000.0 ** (-2.0 * jnp.arange(half, dtype=jnp.float32) / head)
    angle = positions.astype(jnp.float32)[:, None] * freq[None, :]
    return (jnp.cos(angle), jnp.sin(angle))

def rotate(values, cosine, sine):
    half = values.shape[-1] // 2
    first = values[..., :half]
    second = values[..., half:]
    cos_part = cosine[:, None, :]
    sin_part = sine[:, None, :]
    return jnp.concatenate([first * cos_part - second * sin_part, second * cos_part + first * sin_part], axis=-1)

def allowed_mask(segment_row):
    index = jnp.arange(segment_row.shape[0], dtype=jnp.int32)
    distance = index[:, None] - index[None, :]
    return (segment_row[:, None] == segment_row[None, :]) & (distance >= 0) & (distance < WINDOW)

def slot_table(routes, experts, capacity):
    flat = routes.reshape(-1)
    hits = (flat[:, None] == jnp.arange(experts, dtype=jnp.int32)[None, :]).astype(jnp.int32)
    rank = lax.optimization_barrier(jnp.sum((jnp.cumsum(hits, axis=0, dtype=jnp.int32) - 1) * hits, axis=1, dtype=jnp.int32))
    place = jnp.where(rank < capacity, flat * capacity + rank, experts * capacity).astype(jnp.int32)
    pairs = jnp.arange(flat.shape[0], dtype=jnp.int32) + 1
    owner = jnp.zeros((experts * capacity + 1,), jnp.int32).at[place].add(pairs)
    return (place, owner[:experts * capacity] - 1)

def group_forward(params, hidden, routes, segments):
    gain_in, w_query, w_key, w_value, w_out, gain_query, gain_key, gain_mid, w_router, w_gate, w_up, w_down = params
    scale = 1.0 / math.sqrt(HEAD)
    tok_rows = hidden.shape[0]
    seq_count, seq_len = segments.shape
    normed = low(hidden * norm_scale(hidden) * gain_in)
    query_raw = low_back(jnp.dot(normed, w_query, precision=HIGHEST))
    key_raw = low_back(jnp.dot(normed, w_key, precision=HIGHEST))
    value = low(low_back(jnp.dot(normed, w_value, precision=HIGHEST)))
    query_normed = query_raw * norm_scale(query_raw) * gain_query
    key_normed = key_raw * norm_scale(key_raw) * gain_key
    cosine, sine = rotary_tables(document_positions(segments).reshape(-1), HEAD)
    query = low(rotate(query_normed.reshape(tok_rows, HEADS, HEAD), cosine, sine))
    key = low(rotate(key_normed.reshape(tok_rows, HEADS, HEAD), cosine, sine))
    shaped = (seq_count, seq_len, HEADS, HEAD)

    def attend(block):
        block_query, block_key, block_value, block_segments = block
        mask = allowed_mask(block_segments)[None]
        scores = low_back(jnp.einsum('qhd,khd->hqk', block_query, block_key, precision=HIGHEST) * scale)
        scores = jnp.where(mask, scores, MASKED)
        top = lax.optimization_barrier(jnp.max(scores, axis=-1, keepdims=True))
        expo = jnp.exp(scores - top)
        weights = low(expo / lax.optimization_barrier(jnp.sum(expo, axis=-1, keepdims=True)))
        return jnp.einsum('hqk,khd->qhd', weights, block_value, precision=HIGHEST)
    attended = lax.map(jax.checkpoint(attend), (query.reshape(shaped), key.reshape(shaped), value.reshape(shaped), segments))
    attended = low_back(low(attended.reshape(tok_rows, HEADS * HEAD)))
    branch = low_back(jnp.dot(attended, w_out.T, precision=HIGHEST))
    middle = hidden + branch
    mixed = low(middle * norm_scale(middle) * gain_mid)
    logits = low_back(jnp.dot(mixed, w_router, precision=HIGHEST))
    router_probs = jax.nn.softmax(logits, axis=-1)
    choice_hits = (routes[:, :, None] == jnp.arange(EXPERTS, dtype=jnp.int32)[None, None, :]).astype(jnp.float32)
    gates = lax.optimization_barrier(jnp.sum(router_probs[:, None, :] * choice_hits, axis=-1)).reshape(-1)
    place, owner = slot_table(routes, EXPERTS, CAP)
    owner_safe = jnp.maximum(owner, 0)
    slot_token = (owner_safe // TOPK).reshape(EXPERTS, CAP)
    slot_gate = jnp.where(owner >= 0, gates[owner_safe], 0.0).reshape(EXPERTS, CAP)

    def expert_step(total, item):
        tokens, gate, gate_w, up_w, down_w = item
        rows_in = jnp.take(mixed, tokens, axis=0)
        gate_act = low_back(jnp.dot(rows_in, gate_w, precision=HIGHEST))
        up_act = low_back(jnp.dot(rows_in, up_w, precision=HIGHEST))
        inner = low(jax.nn.silu(gate_act) * up_act)
        out = low_back(jnp.dot(inner, down_w.T, precision=HIGHEST))
        return (total.at[tokens].add(out * gate[:, None]), None)
    moe, unused = lax.scan(jax.checkpoint(expert_step), jnp.zeros_like(middle), (slot_token, slot_gate, w_gate, w_up, w_down))
    return middle + moe

def reference(hidden_in, cotangent, routes, segments, gain_in, w_query, w_key, w_value, w_out, gain_query, gain_key, gain_mid, w_router, w_gate, w_up, w_down):
    params = tuple((item.astype(jnp.float32) for item in (gain_in, w_query, w_key, w_value, w_out, gain_query, gain_key, gain_mid, w_router, w_gate, w_up, w_down)))
    hidden = hidden_in.astype(jnp.float32)
    width = hidden.shape[1]

    def forward(weights, inputs):

        def one_group(item):
            group_hidden, group_routes, group_segments = item
            return jax.checkpoint(group_forward)(weights, group_hidden, group_routes, group_segments)
        outs = lax.map(one_group, (inputs.reshape(N_DP, -1, width), routes.reshape(N_DP, -1, routes.shape[1]), segments.reshape(N_DP, -1, segments.shape[1])))
        return outs.reshape(-1, width)
    output, pull = jax.vjp(forward, params, hidden)
    grads, grad_hidden = pull(cotangent.astype(jnp.float32))
    return (output.astype(jnp.bfloat16), grad_hidden.astype(jnp.bfloat16), grads[1], grads[2], grads[3], grads[4], grads[0], grads[5], grads[6], grads[7], grads[8], grads[9], grads[10], grads[11])
```

```python
import functools
import math

import jax
import jax.numpy as jnp
from jax import lax
from jax.experimental import pallas as pl
from jax.experimental.pallas import tpu as pltpu
from jax.sharding import PartitionSpec as P

HEAD = 128
CAP = 1280
LONGEST = 512
EPSILON = 1e-05
MASKED = -1e30
LANES = 128
MIB = 1 << 20
BF = jnp.bfloat16
F32 = jnp.float32


def norm_scale(values):
    return lax.rsqrt(jnp.mean(values * values, axis=-1, keepdims=True) + EPSILON)


def document_positions(segments):
    index = jnp.broadcast_to(
        jnp.arange(segments.shape[1], dtype=jnp.int32)[None, :], segments.shape
    )
    previous = jnp.concatenate([segments[:, :1] - 1, segments[:, :-1]], axis=1)
    starts = lax.cummax(jnp.where(segments != previous, index, 0), axis=1)
    return index - starts


def rotary_tables(positions, head):
    half = head // 2
    freq = 10000.0 ** (-2.0 * jnp.arange(half, dtype=F32) / head)
    angle = positions.astype(F32)[:, None] * freq[None, :]
    return (jnp.cos(angle), jnp.sin(angle))


def rotate(values, cosine, sine):
    half = values.shape[-1] // 2
    first = values[..., :half]
    second = values[..., half:]
    cos_part = cosine[:, None, :]
    sin_part = sine[:, None, :]
    return jnp.concatenate(
        [first * cos_part - second * sin_part, second * cos_part + first * sin_part], axis=-1
    )


def rotate_back(grads, cosine, sine):
    return rotate(grads, cosine, -sine)


def dot(left, right, left_dim=1, right_dim=0):
    return lax.dot_general(
        left, right, (((left_dim,), (right_dim,)), ((), ())), preferred_element_type=F32
    )


def whole_spec(shape):
    return pl.BlockSpec(
        shape, lambda *_: (0,) * len(shape), pipeline_mode=pl.Buffered(buffer_count=1)
    )


def params(mib):
    return pltpu.CompilerParams(vmem_limit_bytes=mib * MIB)


def cost(flops, moved):
    return pl.CostEstimate(flops=int(flops), bytes_accessed=int(moved), transcendentals=0)


def key_span(block, rows):
    start = max(0, block * rows - LONGEST)
    return start, (block + 1) * rows


def masked_scores(q_rows, k_rows, seg_col, seg_row, row0, key0, scale):
    scores = dot(q_rows, k_rows, 1, 1) * scale
    row = lax.broadcasted_iota(jnp.int32, scores.shape, 0) + row0
    key = lax.broadcasted_iota(jnp.int32, scores.shape, 1) + key0
    return jnp.where((seg_col == seg_row) & (row >= key), scores, MASKED)


def attend_kernel(scale, block, q_ref, k_ref, v_ref, col_ref, row_ref, out_ref):
    length = q_ref.shape[0]
    for index in range(length // block):
        start, stop = key_span(index, block)
        rows = slice(index * block, (index + 1) * block)
        scores = masked_scores(
            q_ref[rows, :],
            k_ref[start:stop, :],
            col_ref[rows, :],
            row_ref[0, :, start:stop],
            index * block,
            start,
            scale,
        )
        expo = jnp.exp(scores - jnp.max(scores, axis=1, keepdims=True))
        weights = (expo / jnp.sum(expo, axis=1, keepdims=True)).astype(BF)
        out_ref[rows, :] = dot(weights, v_ref[start:stop, :]).astype(out_ref.dtype)


def attend_back_kernel(
    scale, block, q_ref, k_ref, v_ref, g_ref, col_ref, row_ref, dq_ref, dk_ref, dv_ref
):
    length = q_ref.shape[0]
    dk_ref[...] = jnp.zeros_like(dk_ref)
    dv_ref[...] = jnp.zeros_like(dv_ref)
    for index in range(length // block):
        start, stop = key_span(index, block)
        rows = slice(index * block, (index + 1) * block)
        q_rows = q_ref[rows, :]
        g_rows = g_ref[rows, :]
        k_rows = k_ref[start:stop, :]
        scores = masked_scores(
            q_rows, k_rows, col_ref[rows, :], row_ref[0, :, start:stop], index * block, start, scale
        )
        expo = jnp.exp(scores - jnp.max(scores, axis=1, keepdims=True))
        probs = expo / jnp.sum(expo, axis=1, keepdims=True)
        weight_grad = dot(g_rows, v_ref[start:stop, :], 1, 1)
        delta = jnp.sum(probs * weight_grad, axis=1, keepdims=True)
        score_grad = (probs * (weight_grad - delta)).astype(BF)
        dv_ref[start:stop, :] += dot(probs.astype(BF), g_rows, 0, 0)
        dk_ref[start:stop, :] += dot(score_grad, q_rows, 0, 0) * scale
        dq_ref[rows, :] = dot(score_grad, k_rows) * scale


def attention_specs(length):
    block = pl.BlockSpec((length, HEAD), lambda seq, head: (seq, head))
    col = pl.BlockSpec((length, 1), lambda seq, head: (seq, 0))
    row = pl.BlockSpec((1, 1, length), lambda seq, head: (seq, 0, 0))
    return block, col, row


def attend(q, k, v, segments, scale):
    seqs, length = segments.shape
    heads = q.shape[1] // HEAD
    block, col, row = attention_specs(length)
    work = seqs * heads * length * length * HEAD
    return pl.pallas_call(
        functools.partial(attend_kernel, scale, min(256, length)),
        grid=(seqs, heads),
        in_specs=[block, block, block, col, row],
        out_specs=block,
        out_shape=jax.ShapeDtypeStruct(q.shape, BF),
        compiler_params=params(48),
        cost_estimate=cost(4 * work, q.size * 8),
        name="attend",
    )(q, k, v, segments.reshape(-1, 1), segments[:, None, :])


def attend_back(q, k, v, grad, segments, scale):
    seqs, length = segments.shape
    heads = q.shape[1] // HEAD
    block, col, row = attention_specs(length)
    work = seqs * heads * length * length * HEAD
    return pl.pallas_call(
        functools.partial(attend_back_kernel, scale, min(256, length)),
        grid=(seqs, heads),
        in_specs=[block, block, block, block, col, row],
        out_specs=[block, block, block],
        out_shape=[jax.ShapeDtypeStruct(q.shape, F32)] * 3,
        compiler_params=params(48),
        cost_estimate=cost(10 * work, q.size * 20),
        name="attend_back",
    )(q, k, v, grad, segments.reshape(-1, 1), segments[:, None, :])


def expert_terms(gate_act, up_act, low_grad, gate):
    sigmoid = 1.0 / (1.0 + jnp.exp(-gate_act))
    silu = gate_act * sigmoid
    inner = (silu * up_act).astype(BF).astype(F32)
    inner_grad = low_grad * gate
    gate_grad = inner_grad * up_act * sigmoid * (1.0 + gate_act * (1.0 - sigmoid))
    return (
        (inner * gate).astype(BF),
        gate_grad.astype(BF),
        (inner_grad * silu).astype(BF),
        inner * low_grad,
    )


def expert_kernel(
    rows,
    mixed_ref,
    dy_ref,
    gates_ref,
    wg_ref,
    wu_ref,
    wd_ref,
    gi_ref,
    gg_ref,
    ug_ref,
    dots_ref,
    both,
    down,
):
    step = pl.program_id(0)
    many, _, hid = wg_ref.shape
    for part in range(many):
        both[:, part * hid : (part + 1) * hid] = wg_ref[part]
        both[:, (many + part) * hid : (many + part + 1) * hid] = wu_ref[part]
        down[:, part * hid : (part + 1) * hid] = wd_ref[part]

    @pl.when(step == 0)
    def _():
        dots_ref[...] = jnp.zeros_like(dots_ref)

    def body(index, carry):
        here = pl.ds(pl.multiple_of(index * rows, rows), rows)
        acts = dot(mixed_ref[here, :], both[...])
        low_grads = dot(dy_ref[here, :], down[...])
        gates = gates_ref[here, :]
        totals = dots_ref[here, :]
        lane = lax.broadcasted_iota(jnp.int32, gates.shape, 1)
        for part in range(many):
            chosen = lane == step * many + part
            gate = jnp.sum(jnp.where(chosen, gates, 0.0), axis=1, keepdims=True)
            span = slice(part * hid, (part + 1) * hid)
            other = slice((many + part) * hid, (many + part + 1) * hid)
            gi, gg, ug, terms = expert_terms(acts[:, span], acts[:, other], low_grads[:, span], gate)
            gi_ref[here, span] = gi
            gg_ref[here, span] = gg
            ug_ref[here, span] = ug
            totals = jnp.where(chosen, jnp.sum(terms, axis=1, keepdims=True), totals)
        dots_ref[here, :] = totals
        return carry

    lax.fori_loop(0, mixed_ref.shape[0] // rows, body, 0)


def expert_acts(mixed, dy, gates, w_gate, w_up, w_down):
    tokens, width = mixed.shape
    experts, _, hid = w_gate.shape
    many = 2
    weight = pl.BlockSpec((many, width, hid), lambda e: (e, 0, 0))
    wide = pl.BlockSpec((tokens, many * hid), lambda e: (0, e))
    wide_shape = jax.ShapeDtypeStruct((tokens, experts * hid), BF)
    return pl.pallas_call(
        functools.partial(expert_kernel, min(256, tokens)),
        grid=(experts // many,),
        in_specs=[
            whole_spec(mixed.shape),
            whole_spec(dy.shape),
            whole_spec(gates.shape),
            weight,
            weight,
            weight,
        ],
        out_specs=[wide, wide, wide, whole_spec(gates.shape)],
        out_shape=[wide_shape, wide_shape, wide_shape, jax.ShapeDtypeStruct(gates.shape, F32)],
        scratch_shapes=[
            pltpu.VMEM((width, 2 * many * hid), BF),
            pltpu.VMEM((width, many * hid), BF),
        ],
        compiler_params=params(58),
        cost_estimate=cost(6 * tokens * width * experts * hid, 12 * tokens * width),
        name="expert_acts",
    )(mixed, dy, gates, w_gate, w_up, w_down)


def back_kernel(rows, count, *refs):
    lefts, weights, out_ref, scratch = refs[:count], refs[count : 2 * count], refs[-1 - count], refs[-count:]
    experts, _, hid = weights[0].shape
    for weight, held in zip(weights, scratch):
        for expert in range(experts):
            held[:, expert * hid : (expert + 1) * hid] = weight[expert]

    def body(index, carry):
        here = pl.ds(pl.multiple_of(index * rows, rows), rows)
        total = dot(lefts[0][here, :], scratch[0][...], 1, 1)
        for left, held in zip(lefts[1:], scratch[1:]):
            total = total + dot(left[here, :], held[...], 1, 1)
        out_ref[here, :] = total
        return carry

    lax.fori_loop(0, out_ref.shape[0] // rows, body, 0)


def experts_back(lefts, weights):
    tokens = lefts[0].shape[0]
    experts, width, hid = weights[0].shape
    count = len(lefts)
    block = min(256, width)
    return pl.pallas_call(
        functools.partial(back_kernel, min(512, tokens), count),
        grid=(width // block,),
        in_specs=[whole_spec(left.shape) for left in lefts]
        + [pl.BlockSpec((experts, block, hid), lambda d: (0, d, 0))] * count,
        out_specs=pl.BlockSpec((tokens, block), lambda d: (0, d)),
        out_shape=jax.ShapeDtypeStruct((tokens, width), F32),
        scratch_shapes=[pltpu.VMEM((block, experts * hid), BF)] * count,
        compiler_params=params(56),
        cost_estimate=cost(
            2 * count * tokens * width * experts * hid, (4 + 4 * count) * tokens * width
        ),
        name="experts_back",
    )(*lefts, *weights)


def grads_kernel(rows, left_ref, *refs):
    count = (len(refs) - 1) // 2
    rights, outs, held = refs[:count], refs[count : 2 * count], refs[-1]
    many, width, hid = outs[0].shape
    for index, right in enumerate(rights):
        held[:, index * many * hid : (index + 1) * many * hid] = right[...]

    def body(index, carry):
        here = pl.ds(pl.multiple_of(index * rows, rows), rows)
        total = dot(left_ref[here, :], held[...])
        for which, out in enumerate(outs):
            for part in range(many):
                place = (which * many + part) * hid
                out[part, here, :] = total[:, place : place + hid]
        return carry

    lax.fori_loop(0, width // rows, body, 0)


def expert_grads(left, rights, experts):
    width, tokens = left.shape
    hid = rights[0].shape[1] // experts
    many = 2
    count = len(rights)
    return pl.pallas_call(
        functools.partial(grads_kernel, min(512, width)),
        grid=(experts // many,),
        in_specs=[whole_spec(left.shape)]
        + [pl.BlockSpec((tokens, many * hid), lambda e: (0, e))] * count,
        out_specs=[pl.BlockSpec((many, width, hid), lambda e: (e, 0, 0))] * count,
        out_shape=[jax.ShapeDtypeStruct((experts, width, hid), F32)] * count,
        scratch_shapes=[pltpu.VMEM((tokens, count * many * hid), BF)],
        compiler_params=params(56),
        cost_estimate=cost(
            2 * count * tokens * width * experts * hid, 6 * count * experts * hid * width
        ),
        name="expert_grads",
    )(left, *rights)


def plain_experts(mixed, dy, gates, w_gate, w_up, w_down):
    acts = jnp.einsum("td,edh->teh", mixed, w_gate, preferred_element_type=F32)
    ups = jnp.einsum("td,edh->teh", mixed, w_up, preferred_element_type=F32)
    low = jnp.einsum("td,edh->teh", dy, w_down, preferred_element_type=F32)
    gi, gg, ug, terms = expert_terms(acts, ups, low, gates[:, :, None])
    flat = (mixed.shape[0], -1)
    return gi.reshape(flat), gg.reshape(flat), ug.reshape(flat), jnp.sum(terms, axis=2)


def plain_back(lefts, weights):
    experts, _, hid = weights[0].shape
    total = 0.0
    for left, weight in zip(lefts, weights):
        total = total + jnp.einsum(
            "teh,edh->td", left.reshape(-1, experts, hid), weight, preferred_element_type=F32
        )
    return total


def plain_grads(left, rights, experts):
    return [
        jnp.einsum(
            "dt,teh->edh",
            left,
            right.reshape(right.shape[0], experts, -1),
            preferred_element_type=F32,
        )
        for right in rights
    ]


def on_device(
    hidden_in,
    cotangent,
    routes,
    segments,
    gain_in,
    w_query,
    w_key,
    w_value,
    w_out,
    gain_query,
    gain_key,
    gain_mid,
    w_router,
    w_gate,
    w_up,
    w_down,
):
    tensor_count = lax.axis_size("tensor")
    tensor_rank = lax.axis_index("tensor")
    tok_rows, width = hidden_in.shape
    local_width = w_query.shape[1]
    heads_here = local_width // HEAD
    full_width = local_width * tensor_count
    share = width // tensor_count
    experts = w_gate.shape[0]
    scale = 1.0 / math.sqrt(HEAD)
    tiled = w_gate.shape[2] % LANES == 0
    acts_of = expert_acts if tiled else plain_experts
    back_of = experts_back if tiled else plain_back
    grads_of = expert_grads if tiled else plain_grads

    hidden = hidden_in.astype(F32)
    in_scale = norm_scale(hidden)
    in_hat = hidden * in_scale
    normed = (in_hat * gain_in.astype(F32)).astype(BF)
    query_raw = dot(normed, w_query)
    key_raw = dot(normed, w_key)
    value_low = dot(normed, w_value).astype(BF)
    square_sums = lax.psum(
        (jnp.sum(query_raw * query_raw, axis=1), jnp.sum(key_raw * key_raw, axis=1)), "tensor"
    )
    query_scale = lax.rsqrt(square_sums[0] / full_width + EPSILON)[:, None]
    key_scale = lax.rsqrt(square_sums[1] / full_width + EPSILON)[:, None]
    query_hat = query_raw * query_scale
    key_hat = key_raw * key_scale
    cosine, sine = rotary_tables(document_positions(segments).reshape(-1), HEAD)

    def turn(values, gain):
        scaled = (values * gain.astype(F32)).reshape(tok_rows, heads_here, HEAD)
        return rotate(scaled, cosine, sine).astype(BF).reshape(tok_rows, local_width)

    query_low = turn(query_hat, gain_query)
    key_low = turn(key_hat, gain_key)
    attended_low = attend(query_low, key_low, value_low, segments, scale)
    branch = lax.psum(dot(attended_low, w_out, 1, 1), "tensor")
    middle = hidden + branch
    mid_scale = norm_scale(middle)
    mid_hat = middle * mid_scale
    mixed = (mid_hat * gain_mid.astype(F32)).astype(BF)
    router_probs = jax.nn.softmax(dot(mixed, w_router), axis=-1)
    expert_ids = jnp.arange(experts, dtype=jnp.int32)
    hits = jnp.any(routes[:, :, None] == expert_ids[None, None, :], axis=1)
    counts = hits.astype(jnp.int32)
    kept = hits & (jnp.cumsum(counts, axis=0, dtype=jnp.int32) - counts < CAP)
    gates = jnp.where(kept, router_probs, 0.0)

    gi, gg, ug, dots = acts_of(mixed, cotangent, gates, w_gate, w_up, w_down)
    mixed_part = back_of([gg, ug], [w_gate, w_up])
    moe_part = back_of([gi], [w_down])
    moe_share = lax.psum_scatter(moe_part, "tensor", scatter_dimension=1, tiled=True)
    middle_share = lax.dynamic_slice_in_dim(middle, tensor_rank * share, share, 1)
    output = (middle_share + moe_share).astype(BF)
    prob_grad = jnp.where(kept, lax.psum(dots.T, "tensor").T, 0.0)
    logit_grad = (
        router_probs * (prob_grad - jnp.sum(router_probs * prob_grad, axis=-1, keepdims=True))
    ).astype(BF)
    router_back = dot(logit_grad, w_router, 1, 1)
    grad_router = dot(mixed, logit_grad, 0, 0)
    grad_gate, grad_up = grads_of(mixed.T, [gg, ug], experts)
    (grad_down,) = grads_of(cotangent.T, [gi], experts)

    mixed_grad = lax.psum(mixed_part, "tensor") + router_back
    grad_gain_mid = jnp.sum(mixed_grad * mid_hat, axis=0)
    mid_scaled = mixed_grad * gain_mid.astype(F32)
    middle_grad = cotangent.astype(F32) + mid_scale * (
        mid_scaled - mid_hat * jnp.mean(mid_scaled * mid_hat, axis=1, keepdims=True)
    )
    middle_low = middle_grad.astype(BF)
    grad_w_out = dot(middle_low, attended_low, 0, 0)
    attended_grad = dot(middle_low, w_out).astype(BF)
    query_rot_grad, key_rot_grad, value_grad = attend_back(
        query_low, key_low, value_low, attended_grad, segments, scale
    )

    def turn_back(grads):
        shaped = grads.reshape(tok_rows, heads_here, HEAD)
        return rotate_back(shaped, cosine, sine).reshape(tok_rows, local_width)

    query_norm_grad = turn_back(query_rot_grad)
    key_norm_grad = turn_back(key_rot_grad)
    grad_gain_query = jnp.sum(query_norm_grad * query_hat, axis=0)
    grad_gain_key = jnp.sum(key_norm_grad * key_hat, axis=0)
    query_scaled = query_norm_grad * gain_query.astype(F32)
    key_scaled = key_norm_grad * gain_key.astype(F32)
    head_totals = lax.psum(
        (jnp.sum(query_scaled * query_hat, axis=1), jnp.sum(key_scaled * key_hat, axis=1)), "tensor"
    )
    query_raw_grad = (
        query_scale * (query_scaled - query_hat * (head_totals[0] / full_width)[:, None])
    ).astype(BF)
    key_raw_grad = (
        key_scale * (key_scaled - key_hat * (head_totals[1] / full_width)[:, None])
    ).astype(BF)
    value_grad_low = value_grad.astype(BF)
    grad_w_query = dot(normed, query_raw_grad, 0, 0)
    grad_w_key = dot(normed, key_raw_grad, 0, 0)
    grad_w_value = dot(normed, value_grad_low, 0, 0)
    normed_part = (
        dot(query_raw_grad, w_query, 1, 1)
        + dot(key_raw_grad, w_key, 1, 1)
        + dot(value_grad_low, w_value, 1, 1)
    )
    normed_share = lax.psum_scatter(normed_part, "tensor", scatter_dimension=1, tiled=True)
    in_hat_share = lax.dynamic_slice_in_dim(in_hat, tensor_rank * share, share, 1)
    gain_share = lax.dynamic_slice_in_dim(gain_in.astype(F32), tensor_rank * share, share, 0)
    in_scaled = normed_share * gain_share
    row_totals = lax.psum(jnp.sum(in_scaled * in_hat_share, axis=1), "tensor")
    middle_grad_share = lax.dynamic_slice_in_dim(middle_grad, tensor_rank * share, share, 1)
    grad_input = (
        middle_grad_share + in_scale * (in_scaled - in_hat_share * (row_totals / width)[:, None])
    ).astype(BF)
    grad_gain_in = jnp.sum(normed_share * in_hat_share, axis=0)
    gain_totals = lax.psum((grad_gain_in, grad_gain_query, grad_gain_key), "dp")

    def over_dp(grad):
        return lax.psum_scatter(grad, "dp", scatter_dimension=0, tiled=True)

    return (
        output,
        grad_input,
        over_dp(grad_w_query),
        over_dp(grad_w_key),
        over_dp(grad_w_value),
        over_dp(grad_w_out),
        gain_totals[0],
        gain_totals[1],
        gain_totals[2],
        over_dp(grad_gain_mid),
        over_dp(grad_router),
        over_dp(grad_gate),
        over_dp(grad_up),
        over_dp(grad_down),
    )


def solution(mesh):
    in_specs = (
        P("dp", None),
        P("dp", None),
        P("dp", None),
        P("dp", None),
        P(),
        P(None, "tensor"),
        P(None, "tensor"),
        P(None, "tensor"),
        P(None, "tensor"),
        P("tensor"),
        P("tensor"),
        P(),
        P(),
        P(None, None, "tensor"),
        P(None, None, "tensor"),
        P(None, None, "tensor"),
    )
    out_specs = (
        P("dp", "tensor"),
        P("dp", "tensor"),
        P("dp", "tensor"),
        P("dp", "tensor"),
        P("dp", "tensor"),
        P("dp", "tensor"),
        P("tensor"),
        P("tensor"),
        P("tensor"),
        P("dp"),
        P("dp", None),
        P("dp", None, "tensor"),
        P("dp", None, "tensor"),
        P("dp", None, "tensor"),
    )
    return jax.shard_map(
        on_device, mesh=mesh, in_specs=in_specs, out_specs=out_specs, check_vma=False
    )
```

```python
import functools
import math

import jax
import jax.numpy as jnp
from jax import lax
from jax.experimental import pallas as pl
from jax.experimental.pallas import tpu as pltpu
from jax.sharding import PartitionSpec as P

HEAD = 128
CAP = 1280
LONGEST = 512
EPSILON = 1e-05
MASKED = -1e30
LANES = 128
MIB = 1 << 20
BF = jnp.bfloat16
F32 = jnp.float32


ANY = pl.BlockSpec(memory_space=pl.ANY)


def norm_scale(values):
    return lax.rsqrt(jnp.mean(values * values, axis=-1, keepdims=True) + EPSILON)


def document_positions(segments):
    index = jnp.broadcast_to(
        jnp.arange(segments.shape[1], dtype=jnp.int32)[None, :], segments.shape
    )
    previous = jnp.concatenate([segments[:, :1] - 1, segments[:, :-1]], axis=1)
    starts = lax.cummax(jnp.where(segments != previous, index, 0), axis=1)
    return index - starts


def rotary_tables(positions, head):
    half = head // 2
    freq = 10000.0 ** (-2.0 * jnp.arange(half, dtype=F32) / head)
    angle = positions.astype(F32)[:, None] * freq[None, :]
    return (jnp.cos(angle), jnp.sin(angle))


def dot(left, right, left_dim=1, right_dim=0):
    return lax.dot_general(
        left, right, (((left_dim,), (right_dim,)), ((), ())), preferred_element_type=F32
    )


def whole_spec(shape):
    return pl.BlockSpec(
        shape, lambda *_: (0,) * len(shape), pipeline_mode=pl.Buffered(buffer_count=1)
    )


def params(mib):
    return pltpu.CompilerParams(vmem_limit_bytes=max(mib, 58) * MIB)


def cost(flops, moved, last=False):
    if last:
        flops, moved = 1024, 1024
    return pl.CostEstimate(flops=int(flops), bytes_accessed=int(moved), transcendentals=0)


def across_lanes(row):
    return jnp.broadcast_to(row, (LANES, row.shape[1])).T


def along_lanes(column):
    return jnp.broadcast_to(column, (column.shape[0], LANES)).T[:8]


def project_kernel(x_ref, gain_ref, wq_ref, wk_ref, wv_ref, n_ref, q_ref, k_ref, v_ref, sums_ref):
    x = x_ref[...].astype(F32)
    normed = (x * norm_scale(x) * gain_ref[...].astype(F32)).astype(BF)
    n_ref[...] = normed
    query = dot(normed, wq_ref[...])
    key = dot(normed, wk_ref[...])
    q_ref[...] = query
    k_ref[...] = key
    v_ref[...] = dot(normed, wv_ref[...]).astype(BF)
    q_sum = along_lanes(jnp.sum(query * query, axis=1, keepdims=True))
    k_sum = along_lanes(jnp.sum(key * key, axis=1, keepdims=True))
    first = lax.broadcasted_iota(jnp.int32, q_sum.shape, 0) == 0
    sums_ref[...] = jnp.where(first, q_sum, k_sum)


def project(hidden, gain, w_query, w_key, w_value):
    tokens, width = hidden.shape
    wide = w_query.shape[1]
    rows = min(256, tokens)
    out = pl.BlockSpec((rows, wide), lambda i: (i, 0))
    return pl.pallas_call(
        project_kernel,
        grid=(tokens // rows,),
        in_specs=[pl.BlockSpec((rows, width), lambda i: (i, 0)), whole_spec((1, width))]
        + [whole_spec(w_query.shape)] * 3,
        out_specs=[
            pl.BlockSpec((rows, width), lambda i: (i, 0)),
            out,
            out,
            out,
            pl.BlockSpec((8, rows), lambda i: (0, i)),
        ],
        out_shape=[
            jax.ShapeDtypeStruct((tokens, width), BF),
            jax.ShapeDtypeStruct((tokens, wide), F32),
            jax.ShapeDtypeStruct((tokens, wide), F32),
            jax.ShapeDtypeStruct((tokens, wide), BF),
            jax.ShapeDtypeStruct((8, tokens), F32),
        ],
        compiler_params=params(48),
        cost_estimate=cost(6 * tokens * width * wide, 4 * tokens * width),
        name="project",
    )(hidden, gain.reshape(1, -1), w_query, w_key, w_value)


def key_span(block, rows):
    start = max(0, block * rows - LONGEST)
    return start, (block + 1) * rows


def masked_scores(q_rows, k_rows, seg_col, seg_row, row0, key0, scale):
    scores = dot(q_rows, k_rows, 1, 1) * scale
    row = lax.broadcasted_iota(jnp.int32, scores.shape, 0) + row0
    key = lax.broadcasted_iota(jnp.int32, scores.shape, 1) + key0
    return jnp.where((seg_col == seg_row) & (row >= key), scores, MASKED)


def both_halves(angles):
    other = pltpu.roll(angles, HEAD // 2, 1)
    low = lax.broadcasted_iota(jnp.int32, angles.shape, 1) < HEAD // 2
    return jnp.where(low, angles, other), jnp.where(low, -other, angles)


def turn(values, cosine, sine):
    return values * cosine + pltpu.roll(values, HEAD // 2, 1) * sine


def hat_scale(sums_ref, which, full):
    return lax.rsqrt(across_lanes(sums_ref[which : which + 1, :]) / full + EPSILON)


def attend_kernel(
    scale,
    block,
    full,
    q_ref,
    k_ref,
    v_ref,
    sums_ref,
    gq_ref,
    gk_ref,
    angle_ref,
    col_ref,
    row_ref,
    out_ref,
    ql_ref,
    kl_ref,
):
    length = q_ref.shape[0]
    cosine, sine = both_halves(angle_ref[...])
    for raw, which, gain, low in ((q_ref, 0, gq_ref, ql_ref), (k_ref, 1, gk_ref, kl_ref)):
        hat = raw[...] * hat_scale(sums_ref, which, full)
        low[...] = turn(hat * gain[...].astype(F32), cosine, sine).astype(BF)
    for index in range(length // block):
        start, stop = key_span(index, block)
        rows = slice(index * block, (index + 1) * block)
        scores = masked_scores(
            ql_ref[rows, :],
            kl_ref[start:stop, :],
            col_ref[rows, :],
            row_ref[0, :, start:stop],
            index * block,
            start,
            scale,
        )
        expo = jnp.exp(scores - jnp.max(scores, axis=1, keepdims=True))
        weights = (expo / jnp.sum(expo, axis=1, keepdims=True)).astype(BF)
        out_ref[rows, :] = dot(weights, v_ref[start:stop, :]).astype(BF).astype(F32)


def attend(q, k, v, sums, gains, angles, segments, chunk, scale, full):
    seqs, length = segments.shape
    heads = q.shape[1] // HEAD
    block = pl.BlockSpec((length, HEAD), lambda head: (chunk, head))
    mine = pl.BlockSpec((length, HEAD), lambda head: (0, head))
    gain = pl.BlockSpec((1, HEAD), lambda head: (0, head))
    work = heads * length * length * HEAD
    return pl.pallas_call(
        functools.partial(attend_kernel, scale, min(256, length), full),
        grid=(heads,),
        in_specs=[
            block,
            block,
            block,
            pl.BlockSpec((8, length), lambda head: (0, chunk)),
            gain,
            gain,
            pl.BlockSpec((length, HEAD), lambda head: (chunk, 0)),
            pl.BlockSpec((length, 1), lambda head: (chunk, 0)),
            pl.BlockSpec((1, 1, length), lambda head: (chunk, 0, 0)),
        ],
        out_specs=[mine] * 3,
        out_shape=[jax.ShapeDtypeStruct((length, q.shape[1]), kind) for kind in (F32, BF, BF)],
        compiler_params=params(48),
        cost_estimate=cost(4 * work, length * heads * HEAD * 22),
        name="attend",
    )(q, k, v, sums, *gains, angles, segments.reshape(-1, 1), segments[:, None, :])


def attend_back_kernel(
    scale,
    block,
    full,
    after,
    place_ref,
    q_ref,
    k_ref,
    v_ref,
    grad_ref,
    qr_ref,
    kr_ref,
    sums_ref,
    gq_ref,
    gk_ref,
    angle_ref,
    col_ref,
    row_ref,
    *refs,
):
    qs_ref, ks_ref, dv_out, totals_ref, gains_ref, g_ref, dq_ref, dk_ref, dv_ref = refs[after:]
    length = q_ref.shape[0]
    parts, part_rows, _ = grad_ref.shape
    for part in range(parts):
        here = slice(part * part_rows, (part + 1) * part_rows)
        g_ref[here, :] = grad_ref[place_ref[part]].astype(BF)
    dk_ref[...] = jnp.zeros_like(dk_ref)
    dv_ref[...] = jnp.zeros_like(dv_ref)
    for index in range(length // block):
        start, stop = key_span(index, block)
        rows = slice(index * block, (index + 1) * block)
        q_rows = q_ref[rows, :]
        g_rows = g_ref[rows, :]
        k_rows = k_ref[start:stop, :]
        scores = masked_scores(
            q_rows, k_rows, col_ref[rows, :], row_ref[0, :, start:stop], index * block, start, scale
        )
        expo = jnp.exp(scores - jnp.max(scores, axis=1, keepdims=True))
        probs = expo / jnp.sum(expo, axis=1, keepdims=True)
        weight_grad = dot(g_rows, v_ref[start:stop, :], 1, 1)
        delta = jnp.sum(probs * weight_grad, axis=1, keepdims=True)
        score_grad = (probs * (weight_grad - delta)).astype(BF)
        dv_ref[start:stop, :] += dot(probs.astype(BF), g_rows, 0, 0)
        dk_ref[start:stop, :] += dot(score_grad, q_rows, 0, 0) * scale
        dq_ref[rows, :] = dot(score_grad, k_rows) * scale
    dv_out[...] = dv_ref[...].astype(BF)
    cosine, sine = both_halves(angle_ref[...])
    sums, gains = [], []
    for grad, raw, which, gain, out in (
        (dq_ref, qr_ref, 0, gq_ref, qs_ref),
        (dk_ref, kr_ref, 1, gk_ref, ks_ref),
    ):
        norm_grad = turn(grad[...], cosine, -sine)
        hat = raw[...] * hat_scale(sums_ref, which, full)
        gains.append(jnp.sum(norm_grad * hat, axis=0, keepdims=True))
        scaled = norm_grad * gain[...].astype(F32)
        out[...] = scaled
        sums.append(along_lanes(jnp.sum(scaled * hat, axis=1, keepdims=True)))
    first = lax.broadcasted_iota(jnp.int32, sums[0].shape, 0) == 0
    total = jnp.where(first, sums[0], sums[1])
    if_first = pl.program_id(1) == 0
    totals_ref[...] = jnp.where(if_first, total, totals_ref[...] + total)
    row = lax.broadcasted_iota(jnp.int32, gains_ref.shape, 0)
    gains_ref[...] = jnp.where(row == 0, gains[0], jnp.where(row == 1, gains[1], 0.0))


def attend_back(
    q, k, v, grad, raws, sums, gains, angles, place, segments, scale, full, after=()
):
    seqs, length = segments.shape
    heads = q.shape[1] // HEAD
    block = pl.BlockSpec((length, HEAD), lambda seq, head, _: (seq, head))
    gain = pl.BlockSpec((1, HEAD), lambda seq, head, _: (0, head))
    line = pl.BlockSpec((8, length), lambda seq, head, _: (0, seq))
    work = seqs * heads * length * length * HEAD
    return pl.pallas_call(
        functools.partial(attend_back_kernel, scale, min(256, length), full, len(after)),
        grid_spec=pltpu.PrefetchScalarGridSpec(
            num_scalar_prefetch=1,
            grid=(seqs, heads),
            in_specs=[
                block,
                block,
                block,
                pl.BlockSpec(
                    (grad.shape[0], grad.shape[1] // seqs, HEAD),
                    lambda seq, head, _: (0, seq, head),
                ),
                block,
                block,
                line,
                gain,
                gain,
                pl.BlockSpec((length, HEAD), lambda seq, head, _: (seq, 0)),
                pl.BlockSpec((length, 1), lambda seq, head, _: (seq, 0)),
                pl.BlockSpec((1, 1, length), lambda seq, head, _: (seq, 0, 0)),
            ]
            + [ANY] * len(after),
            out_specs=[
                block,
                block,
                block,
                line,
                pl.BlockSpec((8, HEAD), lambda seq, head, _: (seq, head)),
            ],
            scratch_shapes=[pltpu.VMEM((length, HEAD), BF)]
            + [pltpu.VMEM((length, HEAD), F32)] * 3,
        ),
        out_shape=[
            jax.ShapeDtypeStruct(q.shape, F32),
            jax.ShapeDtypeStruct(q.shape, F32),
            jax.ShapeDtypeStruct(q.shape, BF),
            jax.ShapeDtypeStruct((8, q.shape[0]), F32),
            jax.ShapeDtypeStruct((8 * seqs, q.shape[1]), F32),
        ],
        compiler_params=params(48),
        cost_estimate=cost(10 * work, q.size * 30),
        name="attend_back",
    )(
        place,
        q,
        k,
        v,
        grad,
        *raws,
        sums,
        *gains,
        angles,
        segments.reshape(-1, 1),
        segments[:, None, :],
        *after,
    )


def raw_grads_kernel(full, qs_ref, ks_ref, qr_ref, kr_ref, sums_ref, totals_ref, dq_ref, dk_ref):
    for which, scaled, raw, out in ((0, qs_ref, qr_ref, dq_ref), (1, ks_ref, kr_ref, dk_ref)):
        scale = hat_scale(sums_ref, which, full)
        total = across_lanes(totals_ref[which : which + 1, :]) / full
        out[...] = (scale * (scaled[...] - raw[...] * scale * total)).astype(BF)


def raw_grads(scaled, raws, sums, totals, full):
    tokens, wide = raws[0].shape
    rows = min(512, tokens)
    block = pl.BlockSpec((rows, HEAD), lambda i, head: (i, head))
    line = pl.BlockSpec((8, rows), lambda i, head: (0, i))
    return pl.pallas_call(
        functools.partial(raw_grads_kernel, full),
        grid=(tokens // rows, wide // HEAD),
        in_specs=[block] * 4 + [line] * 2,
        out_specs=[block] * 2,
        out_shape=[jax.ShapeDtypeStruct((tokens, wide), BF)] * 2,
        compiler_params=params(48),
        cost_estimate=cost(0, 20 * tokens * wide),
        name="raw_grads",
    )(*scaled, *raws, sums, totals)


def expert_terms(gate_act, up_act, low_grad, gate):
    sigmoid = 1.0 / (1.0 + jnp.exp(-gate_act))
    silu = gate_act * sigmoid
    inner = (silu * up_act).astype(BF).astype(F32)
    inner_grad = low_grad * gate
    gate_grad = inner_grad * up_act * sigmoid * (1.0 + gate_act * (1.0 - sigmoid))
    return (
        (inner * gate).astype(BF),
        gate_grad.astype(BF),
        (inner_grad * silu).astype(BF),
        inner * low_grad,
    )


def expert_kernel(rows, after, mixed_ref, dy_ref, gates_ref, wg_ref, wu_ref, wd_ref, *refs):
    gi_ref, gg_ref, ug_ref, dots_ref, both, down = refs[after:]
    step = pl.program_id(0)
    many, _, hid = wg_ref.shape
    for part in range(many):
        both[:, part * hid : (part + 1) * hid] = wg_ref[part]
        both[:, (many + part) * hid : (many + part + 1) * hid] = wu_ref[part]
        down[:, part * hid : (part + 1) * hid] = wd_ref[part]

    @pl.when(step == 0)
    def _():
        dots_ref[...] = jnp.zeros_like(dots_ref)

    def body(index, carry):
        here = pl.ds(pl.multiple_of(index * rows, rows), rows)
        acts = dot(mixed_ref[here, :], both[...])
        low_grads = dot(dy_ref[here, :], down[...])
        gates = gates_ref[here, :]
        totals = dots_ref[here, :]
        lane = lax.broadcasted_iota(jnp.int32, gates.shape, 1)
        spot = lax.broadcasted_iota(jnp.int32, totals.shape, 1)
        for part in range(many):
            chosen = lane == step * many + part
            gate = jnp.sum(jnp.where(chosen, gates, 0.0), axis=1, keepdims=True)
            span = slice(part * hid, (part + 1) * hid)
            other = slice((many + part) * hid, (many + part + 1) * hid)
            gi, gg, ug, terms = expert_terms(acts[:, span], acts[:, other], low_grads[:, span], gate)
            gi_ref[here, span] = gi
            gg_ref[here, span] = gg
            ug_ref[here, span] = ug
            mine = spot == step * many + part
            totals = jnp.where(mine, jnp.sum(terms, axis=1, keepdims=True), totals)
        dots_ref[here, :] = totals
        return carry

    lax.fori_loop(0, mixed_ref.shape[0] // rows, body, 0)


def expert_acts(mixed, dy, chunk, gates, w_gate, w_up, w_down, after=(), last=False):
    tokens, width = mixed.shape
    experts, _, hid = w_gate.shape
    many = 2
    weight = pl.BlockSpec((many, width, hid), lambda e: (e, 0, 0))
    wide = pl.BlockSpec((tokens, many * hid), lambda e: (0, e))
    wide_shape = jax.ShapeDtypeStruct((tokens, experts * hid), BF)
    return pl.pallas_call(
        functools.partial(expert_kernel, min(256, tokens), len(after)),
        grid=(experts // many,),
        in_specs=[
            whole_spec(mixed.shape),
            pl.BlockSpec(
                mixed.shape, lambda e: (chunk, 0), pipeline_mode=pl.Buffered(buffer_count=1)
            ),
            whole_spec(gates.shape),
            weight,
            weight,
            weight,
        ]
        + [ANY] * len(after),
        out_specs=[wide, wide, wide, whole_spec((tokens, LANES))],
        out_shape=[wide_shape, wide_shape, wide_shape, jax.ShapeDtypeStruct((tokens, LANES), F32)],
        scratch_shapes=[
            pltpu.VMEM((width, 2 * many * hid), BF),
            pltpu.VMEM((width, many * hid), BF),
        ],
        compiler_params=params(58),
        cost_estimate=cost(6 * tokens * width * experts * hid, 12 * tokens * width, last),
        name="expert_acts",
    )(mixed, dy, gates, w_gate, w_up, w_down, *after)


def fill(held, weight):
    experts, _, hid = weight.shape
    for expert in range(experts):
        held[:, expert * hid : (expert + 1) * hid] = weight[expert]


def back_columns_kernel(rows, count, extra, after, table_ref, rank_ref, *refs):
    lefts, weights = refs[:count], refs[count : 2 * count]
    more = refs[2 * count : 2 * count + extra]
    refs = refs[2 * count + extra + after :]
    outs, held = refs[:-count], refs[-count:]
    step = pl.program_id(0)
    for index in range(count):
        fill(held[index], weights[index])
    places = [out.at[part] for out in outs for part in range(out.shape[0])]
    for number, out_ref in enumerate(places):

        @pl.when(step == number)
        def _(out_ref=out_ref):
            def body(index, carry):
                here = pl.ds(pl.multiple_of(index * rows, rows), rows)
                total = dot(lefts[0][here, :], held[0][...], 1, 1)
                for left, right in zip(lefts[1:], held[1:]):
                    total = total + dot(left[here, :], right[...], 1, 1)
                out_ref[here, :] = total
                return carry

            lax.fori_loop(0, out_ref.shape[0] // rows, body, 0)
            for added in more:
                own = added.shape[0]
                out_ref[pl.ds(pl.multiple_of(rank_ref[0] * own, own), own), :] += added[...]


def back_columns(
    lefts, weights, table, groups, after=(), last=False, rank=None, added=(), chunk=0
):
    rank = jnp.zeros((1,), jnp.int32) if rank is None else rank.reshape(1)
    table = table[jnp.array([k for group in groups for k in group], jnp.int32)]
    tokens = lefts[0].shape[0]
    experts, width, hid = weights[0].shape
    count, parts = len(lefts), table.shape[0]
    block = width // parts
    return pl.pallas_call(
        functools.partial(
            back_columns_kernel, min(512, tokens), count, len(added), len(after)
        ),
        grid_spec=pltpu.PrefetchScalarGridSpec(
            num_scalar_prefetch=2,
            grid=(parts,),
            in_specs=[whole_spec(left.shape) for left in lefts]
            + [pl.BlockSpec((experts, block, hid), lambda d, table, _: (0, table[d], 0))] * count
            + [
                pl.BlockSpec((tokens // parts, block), lambda d, table, _: (chunk, table[d]))
                for item in added
            ]
            + [ANY] * len(after),
            out_specs=[whole_spec((len(group), tokens, block)) for group in groups],
            scratch_shapes=[pltpu.VMEM((block, experts * hid), BF)] * count,
        ),
        out_shape=[jax.ShapeDtypeStruct((len(group), tokens, block), F32) for group in groups],
        compiler_params=params(56),
        cost_estimate=cost(
            2 * count * tokens * width * experts * hid, (4 + 4 * count) * tokens * width, last
        ),
        name="back_columns",
    )(table, rank, *lefts, *weights, *added, *after)


def back_rows_kernel(rows, count, after, table_ref, *refs):
    lefts, weights, dots_ref = refs[:count], refs[count : 2 * count], refs[2 * count]
    refs = refs[2 * count + 1 + after :]
    outs, held, turned = refs[: -2 * count], refs[-2 * count : -count], refs[-count:]
    outs = [out.at[part] for out in outs for part in range(out.shape[0])]
    part_rows = outs[0].shape[0]
    block = held[0].shape[0]
    width = outs[0].shape[1] - LANES
    for index in range(count):
        fill(held[index], weights[index])

    @pl.when(pl.program_id(0) == 0)
    def _():
        for number in range(len(outs)):
            here = pl.ds(pl.multiple_of(table_ref[number] * part_rows, part_rows), part_rows)
            there = slice(number * part_rows, (number + 1) * part_rows)
            for index in range(count):
                turned[index][there, :] = lefts[index][here, :]
            outs[number][:, width:] = dots_ref[here, :]

    columns = pl.ds(pl.multiple_of(pl.program_id(0) * block, block), block)
    for step in range(len(outs) * part_rows // rows):
        here = slice(step * rows, (step + 1) * rows)
        total = dot(turned[0][here, :], held[0][...], 1, 1)
        for left, right in zip(turned[1:], held[1:]):
            total = total + dot(left[here, :], right[...], 1, 1)
        for part in range(rows // part_rows):
            number = step * (rows // part_rows) + part
            outs[number][:, columns] = total[part * part_rows : (part + 1) * part_rows]


def back_rows(lefts, weights, dots, table, groups, after=()):
    table = table[jnp.array([k for group in groups for k in group], jnp.int32)]
    tokens = lefts[0].shape[0]
    experts, width, hid = weights[0].shape
    count, parts = len(lefts), table.shape[0]
    block = min(256, width)
    part_rows = tokens // parts
    return pl.pallas_call(
        functools.partial(back_rows_kernel, min(512, tokens), count, len(after)),
        grid_spec=pltpu.PrefetchScalarGridSpec(
            num_scalar_prefetch=1,
            grid=(width // block,),
            in_specs=[whole_spec(left.shape) for left in lefts]
            + [pl.BlockSpec((experts, block, hid), lambda d, _: (0, d, 0))] * count
            + [whole_spec(dots.shape)]
            + [ANY] * len(after),
            out_specs=[whole_spec((len(group), part_rows, width + LANES)) for group in groups],
            scratch_shapes=[pltpu.VMEM((block, experts * hid), BF)] * count
            + [pltpu.VMEM(left.shape, BF) for left in lefts],
        ),
        out_shape=[
            jax.ShapeDtypeStruct((len(group), part_rows, width + LANES), F32) for group in groups
        ],
        compiler_params=params(56),
        cost_estimate=cost(
            2 * count * tokens * width * experts * hid, (4 + 4 * count) * tokens * width
        ),
        name="back_rows",
    )(table, *lefts, *weights, dots, *after)


def grads_kernel(rows, chunks, after, *refs):
    lefts = refs[:chunks]
    rest = refs[chunks + after :]
    count = (len(rest) - 2 * chunks) // (chunks + 1)
    rights = [rest[c * count : (c + 1) * count] for c in range(chunks)]
    outs = rest[chunks * count : (chunks + 1) * count]
    held, turned = rest[(chunks + 1) * count : -chunks], rest[-chunks:]
    many, width, hid = outs[0].shape

    @pl.when(pl.program_id(0) == 0)
    def _():
        for chunk in range(chunks):
            wide = 256
            for start in range(0, width, wide):
                turned[chunk][start : start + wide, :] = lefts[chunk][:, start : start + wide].T

    for chunk in range(chunks):
        for index, right in enumerate(rights[chunk]):
            held[chunk][:, index * many * hid : (index + 1) * many * hid] = right[...]

    def body(index, carry):
        here = pl.ds(pl.multiple_of(index * rows, rows), rows)
        total = dot(turned[0][here, :], held[0][...])
        for chunk in range(1, chunks):
            total = total + dot(turned[chunk][here, :], held[chunk][...])
        for which, out in enumerate(outs):
            for part in range(many):
                place = (which * many + part) * hid
                out[part, here, :] = total[:, place : place + hid]
        return carry

    lax.fori_loop(0, width // rows, body, 0)


def expert_grads(lefts, rights, experts, after=()):
    chunks, count = len(rights), len(rights[0])
    tokens = rights[0][0].shape[0]
    width = lefts[0].shape[1]
    hid = rights[0][0].shape[1] // experts
    many = 2
    if len(lefts) == chunks:
        left_specs = [whole_spec(left.shape) for left in lefts]
    else:
        left_specs = [
            pl.BlockSpec(
                (tokens, width),
                lambda e, chunk=chunk: (chunk, 0),
                pipeline_mode=pl.Buffered(buffer_count=1),
            )
            for chunk in range(chunks)
        ]
        lefts = list(lefts) * chunks
    return pl.pallas_call(
        functools.partial(grads_kernel, min(512, width), chunks, len(after)),
        grid=(experts // many,),
        in_specs=left_specs
        + [ANY] * len(after)
        + [pl.BlockSpec((tokens, many * hid), lambda e: (0, e))] * (count * chunks),
        out_specs=[pl.BlockSpec((many, width, hid), lambda e: (e, 0, 0))] * count,
        out_shape=[jax.ShapeDtypeStruct((experts, width, hid), F32)] * count,
        scratch_shapes=[pltpu.VMEM((tokens, count * many * hid), BF)] * chunks
        + [pltpu.VMEM((width, tokens), BF)] * chunks,
        compiler_params=params(58),
        cost_estimate=cost(
            2 * count * chunks * tokens * width * experts * hid, 6 * count * experts * hid * width
        ),
        name="expert_grads",
    )(*lefts, *after, *[item for chunk in rights for item in chunk])


def branch_kernel(count, after, table_ref, *refs):
    pieces = refs[:count]
    w_ref, x_ref, gain_ref, router_ref = refs[count : count + 4]
    mid_ref, mixed_ref, logit_ref, all_ref = refs[count + 4 + after :]
    share = pieces[0].shape[1]
    for index, piece in enumerate(pieces):
        span = pl.ds(pl.multiple_of(table_ref[index] * share, LANES), share)
        all_ref[:, span] = piece[...].astype(BF)
    middle = x_ref[...].astype(F32) + dot(all_ref[...], w_ref[...], 1, 1)
    mid_ref[...] = middle
    mid_hat = middle * norm_scale(middle)
    mixed = (mid_hat * gain_ref[...].astype(F32)).astype(BF)
    mixed_ref[...] = mixed
    logit_ref[...] = dot(mixed, router_ref[...])


def branch(pieces, table, w_out, hidden, chunk, gain, w_router, after=()):
    tokens, share = pieces[0].shape
    width, full = w_out.shape
    rows = min(256, tokens)
    steps = tokens // rows
    experts = w_router.shape[1]
    return pl.pallas_call(
        functools.partial(branch_kernel, len(pieces), len(after)),
        grid_spec=pltpu.PrefetchScalarGridSpec(
            num_scalar_prefetch=1,
            grid=(steps,),
            in_specs=[pl.BlockSpec((rows, share), lambda i, _: (i, 0))] * len(pieces)
            + [
                whole_spec(w_out.shape),
                pl.BlockSpec((rows, width), lambda i, _: (chunk * steps + i, 0)),
                whole_spec((1, width)),
                whole_spec(w_router.shape),
            ]
            + [ANY] * len(after),
            out_specs=[
                pl.BlockSpec((rows, width), lambda i, _: (i, 0)),
                pl.BlockSpec((rows, width), lambda i, _: (i, 0)),
                pl.BlockSpec((rows, experts), lambda i, _: (i, 0)),
                pl.BlockSpec((rows, full), lambda i, _: (i, 0)),
            ],
        ),
        out_shape=[
            jax.ShapeDtypeStruct((tokens, width), F32),
            jax.ShapeDtypeStruct((tokens, width), BF),
            jax.ShapeDtypeStruct((tokens, experts), F32),
            jax.ShapeDtypeStruct((tokens, full), BF),
        ],
        compiler_params=params(56),
        cost_estimate=cost(2 * tokens * width * full, 16 * tokens * width),
        name="branch",
    )(table, *pieces, w_out, hidden, gain.reshape(1, -1), w_router, *after)


def cast_kernel(in_ref, out_ref):
    out_ref[...] = in_ref[...].astype(out_ref.dtype)


def cast(value):
    rows, columns = value.shape
    block = pl.BlockSpec((min(256, rows), columns), lambda i: (i, 0))
    return pl.pallas_call(
        cast_kernel,
        grid=(rows // min(256, rows),),
        in_specs=[block],
        out_specs=block,
        out_shape=jax.ShapeDtypeStruct(value.shape, BF),
        compiler_params=params(32),
        cost_estimate=cost(0, 6 * value.size),
        name="cast",
    )(value)


def send_back_kernel(after, table_ref, low_ref, w_ref, *outs):
    for number, out_ref in enumerate(outs[after:]):

        @pl.when(pl.program_id(0) == number)
        def _(out_ref=out_ref):
            out_ref[...] = dot(low_ref[...], w_ref[...]).astype(BF).astype(F32)


def send_back(low, w_out, table, after=()):
    rows, width = low.shape
    parts = table.shape[0]
    full = w_out.shape[1]
    block = full // parts
    return pl.pallas_call(
        functools.partial(send_back_kernel, len(after)),
        grid_spec=pltpu.PrefetchScalarGridSpec(
            num_scalar_prefetch=1,
            grid=(parts,),
            in_specs=[
                whole_spec(low.shape),
                pl.BlockSpec((width, block), lambda k, table: (0, table[k])),
            ]
            + [ANY] * len(after),
            out_specs=[whole_spec((rows, block))] * parts,
        ),
        out_shape=[jax.ShapeDtypeStruct((rows, block), F32)] * parts,
        compiler_params=params(32),
        cost_estimate=cost(2 * rows * width * full, 2 * width * full + 8 * rows * full),
        name="send_back",
    )(table, low, w_out, *after)


def outer_kernel(after, table_ref, columns_ref, left_ref, right_ref, *outs):
    for number, out_ref in enumerate(outs[after:]):

        @pl.when(pl.program_id(0) == number)
        def _(out_ref=out_ref):
            out_ref[0] = dot(left_ref[...], right_ref[...])


def outer(left, right, table, columns, after=()):
    width, rows = left.shape
    parts, pieces = table.shape[0], columns.shape[0]
    high, wide = width // parts, right.shape[1] // pieces
    out_specs = [
        pl.BlockSpec(
            (1, high, wide),
            lambda k, m, *_, number=number: (
                jnp.where(k < number, 0, jnp.where(k > number, pieces - 1, m)),
                0,
                0,
            ),
        )
        for number in range(parts)
    ]
    return pl.pallas_call(
        functools.partial(outer_kernel, len(after)),
        grid_spec=pltpu.PrefetchScalarGridSpec(
            num_scalar_prefetch=2,
            grid=(parts, pieces),
            in_specs=[
                pl.BlockSpec((high, rows), lambda k, m, table, columns: (table[k], 0)),
                pl.BlockSpec((rows, wide), lambda k, m, table, columns: (0, columns[m])),
            ]
            + [ANY] * len(after),
            out_specs=out_specs,
        ),
        out_shape=[jax.ShapeDtypeStruct((pieces, high, wide), F32)] * parts,
        compiler_params=params(32),
        cost_estimate=cost(2 * width * rows * right.shape[1], 4 * width * right.shape[1]),
        name="outer",
    )(table, columns, left, right, *after)


def plain_acts(mixed, dy, chunk, gates, w_gate, w_up, w_down, after=(), last=False):
    dy = lax.dynamic_slice_in_dim(dy, chunk * mixed.shape[0], mixed.shape[0], 0)
    acts = jnp.einsum("td,edh->teh", mixed, w_gate, preferred_element_type=F32)
    ups = jnp.einsum("td,edh->teh", mixed, w_up, preferred_element_type=F32)
    low = jnp.einsum("td,edh->teh", dy, w_down, preferred_element_type=F32)
    gi, gg, ug, terms = expert_terms(acts, ups, low, gates[:, :, None])
    flat = (mixed.shape[0], -1)
    dots = jnp.pad(jnp.sum(terms, axis=2), ((0, 0), (0, LANES - gates.shape[1])))
    return gi.reshape(flat), gg.reshape(flat), ug.reshape(flat), dots


def plain_back(lefts, weights):
    experts, _, hid = weights[0].shape
    total = 0.0
    for left, weight in zip(lefts, weights):
        total = total + jnp.einsum(
            "teh,edh->td", left.reshape(-1, experts, hid), weight, preferred_element_type=F32
        )
    return total


def plain_columns(
    lefts, weights, table, groups, after=(), last=False, rank=None, added=(), chunk=0
):
    total = plain_back(lefts, weights)
    for item in added:
        own = total.shape[0] // table.shape[0]
        mine = lax.slice_in_dim(item, chunk * own, (chunk + 1) * own, axis=0)
        rows = lax.dynamic_slice_in_dim(total, rank * own, own, 0) + mine
        total = lax.dynamic_update_slice_in_dim(total, rows, rank * own, 0)
    block = total.shape[1] // table.shape[0]
    return [
        jnp.stack([lax.dynamic_slice_in_dim(total, table[k] * block, block, 1) for k in group])
        for group in groups
    ]


def plain_rows(lefts, weights, dots, table, groups, after=()):
    total = jnp.concatenate([plain_back(lefts, weights), dots], axis=1)
    block = total.shape[0] // table.shape[0]
    return [
        jnp.stack([lax.dynamic_slice_in_dim(total, table[k] * block, block, 0) for k in group])
        for group in groups
    ]


def plain_grads(lefts, rights, experts, after=()):
    left = jnp.concatenate(lefts, axis=0)
    return [
        jnp.einsum(
            "td,teh->edh",
            left,
            jnp.concatenate(parts, axis=0).reshape(left.shape[0], experts, -1),
            preferred_element_type=F32,
        )
        for parts in zip(*rights)
    ]


def bits_of(count):
    if count & (count - 1):
        raise ValueError("tensor axis")
    return [1 << bit for bit in range(count.bit_length() - 1)]


def swap(value, axis, step):
    count = lax.axis_size(axis)
    return lax.ppermute(value, axis, [(i, i ^ step) for i in range(count)])


def reduce_blocks(blocks, axis="tensor"):
    blocks = list(blocks)
    live = list(range(len(blocks)))
    for bit in bits_of(len(blocks)):
        for k in sorted((k for k in live if k & bit), reverse=True):
            blocks[k ^ bit] = blocks[k ^ bit] + swap(blocks[k], axis, bit)
        live = [k for k in live if not k & bit]
    return blocks[0]


def stage_kernel(sizes, skip, *refs):
    count = sum(sizes)
    terms = refs[:count]
    outs = list(refs[count + skip :])
    used = 0
    for size in sizes:
        total = terms[used][...]
        for term in terms[used + 1 : used + size]:
            total = total + term[...]
        used += size
        done = 0
        while done < total.shape[0]:
            out = outs.pop(0)
            out[...] = total[done : done + out.shape[0]]
            done += out.shape[0]


def stage(sums, passes=(), after=()):
    steps = 4
    terms = [term for _, group in sums for term in group]
    in_specs, out_specs, out_shape = [], [], []
    for term in terms:
        parts, rows, columns = term.shape
        in_specs.append(pl.BlockSpec((parts, rows // steps, columns), lambda i: (0, i, 0)))
    for cuts, group in sums:
        _, rows, columns = group[0].shape
        for parts in cuts:
            out_specs.append(pl.BlockSpec((parts, rows // steps, columns), lambda i: (0, i, 0)))
            out_shape.append(jax.ShapeDtypeStruct((parts, rows, columns), F32))
    made = len(out_shape)
    out_shape += [jax.ShapeDtypeStruct(item.shape, item.dtype) for item in passes]
    outs = pl.pallas_call(
        functools.partial(
            stage_kernel, tuple(len(group) for _, group in sums), len(passes) + len(after)
        ),
        grid=(steps,),
        in_specs=in_specs + [ANY] * (len(passes) + len(after)),
        out_specs=out_specs + [ANY] * len(passes),
        out_shape=out_shape,
        input_output_aliases={len(terms) + i: made + i for i in range(len(passes))},
        compiler_params=params(32),
        cost_estimate=cost(0, sum(4 * term.size for term in terms) * 4 // 3),
        name="stage",
    )(*terms, *passes, *after)
    return outs[:made], outs[made:]


def tie_kernel(*refs):
    pass


def tie(values, after):
    return pl.pallas_call(
        tie_kernel,
        in_specs=[ANY] * (len(values) + len(after)),
        out_specs=[ANY] * len(values),
        out_shape=[jax.ShapeDtypeStruct(value.shape, value.dtype) for value in values],
        input_output_aliases={i: i for i in range(len(values))},
        compiler_params=params(58),
        name="tie",
    )(*values, *after)


class Chain:
    groups = ((7, 3), (5, 1), (6, 2), (4, 0))

    def __init__(self, parts):
        self.first, self.second, self.six_two, self.four_zero = parts

    def send_first(self):
        self.got_first = swap(self.first, "tensor", 1)

    def send_second(self):
        self.got_second = swap(self.second, "tensor", 1)
        self.got_near = swap(self.six_two, "tensor", 2)

    def send_far(self):
        self.got_far = swap(self.four, "tensor", 4)


def odd_stage(ending, starting, passes=(), after=(), hold=False):
    sums = []
    passes = list(passes)
    if starting is not None:
        sums.append(((2,), (starting.six_two, starting.got_first)))
        passes.append(starting.second)
    if ending is not None:
        sums.append(((1,), (ending.zero, ending.got_far)))
    made, passes = stage(sums, passes, after)
    if ending is not None:
        ending.result = made[-1]
    if starting is not None:
        starting.six_two = made[0]
        starting.second = passes[-1]
        if not hold:
            starting.send_second()
        passes = passes[:-1]
    return passes


def even_stage(middle, coming, passes=(), after=()):
    passes = list(passes)
    if coming is not None:
        passes.append(coming.first)
    made, passes = stage(
        [((1, 1), (middle.four_zero, middle.got_second, middle.got_near))], passes, after
    )
    middle.four, middle.zero = made
    middle.send_far()
    if coming is not None:
        coming.first = passes[-1]
        coming.send_first()
        passes = passes[:-1]
    return passes


def halves_order(count):
    bits = bits_of(count)
    return [
        sum(bit for bit, other in zip(bits, reversed(bits)) if m & other) for m in range(count)
    ]


def reduce_halves(stacked, axis="tensor"):
    for bit in bits_of(stacked.shape[0]):
        half = stacked.shape[0] // 2
        stacked = stacked[:half] + swap(stacked[half:], axis, bit)
    return stacked[0]


def gather_blocks(value):
    count = lax.axis_size("tensor")
    have = {0: value}
    for bit in reversed(bits_of(count)):
        for k in sorted(have):
            have[k ^ bit] = swap(have[k], "tensor", bit)
    return [have[k] for k in range(count)]


def exchange_blocks(blocks):
    return [blocks[0]] + [swap(blocks[k], "tensor", k) for k in range(1, len(blocks))]


def small_sum(value, axis):
    for bit in bits_of(lax.axis_size(axis)):
        value = value + swap(value, axis, bit)
    return value


def on_device(
    hidden_in,
    cotangent,
    routes,
    segments,
    gain_in,
    w_query,
    w_key,
    w_value,
    w_out,
    gain_query,
    gain_key,
    gain_mid,
    w_router,
    w_gate,
    w_up,
    w_down,
):
    count = lax.axis_size("tensor")
    rank = lax.axis_index("tensor")
    dp_count = lax.axis_size("dp")
    dp_rank = lax.axis_index("dp")
    tok_rows, width = hidden_in.shape
    local_width = w_query.shape[1]
    heads_here = local_width // HEAD
    full_width = local_width * count
    share = width // count
    experts = w_gate.shape[0]
    seqs, length = segments.shape
    own = length // count
    scale = 1.0 / math.sqrt(HEAD)
    tiled = w_gate.shape[2] % LANES == 0
    acts_of = expert_acts if tiled else plain_acts
    columns_of = back_columns if tiled else plain_columns
    rows_of = back_rows if tiled else plain_rows
    grads_of = expert_grads if tiled else plain_grads
    table = rank ^ jnp.arange(count, dtype=jnp.int32)
    chunks = range(seqs)

    part = width // dp_count
    w_part = lax.dynamic_slice_in_dim(w_out, dp_rank * part, part, 0).astype(F32)
    w_part = lax.all_gather(w_part, "tensor", axis=1, tiled=True)

    hidden = hidden_in.astype(F32)
    in_scale = norm_scale(hidden)
    in_hat = hidden * in_scale
    normed, query_raw, key_raw, value_low, square_sums = project(
        hidden_in, gain_in, w_query, w_key, w_value
    )
    raws = (query_raw, key_raw)
    square_sums = small_sum(square_sums, "tensor")
    angles = jnp.concatenate(
        rotary_tables(document_positions(segments).reshape(-1), HEAD), axis=1
    )
    gains_here = (gain_query.reshape(1, -1), gain_key.reshape(1, -1))
    expert_ids = jnp.arange(experts, dtype=jnp.int32)
    hits = jnp.any(routes[:, :, None] == expert_ids[None, None, :], axis=1)
    counts = hits.astype(jnp.int32)
    kept_all = hits & (jnp.cumsum(counts, axis=0, dtype=jnp.int32) - counts < CAP)

    pieces, last, query_low, key_low = [], None, [], []
    for c in chunks:
        last, query_c, key_c = attend(
            query_raw, key_raw, value_low, square_sums, gains_here, angles, segments, c, scale,
            full_width,
        )
        query_low.append(query_c)
        key_low.append(key_c)
        pieces.append(gather_blocks(last))
    query_low = jnp.concatenate(query_low, axis=0)
    key_low = jnp.concatenate(key_low, axis=0)
    w_part, _ = lax.optimization_barrier((w_part, last))
    w_whole = cast(lax.all_gather(w_part, "dp", axis=0, tiled=True))

    staged = count == 8 and seqs == 2
    groups = Chain.groups if staged else tuple((k,) for k in range(count))

    def plain_reduce(parts):
        return reduce_blocks([item[0] for item in parts])

    middle, mixed, attended, probs, kept, gates = ([] for _ in range(6))

    def forward(c, after, last=False):
        mid_c, mixed_c, logits_c, attended_c = branch(
            pieces[c], table, w_whole, hidden_in, c, gain_mid, w_router, after
        )
        middle.append(mid_c)
        mixed.append(mixed_c)
        attended.append(attended_c)
        probs.append(jax.nn.softmax(logits_c, axis=-1))
        kept.append(lax.slice_in_dim(kept_all, c * length, (c + 1) * length, axis=0))
        gates.append(jnp.where(kept[c], probs[c], 0.0))
        return acts_of(mixed_c, cotangent, c, gates[c], w_gate, w_up, w_down, (), last)

    def mixed_blocks(c, after=()):
        return rows_of(acts[c][1:3], [w_gate, w_up], acts[c][3], table, groups, after)

    def moe_of(c, after=(), last=False):
        return columns_of([acts[c][0]], [w_down], table, groups, after, last)

    def down_grads(after=()):
        return grads_of([cotangent], [a[:1] for a in acts], experts, after)[0]

    def act_grads(after=()):
        return grads_of(mixed, [a[1:3] for a in acts], experts, after)

    def rows_own(value, start=0):
        return lax.dynamic_slice_in_dim(value, start + rank * own, own, 0)

    def columns_own(value):
        return lax.dynamic_slice_in_dim(value, rank * share, share, 1)

    if staged:
        acts = [forward(0, ())]
        mix = [Chain(mixed_blocks(0))]
        mix[0].send_first()
        acts.append(forward(1, (mix[0].four_zero,), True))
        odd_stage(None, mix[0], after=(acts[1][0],))
        mix.append(Chain(mixed_blocks(1, (mix[0].six_two,))))
        even_stage(mix[0], mix[1])
        moe = [Chain(moe_of(0, (mix[0].zero,)))]
        odd_stage(mix[0], mix[1], after=(moe[0].four_zero,))
    else:
        acts = []
        for c in chunks:
            acts.append(forward(c, ()))
        mixed_share = [plain_reduce(mixed_blocks(c)) for c in chunks]
        moe_share = [plain_reduce(moe_of(c)) for c in chunks]
        grad_down = down_grads()
        grad_gate, grad_up = act_grads()

    def all_own(values):
        return jnp.concatenate([rows_own(value) for value in values], axis=0)

    probs_own, kept_own, mid_own = all_own(probs), all_own(kept), all_own(middle)
    mixed_own, attended_own = all_own(mixed), all_own(attended)
    dy_own = jnp.concatenate([rows_own(cotangent, c * length) for c in chunks], axis=0)

    if staged:
        grad_down = down_grads((mix[1].six_two, probs_own, mid_own, mixed_own, attended_own))
        (grad_down,) = even_stage(mix[1], moe[0], passes=(grad_down,))
        grad_gate, grad_up = act_grads((mix[1].zero,))
        grad_gate, grad_up = odd_stage(mix[1], moe[0], passes=(grad_gate, grad_up))
        mixed_share = [item.result[0] for item in mix]

    mixed_share = jnp.concatenate(mixed_share, axis=0)
    prob_grad = jnp.where(kept_own, mixed_share[:, width : width + experts], 0.0)
    logit_own = (
        probs_own * (prob_grad - jnp.sum(probs_own * prob_grad, axis=-1, keepdims=True))
    ).astype(BF)
    mixed_grad = mixed_share[:, :width] + dot(logit_own, w_router, 1, 1)
    mid_scale = norm_scale(mid_own)
    mid_hat = mid_own * mid_scale
    grad_gain_mid = jnp.sum(mixed_grad * mid_hat, axis=0)
    scaled = mixed_grad * gain_mid.astype(F32)
    mid_grad = dy_own.astype(F32) + mid_scale * (
        scaled - mid_hat * jnp.mean(scaled * mid_hat, axis=1, keepdims=True)
    )
    mid_low = mid_grad.astype(BF)
    if staged:
        moe.append(Chain(moe_of(1, (mid_low,), True)))
        (mid_low,) = even_stage(moe[0], moe[1], passes=(mid_low,))
    blocks = send_back(mid_low, w_whole, table)
    attended_grad = jnp.stack(exchange_blocks(blocks))

    q_scaled, k_scaled, value_grad, totals, gain_parts = attend_back(
        query_low, key_low, value_low, attended_grad, raws, square_sums, gains_here, angles,
        table, segments, scale, full_width,
    )
    if staged:
        (totals,) = odd_stage(moe[0], moe[1], passes=(totals,), hold=True)
    gain_parts = jnp.sum(gain_parts.reshape(seqs, 8, local_width), axis=0)
    totals = small_sum(totals, "tensor")
    query_grad, key_grad = raw_grads((q_scaled, k_scaled), raws, square_sums, totals, full_width)
    in_grads = [query_grad, key_grad, value_grad]
    weights_in = [w[None] for w in (w_query, w_key, w_value)]
    columns_in = back_columns if local_width % LANES == 0 and share % LANES == 0 else plain_columns

    hidden_own = jnp.concatenate([rows_own(hidden_in, c * length) for c in chunks], axis=0)
    hidden_own = hidden_own.astype(F32)
    own_scale = norm_scale(hidden_own)
    own_hat = hidden_own * own_scale
    direct = mid_grad / (own_scale * gain_in.astype(F32))

    def normed_blocks(c):
        part_grads = [grad[c * length : (c + 1) * length] for grad in in_grads]
        return columns_in(
            part_grads, weights_in, table, groups, rank=rank, added=(direct,), chunk=c
        )

    if staged:
        moe[1].second, moe[1].six_two = tie((moe[1].second, moe[1].six_two), (totals,))
        moe[1].send_second()
        norm = [Chain(normed_blocks(c)) for c in chunks]
        even_stage(moe[1], norm[0], after=(norm[1].four_zero,))
        odd_stage(moe[1], norm[0])
        even_stage(norm[0], norm[1])
        odd_stage(norm[0], norm[1])
        even_stage(norm[1], None)
        odd_stage(norm[1], None)
        normed_share = [item.result[0] for item in norm]
        moe_share = [item.result[0] for item in moe]
    else:
        normed_share = [plain_reduce(normed_blocks(c)) for c in chunks]
    output = jnp.concatenate(
        [(columns_own(middle[c]) + moe_share[c]).astype(BF) for c in chunks], axis=0
    )

    def over_dp(grad):
        return lax.psum_scatter(grad, "dp", scatter_dimension=0, tiled=True)

    dp_table = dp_rank ^ jnp.arange(dp_count, dtype=jnp.int32)
    order = rank ^ jnp.array(halves_order(count), jnp.int32)
    out_part = reduce_blocks(outer(mid_low.T, attended_own, dp_table, order, (blocks[0],)), "dp")
    grad_w_out = reduce_halves(out_part)

    grad_in = dot(normed, jnp.concatenate(in_grads, axis=1), 0, 0)
    grad_in = reduce_blocks(
        [lax.dynamic_slice_in_dim(grad_in, dp_table[k] * part, part, 0) for k in range(dp_count)],
        "dp",
    )
    grad_w_query, grad_w_key, grad_w_value = (
        grad_in[:, i * local_width : (i + 1) * local_width] for i in range(3)
    )

    normed_share = jnp.concatenate(normed_share, axis=0)
    in_hat_share = columns_own(in_hat)
    gain_share = lax.dynamic_slice_in_dim(gain_in.astype(F32), rank * share, share, 0)
    in_scaled = normed_share * gain_share
    row_sums = jnp.sum(in_scaled * in_hat_share, axis=1).reshape(seqs, length)
    direct_sums = jnp.sum(mid_grad * own_hat, axis=1) / own_scale[:, 0]
    mine = lax.dynamic_slice_in_dim(row_sums, rank * own, own, 1) - direct_sums.reshape(seqs, own)
    row_sums = lax.dynamic_update_slice_in_dim(row_sums, mine, rank * own, 1)
    row_totals = small_sum(row_sums.reshape(1, tok_rows), "tensor")[0]
    grad_input = (
        in_scale * (in_scaled - in_hat_share * (row_totals / width)[:, None])
    ).astype(BF)
    direct_gain = jnp.sum(direct * own_hat, axis=0)
    grad_router = dot(logit_own, mixed_own, 0, 0)
    wide = jnp.concatenate([grad_router, grad_gain_mid[None], direct_gain[None]], axis=0)
    wide = small_sum(wide, "tensor")
    direct_gain = lax.dynamic_slice_in_dim(wide[experts + 1], rank * share, share, 0)
    grad_gain_in = jnp.sum(normed_share * in_hat_share, axis=0) - direct_gain

    wide = small_sum(wide[: experts + 1], "dp")
    wide = lax.dynamic_slice_in_dim(wide, dp_rank * part, part, 1)
    gains = jnp.concatenate([grad_gain_in, gain_parts[0], gain_parts[1]])
    gains = small_sum(gains[None], "dp")[0]

    return (
        output,
        grad_input,
        grad_w_query,
        grad_w_key,
        grad_w_value,
        grad_w_out,
        gains[:share],
        gains[share : share + local_width],
        gains[share + local_width :],
        wide[experts],
        wide[:experts].T,
        over_dp(grad_gate),
        over_dp(grad_up),
        over_dp(grad_down),
    )


def solution(mesh):
    in_specs = (
        P("dp", None),
        P("dp", None),
        P("dp", None),
        P("dp", None),
        P(),
        P(None, "tensor"),
        P(None, "tensor"),
        P(None, "tensor"),
        P(None, "tensor"),
        P("tensor"),
        P("tensor"),
        P(),
        P(),
        P(None, None, "tensor"),
        P(None, None, "tensor"),
        P(None, None, "tensor"),
    )
    out_specs = (
        P("dp", "tensor"),
        P("dp", "tensor"),
        P("dp", "tensor"),
        P("dp", "tensor"),
        P("dp", "tensor"),
        P("dp", "tensor"),
        P("tensor"),
        P("tensor"),
        P("tensor"),
        P("dp"),
        P("dp", None),
        P("dp", None, "tensor"),
        P("dp", None, "tensor"),
        P("dp", None, "tensor"),
    )
    return jax.shard_map(
        on_device, mesh=mesh, in_specs=in_specs, out_specs=out_specs, check_vma=False
    )
```

```python
import functools
import math

import jax
import jax.numpy as jnp
from jax import lax
from jax.experimental import pallas as pl
from jax.experimental.pallas import tpu as pltpu
from jax.sharding import PartitionSpec as P

HEAD = 128
CAP = 1280
LONGEST = 512
EPSILON = 1e-05
MASKED = -1e30
LANES = 128
MIB = 1 << 20
BF = jnp.bfloat16
F32 = jnp.float32


ANY = pl.BlockSpec(memory_space=pl.ANY)


def norm_scale(values):
    return lax.rsqrt(jnp.mean(values * values, axis=-1, keepdims=True) + EPSILON)


def document_positions(segments):
    index = jnp.broadcast_to(
        jnp.arange(segments.shape[1], dtype=jnp.int32)[None, :], segments.shape
    )
    previous = jnp.concatenate([segments[:, :1] - 1, segments[:, :-1]], axis=1)
    starts = lax.cummax(jnp.where(segments != previous, index, 0), axis=1)
    return index - starts


def rotary_tables(positions, head):
    half = head // 2
    freq = 10000.0 ** (-2.0 * jnp.arange(half, dtype=F32) / head)
    angle = positions.astype(F32)[:, None] * freq[None, :]
    return (jnp.cos(angle), jnp.sin(angle))


def dot(left, right, left_dim=1, right_dim=0):
    return lax.dot_general(
        left, right, (((left_dim,), (right_dim,)), ((), ())), preferred_element_type=F32
    )


def whole_spec(shape):
    return pl.BlockSpec(
        shape, lambda *_: (0,) * len(shape), pipeline_mode=pl.Buffered(buffer_count=1)
    )


def params(mib):
    return pltpu.CompilerParams(vmem_limit_bytes=mib * MIB)


def cost(flops, moved, last=False):
    if last:
        flops, moved = 1024, 1024
    return pl.CostEstimate(flops=int(flops), bytes_accessed=int(moved), transcendentals=0)


def across_lanes(row):
    return jnp.broadcast_to(row, (LANES, row.shape[1])).T


def along_lanes(column):
    return jnp.broadcast_to(column, (column.shape[0], LANES)).T[:8]


def project_kernel(x_ref, gain_ref, wq_ref, wk_ref, wv_ref, n_ref, q_ref, k_ref, v_ref, sums_ref):
    x = x_ref[...].astype(F32)
    normed = (x * norm_scale(x) * gain_ref[...].astype(F32)).astype(BF)
    n_ref[...] = normed
    query = dot(normed, wq_ref[...])
    key = dot(normed, wk_ref[...])
    q_ref[...] = query
    k_ref[...] = key
    v_ref[...] = dot(normed, wv_ref[...]).astype(BF)
    q_sum = along_lanes(jnp.sum(query * query, axis=1, keepdims=True))
    k_sum = along_lanes(jnp.sum(key * key, axis=1, keepdims=True))
    first = lax.broadcasted_iota(jnp.int32, q_sum.shape, 0) == 0
    sums_ref[...] = jnp.where(first, q_sum, k_sum)


def project(hidden, gain, w_query, w_key, w_value):
    tokens, width = hidden.shape
    wide = w_query.shape[1]
    rows = min(256, tokens)
    out = pl.BlockSpec((rows, wide), lambda i: (i, 0))
    return pl.pallas_call(
        project_kernel,
        grid=(tokens // rows,),
        in_specs=[pl.BlockSpec((rows, width), lambda i: (i, 0)), whole_spec((1, width))]
        + [whole_spec(w_query.shape)] * 3,
        out_specs=[
            pl.BlockSpec((rows, width), lambda i: (i, 0)),
            out,
            out,
            out,
            pl.BlockSpec((8, rows), lambda i: (0, i)),
        ],
        out_shape=[
            jax.ShapeDtypeStruct((tokens, width), BF),
            jax.ShapeDtypeStruct((tokens, wide), F32),
            jax.ShapeDtypeStruct((tokens, wide), F32),
            jax.ShapeDtypeStruct((tokens, wide), BF),
            jax.ShapeDtypeStruct((8, tokens), F32),
        ],
        compiler_params=params(58),
        cost_estimate=cost(6 * tokens * width * wide, 4 * tokens * width),
        name="project",
    )(hidden, gain.reshape(1, -1), w_query, w_key, w_value)


def key_span(block, rows):
    start = max(0, block * rows - LONGEST)
    return start, (block + 1) * rows


def masked_scores(q_rows, k_rows, seg_col, seg_row, row0, key0, scale):
    scores = dot(q_rows, k_rows, 1, 1) * scale
    row = lax.broadcasted_iota(jnp.int32, scores.shape, 0) + row0
    key = lax.broadcasted_iota(jnp.int32, scores.shape, 1) + key0
    return jnp.where((seg_col == seg_row) & (row >= key), scores, MASKED)


def both_halves(angles):
    other = pltpu.roll(angles, HEAD // 2, 1)
    low = lax.broadcasted_iota(jnp.int32, angles.shape, 1) < HEAD // 2
    return jnp.where(low, angles, other), jnp.where(low, -other, angles)


def turn(values, cosine, sine):
    return values * cosine + pltpu.roll(values, HEAD // 2, 1) * sine


def hat_scale(sums_ref, which, full):
    return lax.rsqrt(across_lanes(sums_ref[which : which + 1, :]) / full + EPSILON)


def attend_kernel(
    scale,
    block,
    full,
    after,
    q_ref,
    k_ref,
    v_ref,
    sums_ref,
    gq_ref,
    gk_ref,
    angle_ref,
    col_ref,
    row_ref,
    *refs,
):
    out_ref, ql_ref, kl_ref = refs[after:]
    length = q_ref.shape[0]
    cosine, sine = both_halves(angle_ref[...])
    for raw, which, gain, low in ((q_ref, 0, gq_ref, ql_ref), (k_ref, 1, gk_ref, kl_ref)):
        hat = raw[...] * hat_scale(sums_ref, which, full)
        low[...] = turn(hat * gain[...].astype(F32), cosine, sine).astype(BF)
    for index in range(length // block):
        start, stop = key_span(index, block)
        rows = slice(index * block, (index + 1) * block)
        scores = masked_scores(
            ql_ref[rows, :],
            kl_ref[start:stop, :],
            col_ref[rows, :],
            row_ref[0, :, start:stop],
            index * block,
            start,
            scale,
        )
        expo = jnp.exp(scores - jnp.max(scores, axis=1, keepdims=True))
        weights = (expo / jnp.sum(expo, axis=1, keepdims=True)).astype(BF)
        out_ref[rows, :] = dot(weights, v_ref[start:stop, :]).astype(BF).astype(F32)


def attend(q, k, v, sums, gains, angles, segments, chunk, scale, full, after=()):
    seqs, length = segments.shape
    heads = q.shape[1] // HEAD
    block = pl.BlockSpec((length, HEAD), lambda head: (chunk, head))
    mine = pl.BlockSpec((length, HEAD), lambda head: (0, head))
    gain = pl.BlockSpec((1, HEAD), lambda head: (0, head))
    work = heads * length * length * HEAD
    return pl.pallas_call(
        functools.partial(attend_kernel, scale, min(256, length), full, len(after)),
        grid=(heads,),
        in_specs=[
            block,
            block,
            block,
            pl.BlockSpec((8, length), lambda head: (0, chunk)),
            gain,
            gain,
            pl.BlockSpec((length, HEAD), lambda head: (chunk, 0)),
            pl.BlockSpec((length, 1), lambda head: (chunk, 0)),
            pl.BlockSpec((1, 1, length), lambda head: (chunk, 0, 0)),
        ]
        + [ANY] * len(after),
        out_specs=[mine] * 3,
        out_shape=[jax.ShapeDtypeStruct((length, q.shape[1]), kind) for kind in (F32, BF, BF)],
        compiler_params=params(58),
        cost_estimate=cost(64 * work, length * heads * HEAD * 22),
        name="attend",
    )(q, k, v, sums, *gains, angles, segments.reshape(-1, 1), segments[:, None, :], *after)


def attend_back_kernel(
    scale,
    block,
    full,
    after,
    place_ref,
    q_ref,
    k_ref,
    v_ref,
    grad_ref,
    qr_ref,
    kr_ref,
    sums_ref,
    gq_ref,
    gk_ref,
    angle_ref,
    col_ref,
    row_ref,
    *refs,
):
    qs_ref, ks_ref, dv_out, totals_ref, gains_ref, g_ref, dq_ref, dk_ref, dv_ref = refs[after:]
    length = q_ref.shape[0]
    parts, part_rows, _ = grad_ref.shape
    for part in range(parts):
        here = slice(part * part_rows, (part + 1) * part_rows)
        g_ref[here, :] = grad_ref[place_ref[part]].astype(BF)
    dk_ref[...] = jnp.zeros_like(dk_ref)
    dv_ref[...] = jnp.zeros_like(dv_ref)
    for index in range(length // block):
        start, stop = key_span(index, block)
        rows = slice(index * block, (index + 1) * block)
        q_rows = q_ref[rows, :]
        g_rows = g_ref[rows, :]
        k_rows = k_ref[start:stop, :]
        scores = masked_scores(
            q_rows, k_rows, col_ref[rows, :], row_ref[0, :, start:stop], index * block, start, scale
        )
        expo = jnp.exp(scores - jnp.max(scores, axis=1, keepdims=True))
        probs = expo / jnp.sum(expo, axis=1, keepdims=True)
        weight_grad = dot(g_rows, v_ref[start:stop, :], 1, 1)
        delta = jnp.sum(probs * weight_grad, axis=1, keepdims=True)
        score_grad = (probs * (weight_grad - delta)).astype(BF)
        dv_ref[start:stop, :] += dot(probs.astype(BF), g_rows, 0, 0)
        dk_ref[start:stop, :] += dot(score_grad, q_rows, 0, 0) * scale
        dq_ref[rows, :] = dot(score_grad, k_rows) * scale
    dv_out[...] = dv_ref[...].astype(BF)
    cosine, sine = both_halves(angle_ref[...])
    sums, gains = [], []
    for grad, raw, which, gain, out in (
        (dq_ref, qr_ref, 0, gq_ref, qs_ref),
        (dk_ref, kr_ref, 1, gk_ref, ks_ref),
    ):
        norm_grad = turn(grad[...], cosine, -sine)
        hat = raw[...] * hat_scale(sums_ref, which, full)
        gains.append(jnp.sum(norm_grad * hat, axis=0, keepdims=True))
        scaled = norm_grad * gain[...].astype(F32)
        out[...] = scaled
        sums.append(along_lanes(jnp.sum(scaled * hat, axis=1, keepdims=True)))
    first = lax.broadcasted_iota(jnp.int32, sums[0].shape, 0) == 0
    total = jnp.where(first, sums[0], sums[1])
    if_first = pl.program_id(1) == 0
    totals_ref[...] = jnp.where(if_first, total, totals_ref[...] + total)
    row = lax.broadcasted_iota(jnp.int32, gains_ref.shape, 0)
    gains_ref[...] = jnp.where(row == 0, gains[0], jnp.where(row == 1, gains[1], 0.0))


def attend_back(
    q, k, v, grad, raws, sums, gains, angles, place, segments, scale, full, after=()
):
    seqs, length = segments.shape
    heads = q.shape[1] // HEAD
    block = pl.BlockSpec((length, HEAD), lambda seq, head, _: (seq, head))
    gain = pl.BlockSpec((1, HEAD), lambda seq, head, _: (0, head))
    line = pl.BlockSpec((8, length), lambda seq, head, _: (0, seq))
    work = seqs * heads * length * length * HEAD
    return pl.pallas_call(
        functools.partial(attend_back_kernel, scale, min(256, length), full, len(after)),
        grid_spec=pltpu.PrefetchScalarGridSpec(
            num_scalar_prefetch=1,
            grid=(seqs, heads),
            in_specs=[
                block,
                block,
                block,
                pl.BlockSpec(
                    (grad.shape[0], grad.shape[1] // seqs, HEAD),
                    lambda seq, head, _: (0, seq, head),
                ),
                block,
                block,
                line,
                gain,
                gain,
                pl.BlockSpec((length, HEAD), lambda seq, head, _: (seq, 0)),
                pl.BlockSpec((length, 1), lambda seq, head, _: (seq, 0)),
                pl.BlockSpec((1, 1, length), lambda seq, head, _: (seq, 0, 0)),
            ]
            + [ANY] * len(after),
            out_specs=[
                block,
                block,
                block,
                line,
                pl.BlockSpec((8, HEAD), lambda seq, head, _: (seq, head)),
            ],
            scratch_shapes=[pltpu.VMEM((length, HEAD), BF)]
            + [pltpu.VMEM((length, HEAD), F32)] * 3,
        ),
        out_shape=[
            jax.ShapeDtypeStruct(q.shape, F32),
            jax.ShapeDtypeStruct(q.shape, F32),
            jax.ShapeDtypeStruct(q.shape, BF),
            jax.ShapeDtypeStruct((8, q.shape[0]), F32),
            jax.ShapeDtypeStruct((8 * seqs, q.shape[1]), F32),
        ],
        compiler_params=params(58),
        cost_estimate=cost(10 * work, q.size * 30),
        name="attend_back",
    )(
        place,
        q,
        k,
        v,
        grad,
        *raws,
        sums,
        *gains,
        angles,
        segments.reshape(-1, 1),
        segments[:, None, :],
        *after,
    )


def raw_grads_kernel(full, qs_ref, ks_ref, qr_ref, kr_ref, sums_ref, totals_ref, dq_ref, dk_ref):
    for which, scaled, raw, out in ((0, qs_ref, qr_ref, dq_ref), (1, ks_ref, kr_ref, dk_ref)):
        scale = hat_scale(sums_ref, which, full)
        total = across_lanes(totals_ref[which : which + 1, :]) / full
        out[...] = (scale * (scaled[...] - raw[...] * scale * total)).astype(BF)


def raw_grads(scaled, raws, sums, totals, full):
    tokens, wide = raws[0].shape
    rows = min(512, tokens)
    block = pl.BlockSpec((rows, HEAD), lambda i, head: (i, head))
    line = pl.BlockSpec((8, rows), lambda i, head: (0, i))
    return pl.pallas_call(
        functools.partial(raw_grads_kernel, full),
        grid=(tokens // rows, wide // HEAD),
        in_specs=[block] * 4 + [line] * 2,
        out_specs=[block] * 2,
        out_shape=[jax.ShapeDtypeStruct((tokens, wide), BF)] * 2,
        compiler_params=params(58),
        cost_estimate=cost(0, 20 * tokens * wide),
        name="raw_grads",
    )(*scaled, *raws, sums, totals)


def expert_terms(gate_act, up_act, low_grad, gate):
    sigmoid = 0.5 * jnp.tanh(0.5 * gate_act) + 0.5
    silu = gate_act * sigmoid
    inner = (silu * up_act).astype(BF).astype(F32)
    inner_grad = low_grad * gate
    gate_grad = inner_grad * up_act * (sigmoid + silu * (1.0 - sigmoid))
    return (
        (inner * gate).astype(BF),
        gate_grad.astype(BF),
        (inner_grad * silu).astype(BF),
        inner * low_grad,
    )


def low_kernel(rows, after, dy_ref, wd_ref, *refs):
    out_ref, down = refs[after:]
    many, _, hid = wd_ref.shape
    for part in range(many):
        down[:, part * hid : (part + 1) * hid] = wd_ref[part]

    def body(index, carry):
        here = pl.ds(pl.multiple_of(index * rows, rows), rows)
        out_ref[here, :] = dot(dy_ref[here, :], down[...])
        return carry

    lax.fori_loop(0, dy_ref.shape[0] // rows, body, 0)


def low_grads(dy, w_down, chunk, tokens, after=(), last=False):
    width = dy.shape[1]
    experts, _, hid = w_down.shape
    many = 2
    return pl.pallas_call(
        functools.partial(low_kernel, min(1024, tokens), len(after)),
        grid=(experts // many,),
        in_specs=[
            pl.BlockSpec(
                (tokens, width), lambda e: (chunk, 0), pipeline_mode=pl.Buffered(buffer_count=1)
            ),
            pl.BlockSpec((many, width, hid), lambda e: (e, 0, 0)),
        ]
        + [ANY] * len(after),
        out_specs=pl.BlockSpec((tokens, many * hid), lambda e: (0, e)),
        out_shape=jax.ShapeDtypeStruct((tokens, experts * hid), F32),
        scratch_shapes=[pltpu.VMEM((width, many * hid), BF)],
        compiler_params=params(58),
        cost_estimate=cost(8 * tokens * width * experts * hid, 8 * tokens * width, last),
        name="low_grads",
    )(dy, w_down, *after)


def expert_kernel(rows, after, mixed_ref, low_ref, gates_ref, wg_ref, wu_ref, *refs):
    gi_ref, gg_ref, ug_ref, dots_ref, both = refs[after:]
    step = pl.program_id(0)
    many, _, hid = wg_ref.shape
    for part in range(many):
        both[:, part * hid : (part + 1) * hid] = wg_ref[part]
        both[:, (many + part) * hid : (many + part + 1) * hid] = wu_ref[part]

    @pl.when(step == 0)
    def _():
        dots_ref[...] = jnp.zeros_like(dots_ref)

    def body(index, carry):
        here = pl.ds(pl.multiple_of(index * rows, rows), rows)
        acts = dot(mixed_ref[here, :], both[...])
        gates = gates_ref[here, :]
        totals = dots_ref[here, :]
        lane = lax.broadcasted_iota(jnp.int32, gates.shape, 1)
        spot = lax.broadcasted_iota(jnp.int32, totals.shape, 1)
        for part in range(many):
            chosen = lane == step * many + part
            gate = jnp.sum(jnp.where(chosen, gates, 0.0), axis=1, keepdims=True)
            span = slice(part * hid, (part + 1) * hid)
            other = slice((many + part) * hid, (many + part + 1) * hid)
            gi, gg, ug, terms = expert_terms(
                acts[:, span], acts[:, other], low_ref[here, span], gate
            )
            gi_ref[here, span] = gi
            gg_ref[here, span] = gg
            ug_ref[here, span] = ug
            mine = spot == step * many + part
            totals = jnp.where(mine, jnp.sum(terms, axis=1, keepdims=True), totals)
        dots_ref[here, :] = totals
        return carry

    lax.fori_loop(0, mixed_ref.shape[0] // rows, body, 0, unroll=True)


def expert_acts(mixed, low, gates, w_gate, w_up, after=(), last=False):
    tokens, width = mixed.shape
    experts, _, hid = w_gate.shape
    many = 2
    weight = pl.BlockSpec((many, width, hid), lambda e: (e, 0, 0))
    wide = pl.BlockSpec((tokens, many * hid), lambda e: (0, e))
    wide_shape = jax.ShapeDtypeStruct((tokens, experts * hid), BF)
    return pl.pallas_call(
        functools.partial(expert_kernel, min(512, tokens), len(after)),
        grid=(experts // many,),
        in_specs=[
            whole_spec(mixed.shape),
            wide,
            whole_spec(gates.shape),
            weight,
            weight,
        ]
        + [ANY] * len(after),
        out_specs=[wide, wide, wide, whole_spec((tokens, LANES))],
        out_shape=[wide_shape, wide_shape, wide_shape, jax.ShapeDtypeStruct((tokens, LANES), F32)],
        scratch_shapes=[pltpu.VMEM((width, 2 * many * hid), BF)],
        compiler_params=params(58),
        cost_estimate=cost(4 * tokens * width * experts * hid, 12 * tokens * width, last),
        name="expert_acts",
    )(mixed, low, gates, w_gate, w_up, *after)


def fill(held, weight):
    experts, _, hid = weight.shape
    for expert in range(experts):
        held[:, expert * hid : (expert + 1) * hid] = weight[expert]


def back_columns_kernel(rows, count, extra, after, table_ref, rank_ref, *refs):
    lefts, weights = refs[:count], refs[count : 2 * count]
    more = refs[2 * count : 2 * count + extra]
    refs = refs[2 * count + extra + after :]
    outs, held = refs[:-count], refs[-count:]
    step = pl.program_id(0)
    for index in range(count):
        fill(held[index], weights[index])
    places = [out.at[part] for out in outs for part in range(out.shape[0])]
    for number, out_ref in enumerate(places):

        @pl.when(step == number)
        def _(out_ref=out_ref):
            def body(index, carry):
                here = pl.ds(pl.multiple_of(index * rows, rows), rows)
                total = dot(lefts[0][here, :], held[0][...], 1, 1)
                for left, right in zip(lefts[1:], held[1:]):
                    total = total + dot(left[here, :], right[...], 1, 1)
                out_ref[here, :] = total
                return carry

            lax.fori_loop(0, out_ref.shape[0] // rows, body, 0)
            for added in more:
                own = added.shape[0]
                out_ref[pl.ds(pl.multiple_of(rank_ref[0] * own, own), own), :] += added[...]


def back_columns(
    lefts, weights, table, groups, after=(), last=False, rank=None, added=(), chunk=0
):
    rank = jnp.zeros((1,), jnp.int32) if rank is None else rank.reshape(1)
    table = table[jnp.array([k for group in groups for k in group], jnp.int32)]
    tokens = lefts[0].shape[0]
    experts, width, hid = weights[0].shape
    count, parts = len(lefts), table.shape[0]
    block = width // parts
    return pl.pallas_call(
        functools.partial(
            back_columns_kernel, min(512, tokens), count, len(added), len(after)
        ),
        grid_spec=pltpu.PrefetchScalarGridSpec(
            num_scalar_prefetch=2,
            grid=(parts,),
            in_specs=[whole_spec(left.shape) for left in lefts]
            + [pl.BlockSpec((experts, block, hid), lambda d, table, _: (0, table[d], 0))] * count
            + [
                pl.BlockSpec((tokens // parts, block), lambda d, table, _: (chunk, table[d]))
                for item in added
            ]
            + [ANY] * len(after),
            out_specs=[whole_spec((len(group), tokens, block)) for group in groups],
            scratch_shapes=[pltpu.VMEM((block, experts * hid), BF)] * count,
        ),
        out_shape=[jax.ShapeDtypeStruct((len(group), tokens, block), F32) for group in groups],
        compiler_params=params(58),
        cost_estimate=cost(
            2 * count * tokens * width * experts * hid, (4 + 4 * count) * tokens * width, last
        ),
        name="back_columns",
    )(table, rank, *lefts, *weights, *added, *after)


def back_rows_kernel(rows, count, after, table_ref, *refs):
    lefts, weights, dots_ref = refs[:count], refs[count : 2 * count], refs[2 * count]
    refs = refs[2 * count + 1 + after :]
    outs, held, turned = refs[:-2], refs[-2], refs[-1]
    outs = [out.at[part] for out in outs for part in range(out.shape[0])]
    part_rows = outs[0].shape[0]
    deep = held.shape[1] // count
    experts, _, hid = weights[0].shape
    last = pl.num_programs(0) - 1

    @pl.when(pl.program_id(0) == 0)
    def _():
        for number in range(len(outs)):
            here = pl.ds(pl.multiple_of(table_ref[number] * part_rows, part_rows), part_rows)
            there = slice(number * part_rows, (number + 1) * part_rows)
            for index in range(count):
                turned[there, index * deep : (index + 1) * deep] = lefts[index][here, :]

    @pl.when(pl.program_id(0) < last)
    def _():
        for index in range(count):
            for expert in range(experts):
                place = index * deep + expert * hid
                held[:, place : place + hid] = weights[index][expert]
        for step in range(len(outs) * part_rows // rows):
            total = dot(turned[step * rows : (step + 1) * rows, :], held[...], 1, 1)
            for part in range(rows // part_rows):
                number = step * (rows // part_rows) + part
                outs[number][...] = total[part * part_rows : (part + 1) * part_rows]

    @pl.when(pl.program_id(0) == last)
    def _():
        for number in range(len(outs)):
            here = pl.ds(pl.multiple_of(table_ref[number] * part_rows, part_rows), part_rows)
            outs[number][:, :LANES] = dots_ref[here, :]


def back_rows(lefts, weights, dots, table, groups, after=()):
    table = table[jnp.array([k for group in groups for k in group], jnp.int32)]
    tokens = lefts[0].shape[0]
    experts, width, hid = weights[0].shape
    count, parts = len(lefts), table.shape[0]
    block = min(256, width)
    part_rows = tokens // parts
    return pl.pallas_call(
        functools.partial(back_rows_kernel, min(512, tokens), count, len(after)),
        grid_spec=pltpu.PrefetchScalarGridSpec(
            num_scalar_prefetch=1,
            grid=(width // block + 1,),
            in_specs=[whole_spec(left.shape) for left in lefts]
            + [
                pl.BlockSpec(
                    (experts, block, hid),
                    lambda d, _: (0, jnp.minimum(d, width // block - 1), 0),
                )
            ]
            * count
            + [whole_spec(dots.shape)]
            + [ANY] * len(after),
            out_specs=[
                pl.BlockSpec((len(group), part_rows, block), lambda d, _: (0, 0, d))
                for group in groups
            ],
            scratch_shapes=[
                pltpu.VMEM((block, count * experts * hid), BF),
                pltpu.VMEM((tokens, count * experts * hid), BF),
            ],
        ),
        out_shape=[
            jax.ShapeDtypeStruct((len(group), part_rows, width + LANES), F32) for group in groups
        ],
        compiler_params=params(58),
        cost_estimate=cost(
            2 * count * tokens * width * experts * hid, (4 + 4 * count) * tokens * width
        ),
        name="back_rows",
    )(table, *lefts, *weights, dots, *after)


def grads_kernel(rows, chunks, after, *refs):
    lefts = refs[:chunks]
    rest = refs[chunks + after :]
    count = (len(rest) - 2 * chunks) // (chunks + 1)
    rights = [rest[c * count : (c + 1) * count] for c in range(chunks)]
    outs = rest[chunks * count : (chunks + 1) * count]
    held, turned = rest[(chunks + 1) * count : -chunks], rest[-chunks:]
    many, width, hid = outs[0].shape

    @pl.when(pl.program_id(0) == 0)
    def _():
        for chunk in range(chunks):
            wide = 256
            for start in range(0, width, wide):
                turned[chunk][start : start + wide, :] = lefts[chunk][:, start : start + wide].T

    for chunk in range(chunks):
        for index, right in enumerate(rights[chunk]):
            held[chunk][:, index * many * hid : (index + 1) * many * hid] = right[...]

    def body(index, carry):
        here = pl.ds(pl.multiple_of(index * rows, rows), rows)
        total = dot(turned[0][here, :], held[0][...])
        for chunk in range(1, chunks):
            total = total + dot(turned[chunk][here, :], held[chunk][...])
        for which, out in enumerate(outs):
            for part in range(many):
                place = (which * many + part) * hid
                out[part, here, :] = total[:, place : place + hid]
        return carry

    lax.fori_loop(0, width // rows, body, 0)


def expert_grads(lefts, rights, experts, after=()):
    chunks, count = len(rights), len(rights[0])
    tokens = rights[0][0].shape[0]
    width = lefts[0].shape[1]
    hid = rights[0][0].shape[1] // experts
    many = 2
    if len(lefts) == chunks:
        left_specs = [whole_spec(left.shape) for left in lefts]
    else:
        left_specs = [
            pl.BlockSpec(
                (tokens, width),
                lambda e, chunk=chunk: (chunk, 0),
                pipeline_mode=pl.Buffered(buffer_count=1),
            )
            for chunk in range(chunks)
        ]
        lefts = list(lefts) * chunks
    return pl.pallas_call(
        functools.partial(grads_kernel, min(512, width), chunks, len(after)),
        grid=(experts // many,),
        in_specs=left_specs
        + [ANY] * len(after)
        + [pl.BlockSpec((tokens, many * hid), lambda e: (0, e))] * (count * chunks),
        out_specs=[pl.BlockSpec((many, width, hid), lambda e: (e, 0, 0))] * count,
        out_shape=[jax.ShapeDtypeStruct((experts, width, hid), F32)] * count,
        scratch_shapes=[pltpu.VMEM((tokens, count * many * hid), BF)] * chunks
        + [pltpu.VMEM((width, tokens), BF)] * chunks,
        compiler_params=params(58),
        cost_estimate=cost(
            2 * count * chunks * tokens * width * experts * hid, 6 * count * experts * hid * width
        ),
        name="expert_grads",
    )(*lefts, *after, *[item for chunk in rights for item in chunk])


def branch_kernel(count, after, *refs):
    pieces = refs[:count]
    w_ref, x_ref, gain_ref, router_ref = refs[count : count + 4]
    mid_ref, mixed_ref, logit_ref, all_ref = refs[count + 4 + after :]
    share = pieces[0].shape[1]
    for index, piece in enumerate(pieces):
        all_ref[:, index * share : (index + 1) * share] = piece[...].astype(BF)
    middle = x_ref[...].astype(F32) + dot(all_ref[...], w_ref[...], 1, 1)
    mid_ref[...] = middle
    mid_hat = middle * norm_scale(middle)
    mixed = (mid_hat * gain_ref[...].astype(F32)).astype(BF)
    mixed_ref[...] = mixed
    logit_ref[...] = dot(mixed, router_ref[...])


def branch(pieces, w_out, hidden, chunk, gain, w_router, after=()):
    tokens, share = pieces[0].shape
    width, full = w_out.shape
    rows = min(256, tokens)
    steps = tokens // rows
    experts = w_router.shape[1]
    return pl.pallas_call(
        functools.partial(branch_kernel, len(pieces), len(after)),
        grid=(steps,),
        in_specs=[pl.BlockSpec((rows, share), lambda i: (i, 0))] * len(pieces)
        + [
            whole_spec(w_out.shape),
            pl.BlockSpec((rows, width), lambda i: (chunk * steps + i, 0)),
            whole_spec((1, width)),
            whole_spec(w_router.shape),
        ]
        + [ANY] * len(after),
        out_specs=[
            pl.BlockSpec((rows, width), lambda i: (i, 0)),
            pl.BlockSpec((rows, width), lambda i: (i, 0)),
            pl.BlockSpec((rows, experts), lambda i: (i, 0)),
            pl.BlockSpec((rows, full), lambda i: (i, 0)),
        ],
        out_shape=[
            jax.ShapeDtypeStruct((tokens, width), F32),
            jax.ShapeDtypeStruct((tokens, width), BF),
            jax.ShapeDtypeStruct((tokens, experts), F32),
            jax.ShapeDtypeStruct((tokens, full), BF),
        ],
        compiler_params=params(58),
        cost_estimate=cost(2 * tokens * width * full, 16 * tokens * width),
        name="branch",
    )(*pieces, w_out, hidden, gain.reshape(1, -1), w_router, *after)


def cast_kernel(table_ref, in_ref, out_ref):
    wide = in_ref.shape[3]
    for index in range(in_ref.shape[1]):
        span = slice(index * wide, (index + 1) * wide)
        out_ref[:, span] = in_ref[0, table_ref[index]].astype(out_ref.dtype)


def cast(parts, table):
    count, blocks, rows, wide = parts.shape
    step = min(256, rows)
    per = rows // step
    return pl.pallas_call(
        cast_kernel,
        grid_spec=pltpu.PrefetchScalarGridSpec(
            num_scalar_prefetch=1,
            grid=(count, per),
            in_specs=[pl.BlockSpec((1, blocks, step, wide), lambda d, i, _: (d, 0, i, 0))],
            out_specs=pl.BlockSpec((step, blocks * wide), lambda d, i, _: (d * per + i, 0)),
        ),
        out_shape=jax.ShapeDtypeStruct((count * rows, blocks * wide), BF),
        compiler_params=params(58),
        cost_estimate=cost(0, 6 * parts.size),
        name="cast",
    )(table, parts)


def send_back_kernel(after, low_ref, w_ref, *outs):
    for number, out_ref in enumerate(outs[after:]):

        @pl.when(pl.program_id(0) == number)
        def _(out_ref=out_ref):
            out_ref[...] = dot(low_ref[...], w_ref[...]).astype(BF).astype(F32)


def send_back(low, w_out, parts, after=()):
    rows, width = low.shape
    full = w_out.shape[1]
    block = full // parts
    return pl.pallas_call(
        functools.partial(send_back_kernel, len(after)),
        grid=(parts,),
        in_specs=[whole_spec(low.shape), pl.BlockSpec((width, block), lambda k: (0, k))]
        + [ANY] * len(after),
        out_specs=[whole_spec((rows, block))] * parts,
        out_shape=[jax.ShapeDtypeStruct((rows, block), F32)] * parts,
        compiler_params=params(58),
        cost_estimate=cost(2 * rows * width * full, 2 * width * full + 8 * rows * full),
        name="send_back",
    )(low, w_out, *after)


def outer_kernel(after, table_ref, columns_ref, left_ref, right_ref, *outs):
    number = pl.program_id(0) * 2 + pl.program_id(1)
    for index, out_ref in enumerate(outs[after:]):

        @pl.when(number == index)
        def _(out_ref=out_ref):
            for part in range(out_ref.shape[0]):
                wide = out_ref.shape[2]
                place = columns_ref[(index % 2) * out_ref.shape[0] + part] * wide
                right = right_ref[:, pl.ds(pl.multiple_of(place, LANES), wide)]
                out_ref[part] = dot(left_ref[...], right)


def outer(left, right, table, columns, after=()):
    width, rows = left.shape
    parts, pieces = table.shape[0], columns.shape[0]
    high, wide = width // parts, right.shape[1] // pieces
    shape = (pieces // 2, high, wide)
    steps = 2
    return pl.pallas_call(
        functools.partial(outer_kernel, len(after)),
        grid_spec=pltpu.PrefetchScalarGridSpec(
            num_scalar_prefetch=2,
            grid=(parts, 2, steps),
            in_specs=[
                pl.BlockSpec(
                    (high // steps, rows), lambda k, m, i, table, columns: (table[k] * steps + i, 0)
                ),
                whole_spec(right.shape),
            ]
            + [ANY] * len(after),
            out_specs=[
                pl.BlockSpec(
                    (pieces // 2, high // steps, wide),
                    lambda k, m, i, *_, index=index: (
                        0,
                        jnp.where(
                            k * 2 + m < index, 0, jnp.where(k * 2 + m > index, steps - 1, i)
                        ),
                        0,
                    ),
                )
                for index in range(2 * parts)
            ],
        ),
        out_shape=[jax.ShapeDtypeStruct(shape, F32)] * (2 * parts),
        compiler_params=params(58),
        cost_estimate=cost(2 * width * rows * right.shape[1], 4 * width * right.shape[1]),
        name="outer",
    )(table, columns, left, right, *after)


def in_grads_kernel(count, after, table_ref, left_ref, *refs):
    rights, refs = refs[:count], refs[count + after :]
    outs, held = refs[:-1], refs[-1]
    wide = rights[0].shape[1]

    @pl.when(pl.program_id(0) == 0)
    def _():
        for index, right in enumerate(rights):
            held[:, index * wide : (index + 1) * wide] = right[...]

    for number, out_ref in enumerate(outs):

        @pl.when(pl.program_id(0) == number)
        def _(out_ref=out_ref):
            out_ref[...] = dot(left_ref[...].T, held[...])


def in_grads_of(left, rights, table, after=()):
    tokens, width = left.shape
    parts, count = table.shape[0], len(rights)
    wide = rights[0].shape[1]
    high = width // parts
    return pl.pallas_call(
        functools.partial(in_grads_kernel, count, len(after)),
        grid_spec=pltpu.PrefetchScalarGridSpec(
            num_scalar_prefetch=1,
            grid=(parts,),
            in_specs=[pl.BlockSpec((tokens, high), lambda k, table: (0, table[k]))]
            + [whole_spec(right.shape) for right in rights]
            + [ANY] * len(after),
            out_specs=[whole_spec((high, count * wide))] * parts,
            scratch_shapes=[pltpu.VMEM((tokens, count * wide), BF)],
        ),
        out_shape=[jax.ShapeDtypeStruct((high, count * wide), F32)] * parts,
        compiler_params=params(58),
        cost_estimate=cost(0, 0, True),
        name="in_grads",
    )(table, left, *rights, *after)


def plain_low(dy, w_down, chunk, tokens, after=(), last=False):
    dy = lax.slice_in_dim(dy, chunk * tokens, (chunk + 1) * tokens, axis=0)
    low = jnp.einsum("td,edh->teh", dy, w_down, preferred_element_type=F32)
    return low.reshape(tokens, -1)


def plain_acts(mixed, low, gates, w_gate, w_up, after=(), last=False):
    acts = jnp.einsum("td,edh->teh", mixed, w_gate, preferred_element_type=F32)
    ups = jnp.einsum("td,edh->teh", mixed, w_up, preferred_element_type=F32)
    gi, gg, ug, terms = expert_terms(acts, ups, low.reshape(acts.shape), gates[:, :, None])
    flat = (mixed.shape[0], -1)
    dots = jnp.pad(jnp.sum(terms, axis=2), ((0, 0), (0, LANES - gates.shape[1])))
    return gi.reshape(flat), gg.reshape(flat), ug.reshape(flat), dots


def plain_back(lefts, weights):
    experts, _, hid = weights[0].shape
    total = 0.0
    for left, weight in zip(lefts, weights):
        total = total + jnp.einsum(
            "teh,edh->td", left.reshape(-1, experts, hid), weight, preferred_element_type=F32
        )
    return total


def plain_columns(
    lefts, weights, table, groups, after=(), last=False, rank=None, added=(), chunk=0
):
    total = plain_back(lefts, weights)
    for item in added:
        own = total.shape[0] // table.shape[0]
        mine = lax.slice_in_dim(item, chunk * own, (chunk + 1) * own, axis=0)
        rows = lax.dynamic_slice_in_dim(total, rank * own, own, 0) + mine
        total = lax.dynamic_update_slice_in_dim(total, rows, rank * own, 0)
    block = total.shape[1] // table.shape[0]
    return [
        jnp.stack([lax.dynamic_slice_in_dim(total, table[k] * block, block, 1) for k in group])
        for group in groups
    ]


def plain_rows(lefts, weights, dots, table, groups, after=()):
    total = jnp.concatenate([plain_back(lefts, weights), dots], axis=1)
    block = total.shape[0] // table.shape[0]
    return [
        jnp.stack([lax.dynamic_slice_in_dim(total, table[k] * block, block, 0) for k in group])
        for group in groups
    ]


def plain_grads(lefts, rights, experts, after=()):
    left = jnp.concatenate(lefts, axis=0)
    return [
        jnp.einsum(
            "td,teh->edh",
            left,
            jnp.concatenate(parts, axis=0).reshape(left.shape[0], experts, -1),
            preferred_element_type=F32,
        )
        for parts in zip(*rights)
    ]


def bits_of(count):
    if count & (count - 1):
        raise ValueError("tensor axis")
    return [1 << bit for bit in range(count.bit_length() - 1)]


def swap(value, axis, step):
    count = lax.axis_size(axis)
    return lax.ppermute(value, axis, [(i, i ^ step) for i in range(count)])


def reduce_blocks(blocks, axis="tensor", start=1):
    blocks = list(blocks)
    live = [k for k in range(len(blocks)) if not k % start]
    for bit in bits_of(len(blocks)):
        if bit < start:
            continue
        for k in sorted((k for k in live if k & bit), reverse=True):
            blocks[k ^ bit] = blocks[k ^ bit] + swap(blocks[k], axis, bit)
        live = [k for k in live if not k & bit]
    return blocks[0]


def stage_kernel(count, parts, skip, *refs):
    terms, out = refs[:count], refs[count + skip]
    total = terms[0][...]
    for term in terms[1:]:
        total = total + term[...]
    out[...] = total


def stage(parts, terms, passes=(), after=()):
    steps = 4
    _, rows, columns = terms[0].shape
    block = pl.BlockSpec((parts, rows // steps, columns), lambda i: (0, i, 0))
    outs = pl.pallas_call(
        functools.partial(stage_kernel, len(terms), parts, len(passes) + len(after)),
        grid=(steps,),
        in_specs=[block] * len(terms) + [ANY] * (len(passes) + len(after)),
        out_specs=[block] + [ANY] * len(passes),
        out_shape=[jax.ShapeDtypeStruct((parts, rows, columns), F32)]
        + [jax.ShapeDtypeStruct(item.shape, item.dtype) for item in passes],
        input_output_aliases={len(terms) + i: 1 + i for i in range(len(passes))},
        compiler_params=params(58),
        cost_estimate=cost(0, 4 * parts * rows * columns * (len(terms) + 1)),
        name="stage",
    )(*terms, *passes, *after)
    return outs[0], outs[1:]


def tie_kernel(*refs):
    pass


def tie(values, after):
    return pl.pallas_call(
        tie_kernel,
        in_specs=[ANY] * (len(values) + len(after)),
        out_specs=[ANY] * len(values),
        out_shape=[jax.ShapeDtypeStruct(value.shape, value.dtype) for value in values],
        input_output_aliases={i: i for i in range(len(values))},
        compiler_params=params(58),
        cost_estimate=cost(0, 0, True),
        name="tie",
    )(*values, *after)


class Chain:
    groups = ((7, 3), (5, 1), (6, 2), (4, 0))

    def __init__(self, parts):
        self.first, self.second, self.six_two, self.four_zero = parts

    def send_first(self):
        self.got_first = swap(self.first, "tensor", 1)

    def send_second(self):
        self.got_second = swap(self.second, "tensor", 1)
        self.got_near = swap(self.six_two, "tensor", 2)

    def send_far(self):
        self.got_far = swap(self.four, "tensor", 4)

    def result(self):
        return self.four_zero[1] + self.got_second[1] + self.got_near[1] + self.got_far[0]


def odd_stage(ending, starting, passes=(), after=(), hold=False):
    if ending is not None:
        after = (*after, ending.got_far)
    passes = (*passes, starting.second)
    starting.six_two, passes = stage(
        2, (starting.six_two, starting.got_first), passes, after
    )
    starting.second = passes[-1]
    if not hold:
        starting.send_second()
    return passes[:-1]


def even_stage(middle, coming, passes=(), after=()):
    if coming is not None:
        passes = (*passes, coming.first)
    middle.four, passes = stage(
        1, (middle.four_zero, middle.got_second, middle.got_near), passes, after
    )
    middle.send_far()
    if coming is not None:
        coming.first = passes[-1]
        coming.send_first()
        passes = passes[:-1]
    return passes


def reduce_first(blocks, axis):
    return [
        item + swap(blocks[k + 1], axis, 1) if not k & 1 else item for k, item in enumerate(blocks)
    ]


def halves_order(count):
    bits = bits_of(count)
    return [
        sum(bit for bit, other in zip(bits, reversed(bits)) if m & other) for m in range(count)
    ]


def reduce_halves(low, high, axis="tensor", start=1):
    for bit in bits_of(2 * start * low.shape[0]):
        if bit < start:
            continue
        total = low + swap(high, axis, bit)
        half = total.shape[0] // 2
        low, high = total[:half], total[half:]
    return total[0]


def gather_blocks(value):
    count = lax.axis_size("tensor")
    have = {0: value}
    for bit in reversed(bits_of(count)):
        for k in sorted(have):
            have[k ^ bit] = swap(have[k], "tensor", bit)
    return [have[k] for k in range(count)]


def exchange_blocks(blocks):
    return [blocks[0]] + [swap(blocks[k], "tensor", k) for k in range(1, len(blocks))]


def small_sum(value, axis):
    for bit in bits_of(lax.axis_size(axis)):
        value = value + swap(value, axis, bit)
    return value


def on_device(
    hidden_in,
    cotangent,
    routes,
    segments,
    gain_in,
    w_query,
    w_key,
    w_value,
    w_out,
    gain_query,
    gain_key,
    gain_mid,
    w_router,
    w_gate,
    w_up,
    w_down,
):
    count = lax.axis_size("tensor")
    rank = lax.axis_index("tensor")
    dp_count = lax.axis_size("dp")
    dp_rank = lax.axis_index("dp")
    tok_rows, width = hidden_in.shape
    local_width = w_query.shape[1]
    heads_here = local_width // HEAD
    full_width = local_width * count
    share = width // count
    experts = w_gate.shape[0]
    seqs, length = segments.shape
    own = length // count
    scale = 1.0 / math.sqrt(HEAD)
    tiled = w_gate.shape[2] % LANES == 0
    acts_of = expert_acts if tiled else plain_acts
    low_of = low_grads if tiled else plain_low
    columns_of = back_columns if tiled else plain_columns
    rows_of = back_rows if tiled else plain_rows
    grads_of = expert_grads if tiled else plain_grads
    table = rank ^ jnp.arange(count, dtype=jnp.int32)
    chunks = range(seqs)

    part = width // dp_count
    w_part = lax.dynamic_slice_in_dim(w_out, dp_rank * part, part, 0).astype(F32)
    if count == 8:
        w_part = lax.all_gather(w_part, "tensor", axis=0, tiled=False)
    staged = count == 8 and seqs == 2

    in_scale = norm_scale(hidden_in.astype(F32))
    normed, query_raw, key_raw, value_low, square_sums = project(
        hidden_in, gain_in, w_query, w_key, w_value
    )
    raws = (query_raw, key_raw)
    square_sums = small_sum(square_sums, "tensor")
    angles = jnp.concatenate(
        rotary_tables(document_positions(segments).reshape(-1), HEAD), axis=1
    )
    gains_here = (gain_query.reshape(1, -1), gain_key.reshape(1, -1))
    expert_ids = jnp.arange(experts, dtype=jnp.int32)
    hits = jnp.any(routes[:, :, None] == expert_ids[None, None, :], axis=1)
    counts = hits.astype(jnp.int32)
    kept_all = hits & (jnp.cumsum(counts, axis=0, dtype=jnp.int32) - counts < CAP)

    query_low, key_low = [], []

    def attend_of(c, after=()):
        attended_c, query_c, key_c = attend(
            query_raw, key_raw, value_low, square_sums, gains_here, angles, segments, c, scale,
            full_width, after,
        )
        query_low.append(query_c)
        key_low.append(key_c)
        return attended_c

    pieces, low = [], []
    if staged:
        first = attend_of(0)
        near = swap(first, "tensor", 2)
        odd = [swap(first, "tensor", 1)]
        second = attend_of(1, (first,))
        near, again = tie((near, first), (odd[0], second))
        far = swap(again, "tensor", 4)
        odd.append(swap(near, "tensor", 1))
        (w_part,) = tie((w_part,), (near,))
        low.append(low_of(cotangent, w_down, 0, length, (near,)))
        low.append(low_of(cotangent, w_down, 1, length, (low[0],), True))
        w_whole = cast(lax.all_gather(w_part, "dp", axis=0, tiled=False), table)
        (far,) = tie((far,), (odd[1], low[1]))
        both = swap(far, "tensor", 2)
        odd.append(swap(far, "tensor", 1))
        both, second = tie((both, second), (odd[2],))
        odd.append(swap(both, "tensor", 1))
        even = [again, near, far, both]
        pieces.append([item for pair in zip(even, odd) for item in pair])
        near = swap(second, "tensor", 2)
        near, again = tie((near, second), (odd[3],))
        far = swap(again, "tensor", 4)
        odd = [swap(again, "tensor", 1), swap(near, "tensor", 1)]
    else:
        for c in chunks:
            pieces.append(gather_blocks(attend_of(c)))
            low.append(low_of(cotangent, w_down, c, length))
    query_low = jnp.concatenate(query_low, axis=0)
    key_low = jnp.concatenate(key_low, axis=0)
    if not staged:
        w_part = jnp.stack(gather_blocks(w_part)) if count != 8 else w_part
        w_table = jnp.arange(count, dtype=jnp.int32) if count != 8 else table
        w_whole = cast(lax.all_gather(w_part, "dp", axis=0, tiled=False), w_table)

    groups = Chain.groups if staged else tuple((k,) for k in range(count))

    def plain_reduce(parts):
        return reduce_blocks([item[0] for item in parts])

    middle, mixed, attended, probs, kept, gates = ([] for _ in range(6))

    def forward(c, after, last=False):
        mid_c, mixed_c, logits_c, attended_c = branch(
            pieces[c], w_whole, hidden_in, c, gain_mid, w_router, after
        )
        middle.append(mid_c)
        mixed.append(mixed_c)
        attended.append(attended_c)
        probs.append(jax.nn.softmax(logits_c, axis=-1))
        kept.append(lax.slice_in_dim(kept_all, c * length, (c + 1) * length, axis=0))
        gates.append(jnp.where(kept[c], probs[c], 0.0))
        return acts_of(mixed_c, low[c], gates[c], w_gate, w_up, (), last)

    def mixed_blocks(c, after=()):
        return rows_of(acts[c][1:3], [w_gate, w_up], acts[c][3], table, groups, after)

    def moe_of(c, after=(), last=False):
        return columns_of([acts[c][0]], [w_down], table, groups, after, last)

    def down_grads(after=()):
        return grads_of([cotangent], [a[:1] for a in acts], experts, after)[0]

    def act_grads(after=()):
        return grads_of(mixed, [a[1:3] for a in acts], experts, after)

    def rows_own(value, start=0):
        return lax.dynamic_slice_in_dim(value, start + rank * own, own, 0)

    def columns_own(value):
        return lax.dynamic_slice_in_dim(value, rank * share, share, 1)

    if staged:
        acts = [forward(0, ())]
        (far,) = tie((far,), (middle[0],))
        both = swap(far, "tensor", 2)
        odd.append(swap(far, "tensor", 1))
        (both,) = tie((both,), (acts[0][0],))
        odd.append(swap(both, "tensor", 1))
        even = [again, near, far, both]
        pieces.append([item for pair in zip(even, odd) for item in pair])
        mix = [Chain(mixed_blocks(0))]
        mix[0].send_first()
        acts.append(forward(1, (mix[0].four_zero,), True))
        odd_stage(None, mix[0], after=(acts[1][0],))
        mix.append(Chain(mixed_blocks(1, (mix[0].six_two,))))
        even_stage(mix[0], mix[1])
        moe = [Chain(moe_of(0, (mix[0].four,)))]
        odd_stage(mix[0], mix[1], after=(moe[0].four_zero,))
    else:
        acts = []
        for c in chunks:
            acts.append(forward(c, ()))
        mixed_share = [plain_reduce(mixed_blocks(c)) for c in chunks]
        moe_share = [plain_reduce(moe_of(c)) for c in chunks]
        grad_down = down_grads()
        grad_gate, grad_up = act_grads()

    def all_own(values):
        return jnp.concatenate([rows_own(value) for value in values], axis=0)

    probs_own, kept_own, mid_own = all_own(probs), all_own(kept), all_own(middle)
    mixed_own, attended_own = all_own(mixed), all_own(attended)
    dy_own = jnp.concatenate([rows_own(cotangent, c * length) for c in chunks], axis=0)

    if staged:
        grad_down = down_grads((mix[1].six_two, probs_own, mid_own, mixed_own, attended_own))
        (grad_down,) = even_stage(mix[1], moe[0], passes=(grad_down,))
        grad_gate, grad_up = act_grads((mix[1].four,))
        grad_gate, grad_up = odd_stage(mix[1], moe[0], passes=(grad_gate, grad_up))
        mixed_share = [item.result() for item in mix]

    mixed_share = jnp.concatenate(mixed_share, axis=0)
    prob_grad = jnp.where(kept_own, mixed_share[:, width : width + experts], 0.0)
    logit_own = (
        probs_own * (prob_grad - jnp.sum(probs_own * prob_grad, axis=-1, keepdims=True))
    ).astype(BF)
    mixed_grad = mixed_share[:, :width] + dot(logit_own, w_router, 1, 1)
    mid_scale = norm_scale(mid_own)
    mid_hat = mid_own * mid_scale
    grad_gain_mid = jnp.sum(mixed_grad * mid_hat, axis=0)
    scaled = mixed_grad * gain_mid.astype(F32)
    mid_grad = dy_own.astype(F32) + mid_scale * (
        scaled - mid_hat * jnp.mean(scaled * mid_hat, axis=1, keepdims=True)
    )
    mid_low = mid_grad.astype(BF)
    if staged:
        moe.append(Chain(moe_of(1, (mid_low,), True)))
        (mid_low,) = even_stage(moe[0], moe[1], passes=(mid_low,))
    blocks = send_back(mid_low, w_whole, count)
    attended_grad = jnp.stack(exchange_blocks(blocks))

    dp_table = dp_rank ^ jnp.arange(dp_count, dtype=jnp.int32)
    order = jnp.array(halves_order(count), jnp.int32)
    out_parts = outer(mid_low.T, attended_own, dp_table, order, (blocks[0],))

    q_scaled, k_scaled, value_grad, totals, gain_parts = attend_back(
        query_low, key_low, value_low, attended_grad, raws, square_sums, gains_here, angles,
        table, segments, scale, full_width, (out_parts[0],),
    )
    if staged:
        (totals,) = odd_stage(moe[0], moe[1], passes=(totals,), hold=True)
    gain_parts = jnp.sum(gain_parts.reshape(seqs, 8, local_width), axis=0)
    totals = small_sum(totals, "tensor")
    query_grad, key_grad = raw_grads((q_scaled, k_scaled), raws, square_sums, totals, full_width)
    in_grads = [query_grad, key_grad, value_grad]
    weights_in = [w[None] for w in (w_query, w_key, w_value)]
    columns_in = back_columns if local_width % LANES == 0 and share % LANES == 0 else plain_columns

    hidden_own = jnp.concatenate([rows_own(hidden_in, c * length) for c in chunks], axis=0)
    hidden_own = hidden_own.astype(F32)
    own_scale = norm_scale(hidden_own)
    own_hat = hidden_own * own_scale
    direct = mid_grad / (own_scale * gain_in.astype(F32))

    def normed_blocks(c):
        part_grads = [grad[c * length : (c + 1) * length] for grad in in_grads]
        return columns_in(
            part_grads, weights_in, table, groups, rank=rank, added=(direct,), chunk=c
        )

    if staged:
        moe[1].second, moe[1].six_two = tie((moe[1].second, moe[1].six_two), (totals,))
        moe[1].send_second()
        norm = [Chain(normed_blocks(c)) for c in chunks]
        even_stage(moe[1], norm[0], after=(norm[1].four_zero,))
        grad_in = in_grads_of(normed, in_grads, dp_table, (moe[1].four,))
        odd_stage(moe[1], norm[0], after=(grad_in[0],))
        even_stage(norm[0], norm[1])
        out_high = reduce_blocks(out_parts[1::2], "dp")
        odd_stage(norm[0], norm[1], after=(out_high,))
        out_low = reduce_blocks(out_parts[::2], "dp")
        grad_in = reduce_blocks(grad_in, "dp")
        (out_high,) = even_stage(norm[1], None, passes=(out_high,), after=(out_low, grad_in))
        grad_w_out = reduce_halves(out_low, out_high)
        normed_share = [item.result() for item in norm]
        moe_share = [item.result() for item in moe]
    else:
        normed_share = [plain_reduce(normed_blocks(c)) for c in chunks]
        out_low = reduce_blocks(out_parts[::2], "dp")
        out_high = reduce_blocks(out_parts[1::2], "dp")
        grad_in = dot(normed, jnp.concatenate(in_grads, axis=1), 0, 0)
        grad_in = reduce_blocks(
            [
                lax.dynamic_slice_in_dim(grad_in, dp_table[k] * part, part, 0)
                for k in range(dp_count)
            ],
            "dp",
        )
        grad_w_out = reduce_halves(out_low, out_high)
    output = jnp.concatenate(
        [(columns_own(middle[c]) + moe_share[c]).astype(BF) for c in chunks], axis=0
    )

    def over_dp(grad):
        return lax.psum_scatter(grad, "dp", scatter_dimension=0, tiled=True)

    grad_w_query, grad_w_key, grad_w_value = (
        grad_in[:, i * local_width : (i + 1) * local_width] for i in range(3)
    )

    normed_share = jnp.concatenate(normed_share, axis=0)
    in_hat_share = columns_own(hidden_in).astype(F32) * in_scale
    gain_share = lax.dynamic_slice_in_dim(gain_in.astype(F32), rank * share, share, 0)
    in_scaled = normed_share * gain_share
    row_sums = jnp.sum(in_scaled * in_hat_share, axis=1).reshape(seqs, length)
    direct_sums = jnp.sum(mid_grad * own_hat, axis=1) / own_scale[:, 0]
    mine = lax.dynamic_slice_in_dim(row_sums, rank * own, own, 1) - direct_sums.reshape(seqs, own)
    row_sums = lax.dynamic_update_slice_in_dim(row_sums, mine, rank * own, 1)
    grad_router = dot(logit_own, mixed_own, 0, 0)
    direct_gain = jnp.sum(direct * own_hat, axis=0)
    wide = jnp.concatenate([grad_router, grad_gain_mid[None], direct_gain[None]], axis=0)
    wide = small_sum(wide, "dp")
    direct_gain = wide[experts + 1]
    wide = lax.dynamic_slice_in_dim(wide[: experts + 1], dp_rank * part, part, 1)
    flat = [row_sums.reshape(-1), wide.reshape(-1), direct_gain]
    flat = small_sum(jnp.concatenate(flat)[None], "tensor")[0]
    row_totals = flat[:tok_rows]
    wide = flat[tok_rows : tok_rows + wide.size].reshape(wide.shape)
    direct_gain = lax.dynamic_slice_in_dim(flat[-width:], rank * share, share, 0)
    grad_input = (
        in_scale * (in_scaled - in_hat_share * (row_totals / width)[:, None])
    ).astype(BF)
    grad_gain_in = jnp.sum(normed_share * in_hat_share, axis=0)
    gains = jnp.concatenate([grad_gain_in, gain_parts[0], gain_parts[1]])
    gains = small_sum(gains[None], "dp")[0]

    return (
        output,
        grad_input,
        grad_w_query,
        grad_w_key,
        grad_w_value,
        grad_w_out,
        gains[:share] - direct_gain,
        gains[share : share + local_width],
        gains[share + local_width :],
        wide[experts],
        wide[:experts].T,
        over_dp(grad_gate),
        over_dp(grad_up),
        over_dp(grad_down),
    )


def solution(mesh):
    in_specs = (
        P("dp", None),
        P("dp", None),
        P("dp", None),
        P("dp", None),
        P(),
        P(None, "tensor"),
        P(None, "tensor"),
        P(None, "tensor"),
        P(None, "tensor"),
        P("tensor"),
        P("tensor"),
        P(),
        P(),
        P(None, None, "tensor"),
        P(None, None, "tensor"),
        P(None, None, "tensor"),
    )
    out_specs = (
        P("dp", "tensor"),
        P("dp", "tensor"),
        P("dp", "tensor"),
        P("dp", "tensor"),
        P("dp", "tensor"),
        P("dp", "tensor"),
        P("tensor"),
        P("tensor"),
        P("tensor"),
        P("dp"),
        P("dp", None),
        P("dp", None, "tensor"),
        P("dp", None, "tensor"),
        P("dp", None, "tensor"),
    )
    return jax.shard_map(
        on_device, mesh=mesh, in_specs=in_specs, out_specs=out_specs, check_vma=False
    )
```

```python
import functools
import math

import jax
import jax.numpy as jnp
from jax import lax
from jax.experimental import pallas as pl
from jax.experimental.pallas import tpu as pltpu
from jax.sharding import PartitionSpec as P

HEAD = 128
CAP = 1280
LONGEST = 512
EPSILON = 1e-05
MASKED = -1e30
LANES = 128
MIB = 1 << 20
BF = jnp.bfloat16
F32 = jnp.float32


ANY = pl.BlockSpec(memory_space=pl.ANY)


def norm_scale(values):
    return lax.rsqrt(jnp.mean(values * values, axis=-1, keepdims=True) + EPSILON)


def document_positions(segments):
    index = jnp.broadcast_to(
        jnp.arange(segments.shape[1], dtype=jnp.int32)[None, :], segments.shape
    )
    previous = jnp.concatenate([segments[:, :1] - 1, segments[:, :-1]], axis=1)
    starts = lax.cummax(jnp.where(segments != previous, index, 0), axis=1)
    return index - starts


def rotary_tables(positions, head):
    half = head // 2
    freq = 10000.0 ** (-2.0 * jnp.arange(half, dtype=F32) / head)
    angle = positions.astype(F32)[:, None] * freq[None, :]
    return (jnp.cos(angle), jnp.sin(angle))


def dot(left, right, left_dim=1, right_dim=0):
    return lax.dot_general(
        left, right, (((left_dim,), (right_dim,)), ((), ())), preferred_element_type=F32
    )


def whole_spec(shape):
    return pl.BlockSpec(
        shape, lambda *_: (0,) * len(shape), pipeline_mode=pl.Buffered(buffer_count=1)
    )


def params(mib):
    return pltpu.CompilerParams(vmem_limit_bytes=mib * MIB)


def cost(flops, moved, last=False):
    if last:
        flops, moved = 1024, 1024
    return pl.CostEstimate(flops=int(flops), bytes_accessed=int(moved), transcendentals=0)


def across_lanes(row):
    return jnp.broadcast_to(row, (LANES, row.shape[1])).T


def along_lanes(column):
    return jnp.broadcast_to(column, (column.shape[0], LANES)).T[:8]


def project_kernel(x_ref, gain_ref, wq_ref, wk_ref, wv_ref, n_ref, q_ref, k_ref, v_ref, sums_ref):
    x = x_ref[...].astype(F32)
    normed = (x * norm_scale(x) * gain_ref[...].astype(F32)).astype(BF)
    n_ref[...] = normed
    query = dot(normed, wq_ref[...])
    key = dot(normed, wk_ref[...])
    q_ref[...] = query
    k_ref[...] = key
    v_ref[...] = dot(normed, wv_ref[...]).astype(BF)
    q_sum = along_lanes(jnp.sum(query * query, axis=1, keepdims=True))
    k_sum = along_lanes(jnp.sum(key * key, axis=1, keepdims=True))
    first = lax.broadcasted_iota(jnp.int32, q_sum.shape, 0) == 0
    sums_ref[...] = jnp.where(first, q_sum, k_sum)


def project(hidden, gain, w_query, w_key, w_value):
    tokens, width = hidden.shape
    wide = w_query.shape[1]
    rows = min(256, tokens)
    out = pl.BlockSpec((rows, wide), lambda i: (i, 0))
    return pl.pallas_call(
        project_kernel,
        grid=(tokens // rows,),
        in_specs=[pl.BlockSpec((rows, width), lambda i: (i, 0)), whole_spec((1, width))]
        + [whole_spec(w_query.shape)] * 3,
        out_specs=[
            pl.BlockSpec((rows, width), lambda i: (i, 0)),
            out,
            out,
            out,
            pl.BlockSpec((8, rows), lambda i: (0, i)),
        ],
        out_shape=[
            jax.ShapeDtypeStruct((tokens, width), BF),
            jax.ShapeDtypeStruct((tokens, wide), F32),
            jax.ShapeDtypeStruct((tokens, wide), F32),
            jax.ShapeDtypeStruct((tokens, wide), BF),
            jax.ShapeDtypeStruct((8, tokens), F32),
        ],
        compiler_params=params(58),
        cost_estimate=cost(6 * tokens * width * wide, 4 * tokens * width),
        name="project",
    )(hidden, gain.reshape(1, -1), w_query, w_key, w_value)


def key_span(block, rows):
    start = max(0, block * rows - LONGEST)
    return start, (block + 1) * rows


def masked_scores(q_rows, k_rows, seg_col, seg_row, row0, key0, scale):
    scores = dot(q_rows, k_rows, 1, 1) * scale
    row = lax.broadcasted_iota(jnp.int32, scores.shape, 0) + row0
    key = lax.broadcasted_iota(jnp.int32, scores.shape, 1) + key0
    return jnp.where((seg_col == seg_row) & (row >= key), scores, MASKED)


def both_halves(angles):
    other = pltpu.roll(angles, HEAD // 2, 1)
    low = lax.broadcasted_iota(jnp.int32, angles.shape, 1) < HEAD // 2
    return jnp.where(low, angles, other), jnp.where(low, -other, angles)


def turn(values, cosine, sine):
    return values * cosine + pltpu.roll(values, HEAD // 2, 1) * sine


def hat_scale(sums_ref, which, full):
    return lax.rsqrt(across_lanes(sums_ref[which : which + 1, :]) / full + EPSILON)


def attend_kernel(
    scale,
    block,
    full,
    after,
    q_ref,
    k_ref,
    v_ref,
    sums_ref,
    gq_ref,
    gk_ref,
    angle_ref,
    col_ref,
    row_ref,
    *refs,
):
    out_ref, ql_ref, kl_ref = refs[after:]
    length = q_ref.shape[0]
    cosine, sine = both_halves(angle_ref[...])
    for raw, which, gain, low in ((q_ref, 0, gq_ref, ql_ref), (k_ref, 1, gk_ref, kl_ref)):
        hat = raw[...] * hat_scale(sums_ref, which, full)
        low[...] = turn(hat * gain[...].astype(F32), cosine, sine).astype(BF)
    for index in range(length // block):
        start, stop = key_span(index, block)
        rows = slice(index * block, (index + 1) * block)
        scores = masked_scores(
            ql_ref[rows, :],
            kl_ref[start:stop, :],
            col_ref[rows, :],
            row_ref[0, :, start:stop],
            index * block,
            start,
            scale,
        )
        expo = jnp.exp(scores - jnp.max(scores, axis=1, keepdims=True))
        weights = (expo / jnp.sum(expo, axis=1, keepdims=True)).astype(BF)
        out_ref[rows, :] = dot(weights, v_ref[start:stop, :]).astype(BF).astype(F32)


def attend(q, k, v, sums, gains, angles, segments, chunk, scale, full, after=()):
    seqs, length = segments.shape
    heads = q.shape[1] // HEAD
    block = pl.BlockSpec((length, HEAD), lambda head: (chunk, head))
    mine = pl.BlockSpec((length, HEAD), lambda head: (0, head))
    gain = pl.BlockSpec((1, HEAD), lambda head: (0, head))
    work = heads * length * length * HEAD
    return pl.pallas_call(
        functools.partial(attend_kernel, scale, min(256, length), full, len(after)),
        grid=(heads,),
        in_specs=[
            block,
            block,
            block,
            pl.BlockSpec((8, length), lambda head: (0, chunk)),
            gain,
            gain,
            pl.BlockSpec((length, HEAD), lambda head: (chunk, 0)),
            pl.BlockSpec((length, 1), lambda head: (chunk, 0)),
            pl.BlockSpec((1, 1, length), lambda head: (chunk, 0, 0)),
        ]
        + [ANY] * len(after),
        out_specs=[mine] * 3,
        out_shape=[jax.ShapeDtypeStruct((length, q.shape[1]), kind) for kind in (F32, BF, BF)],
        compiler_params=params(58),
        cost_estimate=cost(64 * work, length * heads * HEAD * 22),
        name="attend",
    )(q, k, v, sums, *gains, angles, segments.reshape(-1, 1), segments[:, None, :], *after)


def attend_back_kernel(
    scale,
    block,
    full,
    after,
    place_ref,
    q_ref,
    k_ref,
    v_ref,
    grad_ref,
    qr_ref,
    kr_ref,
    sums_ref,
    gq_ref,
    gk_ref,
    angle_ref,
    col_ref,
    row_ref,
    *refs,
):
    qs_ref, ks_ref, dv_out, totals_ref, gains_ref, g_ref, dq_ref, dk_ref, dv_ref = refs[after:]
    length = q_ref.shape[0]
    parts, part_rows, _ = grad_ref.shape
    for part in range(parts):
        here = slice(part * part_rows, (part + 1) * part_rows)
        g_ref[here, :] = grad_ref[place_ref[part]].astype(BF)
    dk_ref[...] = jnp.zeros_like(dk_ref)
    dv_ref[...] = jnp.zeros_like(dv_ref)
    for index in range(length // block):
        start, stop = key_span(index, block)
        rows = slice(index * block, (index + 1) * block)
        q_rows = q_ref[rows, :]
        g_rows = g_ref[rows, :]
        k_rows = k_ref[start:stop, :]
        scores = masked_scores(
            q_rows, k_rows, col_ref[rows, :], row_ref[0, :, start:stop], index * block, start, scale
        )
        expo = jnp.exp(scores - jnp.max(scores, axis=1, keepdims=True))
        probs = expo / jnp.sum(expo, axis=1, keepdims=True)
        weight_grad = dot(g_rows, v_ref[start:stop, :], 1, 1)
        delta = jnp.sum(probs * weight_grad, axis=1, keepdims=True)
        score_grad = (probs * (weight_grad - delta)).astype(BF)
        dv_ref[start:stop, :] += dot(probs.astype(BF), g_rows, 0, 0)
        dk_ref[start:stop, :] += dot(score_grad, q_rows, 0, 0) * scale
        dq_ref[rows, :] = dot(score_grad, k_rows) * scale
    dv_out[...] = dv_ref[...].astype(BF)
    cosine, sine = both_halves(angle_ref[...])
    sums, gains = [], []
    for grad, raw, which, gain, out in (
        (dq_ref, qr_ref, 0, gq_ref, qs_ref),
        (dk_ref, kr_ref, 1, gk_ref, ks_ref),
    ):
        norm_grad = turn(grad[...], cosine, -sine)
        hat = raw[...] * hat_scale(sums_ref, which, full)
        gains.append(jnp.sum(norm_grad * hat, axis=0, keepdims=True))
        scaled = norm_grad * gain[...].astype(F32)
        out[...] = scaled
        sums.append(along_lanes(jnp.sum(scaled * hat, axis=1, keepdims=True)))
    first = lax.broadcasted_iota(jnp.int32, sums[0].shape, 0) == 0
    total = jnp.where(first, sums[0], sums[1])
    if_first = pl.program_id(1) == 0
    totals_ref[...] = jnp.where(if_first, total, totals_ref[...] + total)
    row = lax.broadcasted_iota(jnp.int32, gains_ref.shape, 0)
    gains_ref[...] = jnp.where(row == 0, gains[0], jnp.where(row == 1, gains[1], 0.0))


def attend_back(
    q, k, v, grad, raws, sums, gains, angles, place, segments, scale, full, after=()
):
    seqs, length = segments.shape
    heads = q.shape[1] // HEAD
    block = pl.BlockSpec((length, HEAD), lambda seq, head, _: (seq, head))
    gain = pl.BlockSpec((1, HEAD), lambda seq, head, _: (0, head))
    line = pl.BlockSpec((8, length), lambda seq, head, _: (0, seq))
    work = seqs * heads * length * length * HEAD
    return pl.pallas_call(
        functools.partial(attend_back_kernel, scale, min(256, length), full, len(after)),
        grid_spec=pltpu.PrefetchScalarGridSpec(
            num_scalar_prefetch=1,
            grid=(seqs, heads),
            in_specs=[
                block,
                block,
                block,
                pl.BlockSpec(
                    (grad.shape[0], grad.shape[1] // seqs, HEAD),
                    lambda seq, head, _: (0, seq, head),
                ),
                block,
                block,
                line,
                gain,
                gain,
                pl.BlockSpec((length, HEAD), lambda seq, head, _: (seq, 0)),
                pl.BlockSpec((length, 1), lambda seq, head, _: (seq, 0)),
                pl.BlockSpec((1, 1, length), lambda seq, head, _: (seq, 0, 0)),
            ]
            + [ANY] * len(after),
            out_specs=[
                block,
                block,
                block,
                line,
                pl.BlockSpec((8, HEAD), lambda seq, head, _: (seq, head)),
            ],
            scratch_shapes=[pltpu.VMEM((length, HEAD), BF)]
            + [pltpu.VMEM((length, HEAD), F32)] * 3,
        ),
        out_shape=[
            jax.ShapeDtypeStruct(q.shape, F32),
            jax.ShapeDtypeStruct(q.shape, F32),
            jax.ShapeDtypeStruct(q.shape, BF),
            jax.ShapeDtypeStruct((8, q.shape[0]), F32),
            jax.ShapeDtypeStruct((8 * seqs, q.shape[1]), F32),
        ],
        compiler_params=params(58),
        cost_estimate=cost(10 * work, q.size * 30),
        name="attend_back",
    )(
        place,
        q,
        k,
        v,
        grad,
        *raws,
        sums,
        *gains,
        angles,
        segments.reshape(-1, 1),
        segments[:, None, :],
        *after,
    )


def raw_grads_kernel(full, qs_ref, ks_ref, qr_ref, kr_ref, sums_ref, totals_ref, dq_ref, dk_ref):
    for which, scaled, raw, out in ((0, qs_ref, qr_ref, dq_ref), (1, ks_ref, kr_ref, dk_ref)):
        scale = hat_scale(sums_ref, which, full)
        total = across_lanes(totals_ref[which : which + 1, :]) / full
        out[...] = (scale * (scaled[...] - raw[...] * scale * total)).astype(BF)


def raw_grads(scaled, raws, sums, totals, full):
    tokens, wide = raws[0].shape
    rows = min(512, tokens)
    block = pl.BlockSpec((rows, HEAD), lambda i, head: (i, head))
    line = pl.BlockSpec((8, rows), lambda i, head: (0, i))
    return pl.pallas_call(
        functools.partial(raw_grads_kernel, full),
        grid=(tokens // rows, wide // HEAD),
        in_specs=[block] * 4 + [line] * 2,
        out_specs=[block] * 2,
        out_shape=[jax.ShapeDtypeStruct((tokens, wide), BF)] * 2,
        compiler_params=params(58),
        cost_estimate=cost(0, 20 * tokens * wide),
        name="raw_grads",
    )(*scaled, *raws, sums, totals)


def expert_terms(gate_act, up_act, low_grad, gate):
    sigmoid = 0.5 * jnp.tanh(0.5 * gate_act) + 0.5
    silu = gate_act * sigmoid
    inner = (silu * up_act).astype(BF).astype(F32)
    inner_grad = low_grad * gate
    gate_grad = inner_grad * up_act * (sigmoid + silu * (1.0 - sigmoid))
    return (
        (inner * gate).astype(BF),
        gate_grad.astype(BF),
        (inner_grad * silu).astype(BF),
        inner * low_grad,
    )


def low_kernel(rows, after, dy_ref, wd_ref, *refs):
    out_ref, down = refs[after:]
    many, _, hid = wd_ref.shape
    for part in range(many):
        down[:, part * hid : (part + 1) * hid] = wd_ref[part]

    def body(index, carry):
        here = pl.ds(pl.multiple_of(index * rows, rows), rows)
        out_ref[here, :] = dot(dy_ref[here, :], down[...])
        return carry

    lax.fori_loop(0, dy_ref.shape[0] // rows, body, 0)


def low_grads(dy, w_down, chunk, tokens, after=(), last=False):
    width = dy.shape[1]
    experts, _, hid = w_down.shape
    many = 2
    return pl.pallas_call(
        functools.partial(low_kernel, min(1024, tokens), len(after)),
        grid=(experts // many,),
        in_specs=[
            pl.BlockSpec(
                (tokens, width), lambda e: (chunk, 0), pipeline_mode=pl.Buffered(buffer_count=1)
            ),
            pl.BlockSpec((many, width, hid), lambda e: (e, 0, 0)),
        ]
        + [ANY] * len(after),
        out_specs=pl.BlockSpec((tokens, many * hid), lambda e: (0, e)),
        out_shape=jax.ShapeDtypeStruct((tokens, experts * hid), F32),
        scratch_shapes=[pltpu.VMEM((width, many * hid), BF)],
        compiler_params=params(58),
        cost_estimate=cost(8 * tokens * width * experts * hid, 8 * tokens * width, last),
        name="low_grads",
    )(dy, w_down, *after)


def expert_kernel(rows, after, mixed_ref, low_ref, gates_ref, wg_ref, wu_ref, *refs):
    gi_ref, gg_ref, ug_ref, dots_ref, both = refs[after:]
    step = pl.program_id(0)
    many, _, hid = wg_ref.shape
    for part in range(many):
        both[:, part * hid : (part + 1) * hid] = wg_ref[part]
        both[:, (many + part) * hid : (many + part + 1) * hid] = wu_ref[part]

    @pl.when(step == 0)
    def _():
        dots_ref[...] = jnp.zeros_like(dots_ref)

    def body(index, carry):
        here = pl.ds(pl.multiple_of(index * rows, rows), rows)
        acts = dot(mixed_ref[here, :], both[...])
        gates = gates_ref[here, :]
        totals = dots_ref[here, :]
        lane = lax.broadcasted_iota(jnp.int32, gates.shape, 1)
        spot = lax.broadcasted_iota(jnp.int32, totals.shape, 1)
        for part in range(many):
            chosen = lane == step * many + part
            gate = jnp.sum(jnp.where(chosen, gates, 0.0), axis=1, keepdims=True)
            span = slice(part * hid, (part + 1) * hid)
            other = slice((many + part) * hid, (many + part + 1) * hid)
            gi, gg, ug, terms = expert_terms(
                acts[:, span], acts[:, other], low_ref[here, span], gate
            )
            gi_ref[here, span] = gi
            gg_ref[here, span] = gg
            ug_ref[here, span] = ug
            mine = spot == step * many + part
            totals = jnp.where(mine, jnp.sum(terms, axis=1, keepdims=True), totals)
        dots_ref[here, :] = totals
        return carry

    lax.fori_loop(0, mixed_ref.shape[0] // rows, body, 0, unroll=True)


def expert_acts(mixed, low, gates, w_gate, w_up, after=(), last=False):
    tokens, width = mixed.shape
    experts, _, hid = w_gate.shape
    many = 2
    weight = pl.BlockSpec((many, width, hid), lambda e: (e, 0, 0))
    wide = pl.BlockSpec((tokens, many * hid), lambda e: (0, e))
    wide_shape = jax.ShapeDtypeStruct((tokens, experts * hid), BF)
    return pl.pallas_call(
        functools.partial(expert_kernel, min(512, tokens), len(after)),
        grid=(experts // many,),
        in_specs=[
            whole_spec(mixed.shape),
            wide,
            whole_spec(gates.shape),
            weight,
            weight,
        ]
        + [ANY] * len(after),
        out_specs=[wide, wide, wide, whole_spec((tokens, LANES))],
        out_shape=[wide_shape, wide_shape, wide_shape, jax.ShapeDtypeStruct((tokens, LANES), F32)],
        scratch_shapes=[pltpu.VMEM((width, 2 * many * hid), BF)],
        compiler_params=params(58),
        cost_estimate=cost(4 * tokens * width * experts * hid, 12 * tokens * width, last),
        name="expert_acts",
    )(mixed, low, gates, w_gate, w_up, *after)


def fill(held, weight):
    experts, _, hid = weight.shape
    for expert in range(experts):
        held[:, expert * hid : (expert + 1) * hid] = weight[expert]


def back_columns_kernel(rows, count, extra, after, table_ref, rank_ref, *refs):
    lefts, weights = refs[:count], refs[count : 2 * count]
    more = refs[2 * count : 2 * count + extra]
    refs = refs[2 * count + extra + after :]
    outs, held = refs[:-count], refs[-count:]
    step = pl.program_id(0)
    for index in range(count):
        fill(held[index], weights[index])
    places = [out.at[part] for out in outs for part in range(out.shape[0])]
    for number, out_ref in enumerate(places):

        @pl.when(step == number)
        def _(out_ref=out_ref):
            def body(index, carry):
                here = pl.ds(pl.multiple_of(index * rows, rows), rows)
                total = dot(lefts[0][here, :], held[0][...], 1, 1)
                for left, right in zip(lefts[1:], held[1:]):
                    total = total + dot(left[here, :], right[...], 1, 1)
                out_ref[here, :] = total
                return carry

            lax.fori_loop(0, out_ref.shape[0] // rows, body, 0)
            for added in more:
                own = added.shape[0]
                out_ref[pl.ds(pl.multiple_of(rank_ref[0] * own, own), own), :] += added[...]


def back_columns(
    lefts, weights, table, groups, after=(), last=False, rank=None, added=(), chunk=0
):
    rank = jnp.zeros((1,), jnp.int32) if rank is None else rank.reshape(1)
    table = table[jnp.array([k for group in groups for k in group], jnp.int32)]
    tokens = lefts[0].shape[0]
    experts, width, hid = weights[0].shape
    count, parts = len(lefts), table.shape[0]
    block = width // parts
    return pl.pallas_call(
        functools.partial(
            back_columns_kernel, min(512, tokens), count, len(added), len(after)
        ),
        grid_spec=pltpu.PrefetchScalarGridSpec(
            num_scalar_prefetch=2,
            grid=(parts,),
            in_specs=[whole_spec(left.shape) for left in lefts]
            + [pl.BlockSpec((experts, block, hid), lambda d, table, _: (0, table[d], 0))] * count
            + [
                pl.BlockSpec((tokens // parts, block), lambda d, table, _: (chunk, table[d]))
                for item in added
            ]
            + [ANY] * len(after),
            out_specs=[whole_spec((len(group), tokens, block)) for group in groups],
            scratch_shapes=[pltpu.VMEM((block, experts * hid), BF)] * count,
        ),
        out_shape=[jax.ShapeDtypeStruct((len(group), tokens, block), F32) for group in groups],
        compiler_params=params(58),
        cost_estimate=cost(
            2 * count * tokens * width * experts * hid, (4 + 4 * count) * tokens * width, last
        ),
        name="back_columns",
    )(table, rank, *lefts, *weights, *added, *after)


def back_rows_kernel(rows, count, after, table_ref, *refs):
    lefts, weights, dots_ref = refs[:count], refs[count : 2 * count], refs[2 * count]
    refs = refs[2 * count + 1 + after :]
    outs, held, turned = refs[:-2], refs[-2], refs[-1]
    outs = [out.at[part] for out in outs for part in range(out.shape[0])]
    part_rows = outs[0].shape[0]
    deep = held.shape[1] // count
    experts, _, hid = weights[0].shape
    last = pl.num_programs(0) - 1

    @pl.when(pl.program_id(0) == 0)
    def _():
        for number in range(len(outs)):
            here = pl.ds(pl.multiple_of(table_ref[number] * part_rows, part_rows), part_rows)
            there = slice(number * part_rows, (number + 1) * part_rows)
            for index in range(count):
                turned[there, index * deep : (index + 1) * deep] = lefts[index][here, :]

    @pl.when(pl.program_id(0) < last)
    def _():
        for index in range(count):
            for expert in range(experts):
                place = index * deep + expert * hid
                held[:, place : place + hid] = weights[index][expert]
        for step in range(len(outs) * part_rows // rows):
            total = dot(turned[step * rows : (step + 1) * rows, :], held[...], 1, 1)
            for part in range(rows // part_rows):
                number = step * (rows // part_rows) + part
                outs[number][...] = total[part * part_rows : (part + 1) * part_rows]

    @pl.when(pl.program_id(0) == last)
    def _():
        for number in range(len(outs)):
            here = pl.ds(pl.multiple_of(table_ref[number] * part_rows, part_rows), part_rows)
            outs[number][:, :LANES] = dots_ref[here, :]


def back_rows(lefts, weights, dots, table, groups, after=()):
    table = table[jnp.array([k for group in groups for k in group], jnp.int32)]
    tokens = lefts[0].shape[0]
    experts, width, hid = weights[0].shape
    count, parts = len(lefts), table.shape[0]
    block = min(256, width)
    part_rows = tokens // parts
    return pl.pallas_call(
        functools.partial(back_rows_kernel, min(512, tokens), count, len(after)),
        grid_spec=pltpu.PrefetchScalarGridSpec(
            num_scalar_prefetch=1,
            grid=(width // block + 1,),
            in_specs=[whole_spec(left.shape) for left in lefts]
            + [
                pl.BlockSpec(
                    (experts, block, hid),
                    lambda d, _: (0, jnp.minimum(d, width // block - 1), 0),
                )
            ]
            * count
            + [whole_spec(dots.shape)]
            + [ANY] * len(after),
            out_specs=[
                pl.BlockSpec((len(group), part_rows, block), lambda d, _: (0, 0, d))
                for group in groups
            ],
            scratch_shapes=[
                pltpu.VMEM((block, count * experts * hid), BF),
                pltpu.VMEM((tokens, count * experts * hid), BF),
            ],
        ),
        out_shape=[
            jax.ShapeDtypeStruct((len(group), part_rows, width + LANES), F32) for group in groups
        ],
        compiler_params=params(58),
        cost_estimate=cost(
            2 * count * tokens * width * experts * hid, (4 + 4 * count) * tokens * width
        ),
        name="back_rows",
    )(table, *lefts, *weights, dots, *after)


def grads_kernel(rows, chunks, after, *refs):
    lefts = refs[:chunks]
    rest = refs[chunks + after :]
    count = (len(rest) - 2 * chunks) // (chunks + 1)
    rights = [rest[c * count : (c + 1) * count] for c in range(chunks)]
    outs = rest[chunks * count : (chunks + 1) * count]
    held, turned = rest[(chunks + 1) * count : -chunks], rest[-chunks:]
    many, width, hid = outs[0].shape

    @pl.when(pl.program_id(0) == 0)
    def _():
        for chunk in range(chunks):
            wide = 256
            for start in range(0, width, wide):
                turned[chunk][start : start + wide, :] = lefts[chunk][:, start : start + wide].T

    for chunk in range(chunks):
        for index, right in enumerate(rights[chunk]):
            held[chunk][:, index * many * hid : (index + 1) * many * hid] = right[...]

    def body(index, carry):
        here = pl.ds(pl.multiple_of(index * rows, rows), rows)
        total = dot(turned[0][here, :], held[0][...])
        for chunk in range(1, chunks):
            total = total + dot(turned[chunk][here, :], held[chunk][...])
        for which, out in enumerate(outs):
            for part in range(many):
                place = (which * many + part) * hid
                out[part, here, :] = total[:, place : place + hid]
        return carry

    lax.fori_loop(0, width // rows, body, 0)


def expert_grads(lefts, rights, experts, after=()):
    chunks, count = len(rights), len(rights[0])
    tokens = rights[0][0].shape[0]
    width = lefts[0].shape[1]
    hid = rights[0][0].shape[1] // experts
    many = 2
    if len(lefts) == chunks:
        left_specs = [whole_spec(left.shape) for left in lefts]
    else:
        left_specs = [
            pl.BlockSpec(
                (tokens, width),
                lambda e, chunk=chunk: (chunk, 0),
                pipeline_mode=pl.Buffered(buffer_count=1),
            )
            for chunk in range(chunks)
        ]
        lefts = list(lefts) * chunks
    return pl.pallas_call(
        functools.partial(grads_kernel, min(512, width), chunks, len(after)),
        grid=(experts // many,),
        in_specs=left_specs
        + [ANY] * len(after)
        + [pl.BlockSpec((tokens, many * hid), lambda e: (0, e))] * (count * chunks),
        out_specs=[pl.BlockSpec((many, width, hid), lambda e: (e, 0, 0))] * count,
        out_shape=[jax.ShapeDtypeStruct((experts, width, hid), F32)] * count,
        scratch_shapes=[pltpu.VMEM((tokens, count * many * hid), BF)] * chunks
        + [pltpu.VMEM((width, tokens), BF)] * chunks,
        compiler_params=params(58),
        cost_estimate=cost(
            2 * count * chunks * tokens * width * experts * hid, 6 * count * experts * hid * width
        ),
        name="expert_grads",
    )(*lefts, *after, *[item for chunk in rights for item in chunk])


def branch_kernel(count, after, *refs):
    pieces = refs[:count]
    w_ref, x_ref, gain_ref, router_ref, kept_ref = refs[count : count + 5]
    mid_ref, mixed_ref, probs_ref, gates_ref, all_ref = refs[count + 5 + after :]
    share = pieces[0].shape[1]
    for index, piece in enumerate(pieces):
        all_ref[:, index * share : (index + 1) * share] = piece[...].astype(BF)
    middle = x_ref[...].astype(F32) + dot(all_ref[...], w_ref[...], 1, 1)
    mid_ref[...] = middle
    mid_hat = middle * norm_scale(middle)
    mixed = (mid_hat * gain_ref[...].astype(F32)).astype(BF)
    mixed_ref[...] = mixed
    logits = dot(mixed, router_ref[...])
    expo = jnp.exp(logits - jnp.max(logits, axis=1, keepdims=True))
    probs = expo / jnp.sum(expo, axis=1, keepdims=True)
    probs_ref[...] = probs
    gates_ref[...] = probs * kept_ref[...]


def branch(pieces, w_out, hidden, chunk, gain, w_router, kept, after=()):
    tokens, share = pieces[0].shape
    width, full = w_out.shape
    rows = min(256, tokens)
    steps = tokens // rows
    experts = w_router.shape[1]
    return pl.pallas_call(
        functools.partial(branch_kernel, len(pieces), len(after)),
        grid=(steps,),
        in_specs=[pl.BlockSpec((rows, share), lambda i: (i, 0))] * len(pieces)
        + [
            whole_spec(w_out.shape),
            pl.BlockSpec((rows, width), lambda i: (chunk * steps + i, 0)),
            whole_spec((1, width)),
            whole_spec(w_router.shape),
            pl.BlockSpec((rows, experts), lambda i: (chunk * steps + i, 0)),
        ]
        + [ANY] * len(after),
        out_specs=[
            pl.BlockSpec((rows, width), lambda i: (i, 0)),
            pl.BlockSpec((rows, width), lambda i: (i, 0)),
            pl.BlockSpec((rows, experts), lambda i: (i, 0)),
            pl.BlockSpec((rows, experts), lambda i: (i, 0)),
            pl.BlockSpec((rows, full), lambda i: (i, 0)),
        ],
        out_shape=[
            jax.ShapeDtypeStruct((tokens, width), F32),
            jax.ShapeDtypeStruct((tokens, width), BF),
            jax.ShapeDtypeStruct((tokens, experts), F32),
            jax.ShapeDtypeStruct((tokens, experts), F32),
            jax.ShapeDtypeStruct((tokens, full), BF),
        ],
        compiler_params=params(58),
        cost_estimate=cost(2 * tokens * width * full, 16 * tokens * width),
        name="branch",
    )(*pieces, w_out, hidden, gain.reshape(1, -1), w_router, kept, *after)


def cast_kernel(table_ref, in_ref, out_ref):
    wide = in_ref.shape[3]
    for index in range(in_ref.shape[1]):
        span = slice(index * wide, (index + 1) * wide)
        out_ref[:, span] = in_ref[0, table_ref[index]].astype(out_ref.dtype)


def cast(parts, table):
    count, blocks, rows, wide = parts.shape
    step = min(256, rows)
    per = rows // step
    return pl.pallas_call(
        cast_kernel,
        grid_spec=pltpu.PrefetchScalarGridSpec(
            num_scalar_prefetch=1,
            grid=(count, per),
            in_specs=[pl.BlockSpec((1, blocks, step, wide), lambda d, i, _: (d, 0, i, 0))],
            out_specs=pl.BlockSpec((step, blocks * wide), lambda d, i, _: (d * per + i, 0)),
        ),
        out_shape=jax.ShapeDtypeStruct((count * rows, blocks * wide), BF),
        compiler_params=params(58),
        cost_estimate=cost(0, 6 * parts.size),
        name="cast",
    )(table, parts)


def send_back_kernel(after, low_ref, w_ref, *outs):
    for number, out_ref in enumerate(outs[after:]):

        @pl.when(pl.program_id(0) == number)
        def _(out_ref=out_ref):
            out_ref[...] = dot(low_ref[...], w_ref[...]).astype(BF).astype(F32)


def send_back(low, w_out, parts, after=()):
    rows, width = low.shape
    full = w_out.shape[1]
    block = full // parts
    return pl.pallas_call(
        functools.partial(send_back_kernel, len(after)),
        grid=(parts,),
        in_specs=[whole_spec(low.shape), pl.BlockSpec((width, block), lambda k: (0, k))]
        + [ANY] * len(after),
        out_specs=[whole_spec((rows, block))] * parts,
        out_shape=[jax.ShapeDtypeStruct((rows, block), F32)] * parts,
        compiler_params=params(58),
        cost_estimate=cost(2 * rows * width * full, 2 * width * full + 8 * rows * full),
        name="send_back",
    )(low, w_out, *after)


def mid_back_kernel(counts, rank_ref, *refs):
    chunks = len(counts)
    terms, refs = refs[: sum(counts)], refs[sum(counts) :]
    by_chunk = [refs[c * 6 : (c + 1) * 6] for c in range(chunks)]
    gain_ref, in_ref, router_ref = refs[6 * chunks : 6 * chunks + 3]
    low_ref, direct_ref, sums_ref, vectors_ref = refs[6 * chunks + 3 :]
    experts = router_ref.shape[1]
    own, width = by_chunk[0][0].shape
    gain, gain_in = gain_ref[...].astype(F32), in_ref[...].astype(F32)
    gain_mid, direct_gain, router = 0.0, 0.0, 0.0
    used = 0
    for chunk in range(chunks):
        mid_ref, dy_ref, x_ref, probs_ref, kept_ref, mixed_ref = by_chunk[chunk]
        total = terms[used][0]
        for term in terms[used + 1 : used + counts[chunk]]:
            total = total + term[0]
        used += counts[chunk]
        probs = probs_ref[...]
        prob_grad = total[:, width : width + experts] * kept_ref[...]
        logit_grad = (
            probs * (prob_grad - jnp.sum(probs * prob_grad, axis=1, keepdims=True))
        ).astype(BF)
        mixed_grad = total[:, :width] + dot(logit_grad, router_ref[...], 1, 1)
        middle = mid_ref[...]
        scale = norm_scale(middle)
        hat = middle * scale
        gain_mid = gain_mid + jnp.sum(mixed_grad * hat, axis=0, keepdims=True)
        scaled = mixed_grad * gain
        grad = dy_ref[...].astype(F32) + scale * (
            scaled - hat * jnp.mean(scaled * hat, axis=1, keepdims=True)
        )
        here = slice(chunk * own, (chunk + 1) * own)
        low_ref[here, :] = grad.astype(BF)
        hidden = x_ref[...].astype(F32)
        in_scale = norm_scale(hidden)
        in_hat = hidden * in_scale
        direct = grad / (in_scale * gain_in)
        direct_ref[here, :] = direct
        sums_ref[here, :] = jnp.broadcast_to(
            jnp.sum(grad * in_hat, axis=1, keepdims=True) / in_scale, (own, LANES)
        )
        direct_gain = direct_gain + jnp.sum(direct * in_hat, axis=0, keepdims=True)
        router = router + dot(logit_grad, mixed_ref[...], 0, 0)
    vectors_ref[:experts, :] = router
    row = lax.broadcasted_iota(jnp.int32, (8, width), 0)
    vectors_ref[experts:, :] = jnp.where(
        row == 0, gain_mid, jnp.where(row == 1, direct_gain, 0.0)
    )


def mid_back(rank, shares, middle, dy, hidden, probs, kept, mixed, gain, gain_in, w_router):
    chunks = len(shares)
    own, width = shares[0][0][0].shape[1], middle[0].shape[1]
    experts = w_router.shape[1]
    parts = middle[0].shape[0] // own
    specs, arrays = [], []
    for chunk in shares:
        for array, block in chunk:
            specs.append(
                pl.BlockSpec((1,) + array.shape[1:], lambda i, _, block=block: (block, 0, 0))
            )
            arrays.append(array)
    for c in range(chunks):
        mine = pl.BlockSpec((own, width), lambda i, rank: (rank[0], 0))
        far = pl.BlockSpec((own, width), lambda i, rank, c=c: (c * parts + rank[0], 0))
        few = pl.BlockSpec((own, experts), lambda i, rank: (rank[0], 0))
        some = pl.BlockSpec((own, experts), lambda i, rank, c=c: (c * parts + rank[0], 0))
        specs += [mine, far, far, few, some, mine]
        arrays += [middle[c], dy, hidden, probs[c], kept, mixed[c]]
    rows = chunks * own
    return pl.pallas_call(
        functools.partial(mid_back_kernel, tuple(len(chunk) for chunk in shares)),
        grid_spec=pltpu.PrefetchScalarGridSpec(
            num_scalar_prefetch=1,
            grid=(1,),
            in_specs=specs
            + [whole_spec((1, width)), whole_spec((1, width)), whole_spec(w_router.shape)],
            out_specs=[
                whole_spec((rows, width)),
                whole_spec((rows, width)),
                whole_spec((rows, LANES)),
                whole_spec((experts + 8, width)),
            ],
        ),
        out_shape=[
            jax.ShapeDtypeStruct((rows, width), BF),
            jax.ShapeDtypeStruct((rows, width), F32),
            jax.ShapeDtypeStruct((rows, LANES), F32),
            jax.ShapeDtypeStruct((experts + 8, width), F32),
        ],
        compiler_params=params(58),
        cost_estimate=cost(0, 0, True),
        name="mid_back",
    )(rank.reshape(1), *arrays, gain.reshape(1, -1), gain_in.reshape(1, -1), w_router)


def outer_kernel(count, after, table_ref, columns_ref, rank_ref, left_ref, *refs):
    rights, refs = refs[:count], refs[count + after :]
    outs, held = refs[:-1], refs[-1]
    own = rights[0].shape[0]
    number = pl.program_id(0) * 2 + pl.program_id(1)

    @pl.when((number == 0) & (pl.program_id(2) == 0))
    def _():
        for index, right in enumerate(rights):
            held[index * own : (index + 1) * own, :] = right[...]

    left = left_ref[...].T
    for index, out_ref in enumerate(outs):

        @pl.when(number == index)
        def _(out_ref=out_ref):
            for part in range(out_ref.shape[0]):
                wide = out_ref.shape[2]
                place = columns_ref[(index % 2) * out_ref.shape[0] + part] * wide
                right = held[:, pl.ds(pl.multiple_of(place, LANES), wide)]
                out_ref[part] = dot(left, right)


def outer(left, rights, rank, table, columns, after=()):
    rows, width = left.shape
    count = len(rights)
    own, full = rows // count, rights[0].shape[1]
    parts, pieces = table.shape[0], columns.shape[0]
    high, wide = width // parts, full // pieces
    steps = 2 if high % (2 * LANES) == 0 else 1
    return pl.pallas_call(
        functools.partial(outer_kernel, count, len(after)),
        grid_spec=pltpu.PrefetchScalarGridSpec(
            num_scalar_prefetch=3,
            grid=(parts, 2, steps),
            in_specs=[
                pl.BlockSpec(
                    (rows, high // steps), lambda k, m, i, table, *_: (0, table[k] * steps + i)
                ),
            ]
            + [pl.BlockSpec((own, full), lambda k, m, i, t, c, rank: (rank[0], 0))] * count
            + [ANY] * len(after),
            out_specs=[
                pl.BlockSpec(
                    (pieces // 2, high // steps, wide),
                    lambda k, m, i, *_, index=index: (
                        0,
                        jnp.where(
                            k * 2 + m < index, 0, jnp.where(k * 2 + m > index, steps - 1, i)
                        ),
                        0,
                    ),
                )
                for index in range(2 * parts)
            ],
            scratch_shapes=[pltpu.VMEM((rows, full), BF)],
        ),
        out_shape=[jax.ShapeDtypeStruct((pieces // 2, high, wide), F32)] * (2 * parts),
        compiler_params=params(58),
        cost_estimate=cost(2 * width * rows * full, 4 * width * full),
        name="outer",
    )(table, columns, rank.reshape(1), left, *rights, *after)


def in_grads_kernel(count, after, table_ref, left_ref, *refs):
    rights, refs = refs[:count], refs[count + after :]
    outs, held = refs[:-1], refs[-1]
    wide = rights[0].shape[1]

    @pl.when(pl.program_id(0) == 0)
    def _():
        for index, right in enumerate(rights):
            held[:, index * wide : (index + 1) * wide] = right[...]

    for number, out_ref in enumerate(outs):

        @pl.when(pl.program_id(0) == number)
        def _(out_ref=out_ref):
            out_ref[...] = dot(left_ref[...].T, held[...])


def in_grads_of(left, rights, table, after=()):
    tokens, width = left.shape
    parts, count = table.shape[0], len(rights)
    wide = rights[0].shape[1]
    high = width // parts
    return pl.pallas_call(
        functools.partial(in_grads_kernel, count, len(after)),
        grid_spec=pltpu.PrefetchScalarGridSpec(
            num_scalar_prefetch=1,
            grid=(parts,),
            in_specs=[pl.BlockSpec((tokens, high), lambda k, table: (0, table[k]))]
            + [whole_spec(right.shape) for right in rights]
            + [ANY] * len(after),
            out_specs=[whole_spec((high, count * wide))] * parts,
            scratch_shapes=[pltpu.VMEM((tokens, count * wide), BF)],
        ),
        out_shape=[jax.ShapeDtypeStruct((high, count * wide), F32)] * parts,
        compiler_params=params(58),
        cost_estimate=cost(0, 0, True),
        name="in_grads",
    )(table, left, *rights, *after)


def plain_low(dy, w_down, chunk, tokens, after=(), last=False):
    dy = lax.slice_in_dim(dy, chunk * tokens, (chunk + 1) * tokens, axis=0)
    low = jnp.einsum("td,edh->teh", dy, w_down, preferred_element_type=F32)
    return low.reshape(tokens, -1)


def plain_acts(mixed, low, gates, w_gate, w_up, after=(), last=False):
    acts = jnp.einsum("td,edh->teh", mixed, w_gate, preferred_element_type=F32)
    ups = jnp.einsum("td,edh->teh", mixed, w_up, preferred_element_type=F32)
    gi, gg, ug, terms = expert_terms(acts, ups, low.reshape(acts.shape), gates[:, :, None])
    flat = (mixed.shape[0], -1)
    dots = jnp.pad(jnp.sum(terms, axis=2), ((0, 0), (0, LANES - gates.shape[1])))
    return gi.reshape(flat), gg.reshape(flat), ug.reshape(flat), dots


def plain_back(lefts, weights):
    experts, _, hid = weights[0].shape
    total = 0.0
    for left, weight in zip(lefts, weights):
        total = total + jnp.einsum(
            "teh,edh->td", left.reshape(-1, experts, hid), weight, preferred_element_type=F32
        )
    return total


def plain_columns(
    lefts, weights, table, groups, after=(), last=False, rank=None, added=(), chunk=0
):
    total = plain_back(lefts, weights)
    for item in added:
        own = total.shape[0] // table.shape[0]
        mine = lax.slice_in_dim(item, chunk * own, (chunk + 1) * own, axis=0)
        rows = lax.dynamic_slice_in_dim(total, rank * own, own, 0) + mine
        total = lax.dynamic_update_slice_in_dim(total, rows, rank * own, 0)
    block = total.shape[1] // table.shape[0]
    return [
        jnp.stack([lax.dynamic_slice_in_dim(total, table[k] * block, block, 1) for k in group])
        for group in groups
    ]


def plain_rows(lefts, weights, dots, table, groups, after=()):
    total = jnp.concatenate([plain_back(lefts, weights), dots], axis=1)
    block = total.shape[0] // table.shape[0]
    return [
        jnp.stack([lax.dynamic_slice_in_dim(total, table[k] * block, block, 0) for k in group])
        for group in groups
    ]


def plain_grads(lefts, rights, experts, after=()):
    left = jnp.concatenate(lefts, axis=0)
    return [
        jnp.einsum(
            "td,teh->edh",
            left,
            jnp.concatenate(parts, axis=0).reshape(left.shape[0], experts, -1),
            preferred_element_type=F32,
        )
        for parts in zip(*rights)
    ]


def bits_of(count):
    if count & (count - 1):
        raise ValueError("tensor axis")
    return [1 << bit for bit in range(count.bit_length() - 1)]


def swap(value, axis, step):
    count = lax.axis_size(axis)
    return lax.ppermute(value, axis, [(i, i ^ step) for i in range(count)])


def reduce_blocks(blocks, axis="tensor", start=1):
    blocks = list(blocks)
    live = [k for k in range(len(blocks)) if not k % start]
    for bit in bits_of(len(blocks)):
        if bit < start:
            continue
        for k in sorted((k for k in live if k & bit), reverse=True):
            blocks[k ^ bit] = blocks[k ^ bit] + swap(blocks[k], axis, bit)
        live = [k for k in live if not k & bit]
    return blocks[0]


def stage_kernel(count, parts, skip, *refs):
    terms, out = refs[:count], refs[count + skip]
    total = terms[0][...]
    for term in terms[1:]:
        total = total + term[...]
    out[...] = total


def stage(parts, terms, passes=(), after=()):
    steps = 4
    _, rows, columns = terms[0].shape
    block = pl.BlockSpec((parts, rows // steps, columns), lambda i: (0, i, 0))
    outs = pl.pallas_call(
        functools.partial(stage_kernel, len(terms), parts, len(passes) + len(after)),
        grid=(steps,),
        in_specs=[block] * len(terms) + [ANY] * (len(passes) + len(after)),
        out_specs=[block] + [ANY] * len(passes),
        out_shape=[jax.ShapeDtypeStruct((parts, rows, columns), F32)]
        + [jax.ShapeDtypeStruct(item.shape, item.dtype) for item in passes],
        input_output_aliases={len(terms) + i: 1 + i for i in range(len(passes))},
        compiler_params=params(58),
        cost_estimate=cost(0, 4 * parts * rows * columns * (len(terms) + 1)),
        name="stage",
    )(*terms, *passes, *after)
    return outs[0], outs[1:]


def tie_kernel(*refs):
    pass


def tie(values, after):
    return pl.pallas_call(
        tie_kernel,
        in_specs=[ANY] * (len(values) + len(after)),
        out_specs=[ANY] * len(values),
        out_shape=[jax.ShapeDtypeStruct(value.shape, value.dtype) for value in values],
        input_output_aliases={i: i for i in range(len(values))},
        compiler_params=params(58),
        cost_estimate=cost(0, 0, True),
        name="tie",
    )(*values, *after)


class Chain:
    groups = ((7, 3), (5, 1), (6, 2), (4, 0))

    def __init__(self, parts):
        self.first, self.second, self.six_two, self.four_zero = parts

    def send_first(self):
        self.got_first = swap(self.first, "tensor", 1)

    def send_second(self):
        self.got_second = swap(self.second, "tensor", 1)
        self.got_near = swap(self.six_two, "tensor", 2)

    def send_far(self):
        self.got_far = swap(self.four, "tensor", 4)

    def terms(self):
        return [
            (self.four_zero, 1),
            (self.got_second, 1),
            (self.got_near, 1),
            (self.got_far, 0),
        ]

    def result(self):
        return sum(array[block] for array, block in self.terms())


def odd_stage(ending, starting, passes=(), after=(), hold=False):
    if ending is not None:
        after = (*after, ending.got_far)
    passes = (*passes, starting.second)
    starting.six_two, passes = stage(
        2, (starting.six_two, starting.got_first), passes, after
    )
    starting.second = passes[-1]
    if not hold:
        starting.send_second()
    return passes[:-1]


def even_stage(middle, coming, passes=(), after=()):
    if coming is not None:
        passes = (*passes, coming.first)
    middle.four, passes = stage(
        1, (middle.four_zero, middle.got_second, middle.got_near), passes, after
    )
    middle.send_far()
    if coming is not None:
        coming.first = passes[-1]
        coming.send_first()
        passes = passes[:-1]
    return passes


def reduce_first(blocks, axis):
    return [
        item + swap(blocks[k + 1], axis, 1) if not k & 1 else item for k, item in enumerate(blocks)
    ]


def halves_order(count):
    bits = bits_of(count)
    return [
        sum(bit for bit, other in zip(bits, reversed(bits)) if m & other) for m in range(count)
    ]


def reduce_halves(low, high, axis="tensor", start=1):
    for bit in bits_of(2 * start * low.shape[0]):
        if bit < start:
            continue
        total = low + swap(high, axis, bit)
        half = total.shape[0] // 2
        low, high = total[:half], total[half:]
    return total[0]


def gather_blocks(value):
    count = lax.axis_size("tensor")
    have = {0: value}
    for bit in reversed(bits_of(count)):
        for k in sorted(have):
            have[k ^ bit] = swap(have[k], "tensor", bit)
    return [have[k] for k in range(count)]


def exchange_blocks(blocks):
    return [blocks[0]] + [swap(blocks[k], "tensor", k) for k in range(1, len(blocks))]


def small_sum(value, axis):
    for bit in bits_of(lax.axis_size(axis)):
        value = value + swap(value, axis, bit)
    return value


def on_device(
    hidden_in,
    cotangent,
    routes,
    segments,
    gain_in,
    w_query,
    w_key,
    w_value,
    w_out,
    gain_query,
    gain_key,
    gain_mid,
    w_router,
    w_gate,
    w_up,
    w_down,
):
    count = lax.axis_size("tensor")
    rank = lax.axis_index("tensor")
    dp_count = lax.axis_size("dp")
    dp_rank = lax.axis_index("dp")
    tok_rows, width = hidden_in.shape
    local_width = w_query.shape[1]
    heads_here = local_width // HEAD
    full_width = local_width * count
    share = width // count
    experts = w_gate.shape[0]
    seqs, length = segments.shape
    own = length // count
    scale = 1.0 / math.sqrt(HEAD)
    tiled = w_gate.shape[2] % LANES == 0
    acts_of = expert_acts if tiled else plain_acts
    low_of = low_grads if tiled else plain_low
    columns_of = back_columns if tiled else plain_columns
    rows_of = back_rows if tiled else plain_rows
    grads_of = expert_grads if tiled else plain_grads
    table = rank ^ jnp.arange(count, dtype=jnp.int32)
    chunks = range(seqs)

    part = width // dp_count
    w_part = lax.dynamic_slice_in_dim(w_out, dp_rank * part, part, 0).astype(F32)
    if count == 8:
        w_part = lax.all_gather(w_part, "tensor", axis=0, tiled=False)
    staged = count == 8 and seqs == 2

    in_scale = norm_scale(hidden_in.astype(F32))
    normed, query_raw, key_raw, value_low, square_sums = project(
        hidden_in, gain_in, w_query, w_key, w_value
    )
    raws = (query_raw, key_raw)
    square_sums = small_sum(square_sums, "tensor")
    angles = jnp.concatenate(
        rotary_tables(document_positions(segments).reshape(-1), HEAD), axis=1
    )
    gains_here = (gain_query.reshape(1, -1), gain_key.reshape(1, -1))
    expert_ids = jnp.arange(experts, dtype=jnp.int32)
    hits = jnp.any(routes[:, :, None] == expert_ids[None, None, :], axis=1)
    counts = hits.astype(jnp.int32)
    kept_all = hits & (jnp.cumsum(counts, axis=0, dtype=jnp.int32) - counts < CAP)
    kept_all = kept_all.astype(F32)

    query_low, key_low = [], []

    def attend_of(c, after=()):
        attended_c, query_c, key_c = attend(
            query_raw, key_raw, value_low, square_sums, gains_here, angles, segments, c, scale,
            full_width, after,
        )
        query_low.append(query_c)
        key_low.append(key_c)
        return attended_c

    pieces, low = [], []
    if staged:
        first = attend_of(0)
        near = swap(first, "tensor", 2)
        odd = [swap(first, "tensor", 1)]
        second = attend_of(1, (first,))
        near, again = tie((near, first), (odd[0], second))
        far = swap(again, "tensor", 4)
        odd.append(swap(near, "tensor", 1))
        (w_part,) = tie((w_part,), (near,))
        low.append(low_of(cotangent, w_down, 0, length, (near,)))
        low.append(low_of(cotangent, w_down, 1, length, (low[0],), True))
        w_whole = cast(lax.all_gather(w_part, "dp", axis=0, tiled=False), table)
        (far,) = tie((far,), (odd[1], low[1]))
        both = swap(far, "tensor", 2)
        odd.append(swap(far, "tensor", 1))
        both, second = tie((both, second), (odd[2],))
        odd.append(swap(both, "tensor", 1))
        even = [again, near, far, both]
        pieces.append([item for pair in zip(even, odd) for item in pair])
        near = swap(second, "tensor", 2)
        near, again = tie((near, second), (odd[3],))
        far = swap(again, "tensor", 4)
        odd = [swap(again, "tensor", 1), swap(near, "tensor", 1)]
    else:
        for c in chunks:
            pieces.append(gather_blocks(attend_of(c)))
            low.append(low_of(cotangent, w_down, c, length))
    query_low = jnp.concatenate(query_low, axis=0)
    key_low = jnp.concatenate(key_low, axis=0)
    if not staged:
        w_part = jnp.stack(gather_blocks(w_part)) if count != 8 else w_part
        w_table = jnp.arange(count, dtype=jnp.int32) if count != 8 else table
        w_whole = cast(lax.all_gather(w_part, "dp", axis=0, tiled=False), w_table)

    groups = Chain.groups if staged else tuple((k,) for k in range(count))

    def plain_reduce(parts):
        return reduce_blocks([item[0] for item in parts])

    middle, mixed, attended, probs, gates = ([] for _ in range(5))

    def forward(c, after, last=False):
        mid_c, mixed_c, probs_c, gates_c, attended_c = branch(
            pieces[c], w_whole, hidden_in, c, gain_mid, w_router, kept_all, after
        )
        middle.append(mid_c)
        mixed.append(mixed_c)
        attended.append(attended_c)
        probs.append(probs_c)
        gates.append(gates_c)
        return acts_of(mixed_c, low[c], gates[c], w_gate, w_up, (), last)

    def mixed_blocks(c, after=()):
        return rows_of(acts[c][1:3], [w_gate, w_up], acts[c][3], table, groups, after)

    def moe_of(c, after=(), last=False):
        return columns_of([acts[c][0]], [w_down], table, groups, after, last)

    def down_grads(after=()):
        return grads_of([cotangent], [a[:1] for a in acts], experts, after)[0]

    def act_grads(after=()):
        return grads_of(mixed, [a[1:3] for a in acts], experts, after)

    def rows_own(value, start=0):
        return lax.dynamic_slice_in_dim(value, start + rank * own, own, 0)

    def columns_own(value):
        return lax.dynamic_slice_in_dim(value, rank * share, share, 1)

    if staged:
        acts = [forward(0, ())]
        (far,) = tie((far,), (middle[0], odd[0], odd[1]))
        both = swap(far, "tensor", 2)
        odd.append(swap(far, "tensor", 1))
        (both,) = tie((both,), (acts[0][0], odd[2]))
        odd.append(swap(both, "tensor", 1))
        even = [again, near, far, both]
        pieces.append([item for pair in zip(even, odd) for item in pair])
        mix = [Chain(mixed_blocks(0))]
        (mix[0].first,) = tie((mix[0].first,), (odd[3],))
        mix[0].send_first()
        acts.append(forward(1, (mix[0].four_zero,), True))
        odd_stage(None, mix[0], after=(acts[1][0],))
        mix.append(Chain(mixed_blocks(1, (mix[0].six_two,))))
        even_stage(mix[0], mix[1])
        grad_down = down_grads((mix[0].four,))
        (grad_down,) = odd_stage(mix[0], mix[1], passes=(grad_down,))
    else:
        acts = []
        for c in chunks:
            acts.append(forward(c, ()))
        mixed_share = [plain_reduce(mixed_blocks(c)) for c in chunks]
        moe_share = [plain_reduce(moe_of(c)) for c in chunks]
        grad_down = down_grads()
        grad_gate, grad_up = act_grads()

    if staged:
        moe = [Chain(moe_of(0, (mix[1].six_two,)))]
        even_stage(mix[1], moe[0])
        grad_gate, grad_up = act_grads((mix[1].four,))
        grad_gate, grad_up = odd_stage(mix[1], moe[0], passes=(grad_gate, grad_up))
        mixed_terms = [item.terms() for item in mix]
    else:
        mixed_terms = [[(item[None], 0)] for item in mixed_share]

    mid_low, direct, direct_sums, vectors = mid_back(
        rank, mixed_terms, middle, cotangent, hidden_in, probs, kept_all, mixed, gain_mid,
        gain_in, w_router,
    )
    if staged:
        moe.append(Chain(moe_of(1, (mid_low,), True)))
        (mid_low,) = even_stage(moe[0], moe[1], passes=(mid_low,))
    blocks = send_back(mid_low, w_whole, count)
    attended_grad = jnp.stack(exchange_blocks(blocks))

    dp_table = dp_rank ^ jnp.arange(dp_count, dtype=jnp.int32)
    order = jnp.array(halves_order(count), jnp.int32)
    out_parts = outer(mid_low, attended, rank, dp_table, order, (blocks[0],))

    q_scaled, k_scaled, value_grad, totals, gain_parts = attend_back(
        query_low, key_low, value_low, attended_grad, raws, square_sums, gains_here, angles,
        table, segments, scale, full_width, (out_parts[0],),
    )
    if staged:
        odd_stage(moe[0], moe[1], after=(q_scaled,), hold=True)
    gain_parts = jnp.sum(gain_parts.reshape(seqs, 8, local_width), axis=0)
    totals = small_sum(totals, "tensor")
    query_grad, key_grad = raw_grads((q_scaled, k_scaled), raws, square_sums, totals, full_width)
    in_grads = [query_grad, key_grad, value_grad]
    weights_in = [w[None] for w in (w_query, w_key, w_value)]
    columns_in = back_columns if local_width % LANES == 0 and share % LANES == 0 else plain_columns

    def normed_blocks(c):
        part_grads = [grad[c * length : (c + 1) * length] for grad in in_grads]
        return columns_in(
            part_grads, weights_in, table, groups, rank=rank, added=(direct,), chunk=c
        )

    if staged:
        moe[1].second, moe[1].six_two = tie((moe[1].second, moe[1].six_two), (totals,))
        moe[1].send_second()
        norm = [Chain(normed_blocks(c)) for c in chunks]
        even_stage(moe[1], norm[0], after=(norm[1].four_zero,))
        grad_in = in_grads_of(normed, in_grads, dp_table, (moe[1].four,))
        odd_stage(moe[1], norm[0], after=(grad_in[0],))
        even_stage(norm[0], norm[1])
        out_high = reduce_blocks(out_parts[1::2], "dp")
        odd_stage(norm[0], norm[1], after=(out_high,))
        out_low = reduce_blocks(out_parts[::2], "dp")
        grad_in = reduce_blocks(grad_in, "dp")
        (out_high,) = even_stage(norm[1], None, passes=(out_high,), after=(out_low, grad_in))
        grad_w_out = reduce_halves(out_low, out_high)
        normed_share = [item.result() for item in norm]
        moe_share = [item.result() for item in moe]
    else:
        normed_share = [plain_reduce(normed_blocks(c)) for c in chunks]
        out_low = reduce_blocks(out_parts[::2], "dp")
        out_high = reduce_blocks(out_parts[1::2], "dp")
        grad_in = dot(normed, jnp.concatenate(in_grads, axis=1), 0, 0)
        grad_in = reduce_blocks(
            [
                lax.dynamic_slice_in_dim(grad_in, dp_table[k] * part, part, 0)
                for k in range(dp_count)
            ],
            "dp",
        )
        grad_w_out = reduce_halves(out_low, out_high)
    output = jnp.concatenate(
        [(columns_own(middle[c]) + moe_share[c]).astype(BF) for c in chunks], axis=0
    )

    def over_dp(grad):
        return lax.psum_scatter(grad, "dp", scatter_dimension=0, tiled=True)

    grad_w_query, grad_w_key, grad_w_value = (
        grad_in[:, i * local_width : (i + 1) * local_width] for i in range(3)
    )

    normed_share = jnp.concatenate(normed_share, axis=0)
    in_hat_share = columns_own(hidden_in).astype(F32) * in_scale
    gain_share = lax.dynamic_slice_in_dim(gain_in.astype(F32), rank * share, share, 0)
    in_scaled = normed_share * gain_share
    row_sums = jnp.sum(in_scaled * in_hat_share, axis=1).reshape(seqs, length)
    mine = lax.dynamic_slice_in_dim(row_sums, rank * own, own, 1)
    mine = mine - direct_sums[:, 0].reshape(seqs, own)
    row_sums = lax.dynamic_update_slice_in_dim(row_sums, mine, rank * own, 1)
    wide = small_sum(vectors, "dp")
    direct_gain = wide[experts + 1]
    wide = lax.dynamic_slice_in_dim(wide[: experts + 1], dp_rank * part, part, 1)
    flat = [row_sums.reshape(-1), wide.reshape(-1), direct_gain]
    flat = small_sum(jnp.concatenate(flat)[None], "tensor")[0]
    row_totals = flat[:tok_rows]
    wide = flat[tok_rows : tok_rows + wide.size].reshape(wide.shape)
    direct_gain = lax.dynamic_slice_in_dim(flat[-width:], rank * share, share, 0)
    grad_input = (
        in_scale * (in_scaled - in_hat_share * (row_totals / width)[:, None])
    ).astype(BF)
    grad_gain_in = jnp.sum(normed_share * in_hat_share, axis=0)
    gains = jnp.concatenate([grad_gain_in, gain_parts[0], gain_parts[1]])
    gains = small_sum(gains[None], "dp")[0]

    return (
        output,
        grad_input,
        grad_w_query,
        grad_w_key,
        grad_w_value,
        grad_w_out,
        gains[:share] - direct_gain,
        gains[share : share + local_width],
        gains[share + local_width :],
        wide[experts],
        wide[:experts].T,
        over_dp(grad_gate),
        over_dp(grad_up),
        over_dp(grad_down),
    )


def solution(mesh):
    in_specs = (
        P("dp", None),
        P("dp", None),
        P("dp", None),
        P("dp", None),
        P(),
        P(None, "tensor"),
        P(None, "tensor"),
        P(None, "tensor"),
        P(None, "tensor"),
        P("tensor"),
        P("tensor"),
        P(),
        P(),
        P(None, None, "tensor"),
        P(None, None, "tensor"),
        P(None, None, "tensor"),
    )
    out_specs = (
        P("dp", "tensor"),
        P("dp", "tensor"),
        P("dp", "tensor"),
        P("dp", "tensor"),
        P("dp", "tensor"),
        P("dp", "tensor"),
        P("tensor"),
        P("tensor"),
        P("tensor"),
        P("dp"),
        P("dp", None),
        P("dp", None, "tensor"),
        P("dp", None, "tensor"),
        P("dp", None, "tensor"),
    )
    return jax.shard_map(
        on_device, mesh=mesh, in_specs=in_specs, out_specs=out_specs, check_vma=False
    )
```

```python
import functools
import math

import jax
import jax.numpy as jnp
from jax import lax
from jax.experimental import pallas as pl
from jax.experimental.pallas import tpu as pltpu
from jax.sharding import PartitionSpec as P

HEAD = 128
CAP = 1280
LONGEST = 512
EPSILON = 1e-05
MASKED = -1e30
LANES = 128
MIB = 1 << 20
BF = jnp.bfloat16
F32 = jnp.float32


ANY = pl.BlockSpec(memory_space=pl.ANY)


def norm_scale(values):
    return lax.rsqrt(jnp.mean(values * values, axis=-1, keepdims=True) + EPSILON)


def document_positions(segments):
    index = jnp.broadcast_to(
        jnp.arange(segments.shape[1], dtype=jnp.int32)[None, :], segments.shape
    )
    previous = jnp.concatenate([segments[:, :1] - 1, segments[:, :-1]], axis=1)
    starts = lax.cummax(jnp.where(segments != previous, index, 0), axis=1)
    return index - starts


def rotary_tables(positions, head):
    half = head // 2
    freq = 10000.0 ** (-2.0 * jnp.arange(half, dtype=F32) / head)
    angle = positions.astype(F32)[:, None] * freq[None, :]
    return (jnp.cos(angle), jnp.sin(angle))


def dot(left, right, left_dim=1, right_dim=0):
    return lax.dot_general(
        left, right, (((left_dim,), (right_dim,)), ((), ())), preferred_element_type=F32
    )


def whole_spec(shape):
    return pl.BlockSpec(
        shape, lambda *_: (0,) * len(shape), pipeline_mode=pl.Buffered(buffer_count=1)
    )


def params(mib):
    return pltpu.CompilerParams(vmem_limit_bytes=mib * MIB)


def cost(flops, moved, last=False):
    if last:
        flops, moved = 1024, 1024
    return pl.CostEstimate(flops=int(flops), bytes_accessed=int(moved), transcendentals=0)


def across_lanes(row):
    return jnp.broadcast_to(row, (LANES, row.shape[1])).T


def along_lanes(column):
    return jnp.broadcast_to(column, (column.shape[0], LANES)).T[:8]


def project_kernel(x_ref, gain_ref, wq_ref, wk_ref, wv_ref, n_ref, q_ref, k_ref, v_ref, sums_ref):
    x = x_ref[...].astype(F32)
    normed = (x * norm_scale(x) * gain_ref[...].astype(F32)).astype(BF)
    n_ref[...] = normed
    query = dot(normed, wq_ref[...])
    key = dot(normed, wk_ref[...])
    q_ref[...] = query
    k_ref[...] = key
    v_ref[...] = dot(normed, wv_ref[...]).astype(BF)
    q_sum = along_lanes(jnp.sum(query * query, axis=1, keepdims=True))
    k_sum = along_lanes(jnp.sum(key * key, axis=1, keepdims=True))
    first = lax.broadcasted_iota(jnp.int32, q_sum.shape, 0) == 0
    sums_ref[...] = jnp.where(first, q_sum, k_sum)


def project(hidden, gain, w_query, w_key, w_value):
    tokens, width = hidden.shape
    wide = w_query.shape[1]
    rows = min(256, tokens)
    out = pl.BlockSpec((rows, wide), lambda i: (i, 0))
    return pl.pallas_call(
        project_kernel,
        grid=(tokens // rows,),
        in_specs=[pl.BlockSpec((rows, width), lambda i: (i, 0)), whole_spec((1, width))]
        + [whole_spec(w_query.shape)] * 3,
        out_specs=[
            pl.BlockSpec((rows, width), lambda i: (i, 0)),
            out,
            out,
            out,
            pl.BlockSpec((8, rows), lambda i: (0, i)),
        ],
        out_shape=[
            jax.ShapeDtypeStruct((tokens, width), BF),
            jax.ShapeDtypeStruct((tokens, wide), F32),
            jax.ShapeDtypeStruct((tokens, wide), F32),
            jax.ShapeDtypeStruct((tokens, wide), BF),
            jax.ShapeDtypeStruct((8, tokens), F32),
        ],
        compiler_params=params(58),
        cost_estimate=cost(6 * tokens * width * wide, 4 * tokens * width),
        name="project",
    )(hidden, gain.reshape(1, -1), w_query, w_key, w_value)


def key_span(block, rows):
    start = max(0, block * rows - LONGEST)
    return start, (block + 1) * rows


def masked_scores(q_rows, k_rows, seg_col, seg_row, row0, key0, scale):
    scores = dot(q_rows, k_rows, 1, 1) * scale
    row = lax.broadcasted_iota(jnp.int32, scores.shape, 0) + row0
    key = lax.broadcasted_iota(jnp.int32, scores.shape, 1) + key0
    return jnp.where((seg_col == seg_row) & (row >= key), scores, MASKED)


def both_halves(angles):
    other = pltpu.roll(angles, HEAD // 2, 1)
    low = lax.broadcasted_iota(jnp.int32, angles.shape, 1) < HEAD // 2
    return jnp.where(low, angles, other), jnp.where(low, -other, angles)


def turn(values, cosine, sine):
    return values * cosine + pltpu.roll(values, HEAD // 2, 1) * sine


def hat_scale(sums_ref, which, full):
    return lax.rsqrt(across_lanes(sums_ref[which : which + 1, :]) / full + EPSILON)


def attend_kernel(
    scale,
    block,
    full,
    after,
    q_ref,
    k_ref,
    v_ref,
    sums_ref,
    gq_ref,
    gk_ref,
    angle_ref,
    col_ref,
    row_ref,
    *refs,
):
    out_ref, ql_ref, kl_ref = refs[after:]
    length = q_ref.shape[0]
    cosine, sine = both_halves(angle_ref[...])
    for raw, which, gain, low in ((q_ref, 0, gq_ref, ql_ref), (k_ref, 1, gk_ref, kl_ref)):
        hat = raw[...] * hat_scale(sums_ref, which, full)
        low[...] = turn(hat * gain[...].astype(F32), cosine, sine).astype(BF)
    for index in range(length // block):
        start, stop = key_span(index, block)
        rows = slice(index * block, (index + 1) * block)
        scores = masked_scores(
            ql_ref[rows, :],
            kl_ref[start:stop, :],
            col_ref[rows, :],
            row_ref[0, :, start:stop],
            index * block,
            start,
            scale,
        )
        expo = jnp.exp(scores - jnp.max(scores, axis=1, keepdims=True))
        weights = (expo / jnp.sum(expo, axis=1, keepdims=True)).astype(BF)
        out_ref[rows, :] = dot(weights, v_ref[start:stop, :]).astype(BF).astype(F32)


def attend(q, k, v, sums, gains, angles, segments, chunk, scale, full, after=()):
    seqs, length = segments.shape
    heads = q.shape[1] // HEAD
    block = pl.BlockSpec((length, HEAD), lambda head: (chunk, head))
    mine = pl.BlockSpec((length, HEAD), lambda head: (0, head))
    gain = pl.BlockSpec((1, HEAD), lambda head: (0, head))
    work = heads * length * length * HEAD
    return pl.pallas_call(
        functools.partial(attend_kernel, scale, min(256, length), full, len(after)),
        grid=(heads,),
        in_specs=[
            block,
            block,
            block,
            pl.BlockSpec((8, length), lambda head: (0, chunk)),
            gain,
            gain,
            pl.BlockSpec((length, HEAD), lambda head: (chunk, 0)),
            pl.BlockSpec((length, 1), lambda head: (chunk, 0)),
            pl.BlockSpec((1, 1, length), lambda head: (chunk, 0, 0)),
        ]
        + [ANY] * len(after),
        out_specs=[mine] * 3,
        out_shape=[jax.ShapeDtypeStruct((length, q.shape[1]), kind) for kind in (F32, BF, BF)],
        compiler_params=params(58),
        cost_estimate=cost(64 * work, length * heads * HEAD * 22),
        name="attend",
    )(q, k, v, sums, *gains, angles, segments.reshape(-1, 1), segments[:, None, :], *after)


def attend_back_kernel(
    scale,
    block,
    full,
    after,
    place_ref,
    q_ref,
    k_ref,
    v_ref,
    grad_ref,
    qr_ref,
    kr_ref,
    sums_ref,
    gq_ref,
    gk_ref,
    angle_ref,
    col_ref,
    row_ref,
    *refs,
):
    qs_ref, ks_ref, dv_out, totals_ref, gains_ref, g_ref, dq_ref, dk_ref, dv_ref = refs[after:]
    length = q_ref.shape[0]
    parts, part_rows, _ = grad_ref.shape
    for part in range(parts):
        here = slice(part * part_rows, (part + 1) * part_rows)
        g_ref[here, :] = grad_ref[place_ref[part]].astype(BF)
    dk_ref[...] = jnp.zeros_like(dk_ref)
    dv_ref[...] = jnp.zeros_like(dv_ref)
    for index in range(length // block):
        start, stop = key_span(index, block)
        rows = slice(index * block, (index + 1) * block)
        q_rows = q_ref[rows, :]
        g_rows = g_ref[rows, :]
        k_rows = k_ref[start:stop, :]
        scores = masked_scores(
            q_rows, k_rows, col_ref[rows, :], row_ref[0, :, start:stop], index * block, start, scale
        )
        expo = jnp.exp(scores - jnp.max(scores, axis=1, keepdims=True))
        probs = expo / jnp.sum(expo, axis=1, keepdims=True)
        weight_grad = dot(g_rows, v_ref[start:stop, :], 1, 1)
        delta = jnp.sum(probs * weight_grad, axis=1, keepdims=True)
        score_grad = (probs * (weight_grad - delta)).astype(BF)
        dv_ref[start:stop, :] += dot(probs.astype(BF), g_rows, 0, 0)
        dk_ref[start:stop, :] += dot(score_grad, q_rows, 0, 0) * scale
        dq_ref[rows, :] = dot(score_grad, k_rows) * scale
    dv_out[...] = dv_ref[...].astype(BF)
    cosine, sine = both_halves(angle_ref[...])
    sums, gains = [], []
    for grad, raw, which, gain, out in (
        (dq_ref, qr_ref, 0, gq_ref, qs_ref),
        (dk_ref, kr_ref, 1, gk_ref, ks_ref),
    ):
        norm_grad = turn(grad[...], cosine, -sine)
        hat = raw[...] * hat_scale(sums_ref, which, full)
        gains.append(jnp.sum(norm_grad * hat, axis=0, keepdims=True))
        scaled = norm_grad * gain[...].astype(F32)
        out[...] = scaled
        sums.append(along_lanes(jnp.sum(scaled * hat, axis=1, keepdims=True)))
    first = lax.broadcasted_iota(jnp.int32, sums[0].shape, 0) == 0
    total = jnp.where(first, sums[0], sums[1])
    if_first = pl.program_id(1) == 0
    totals_ref[...] = jnp.where(if_first, total, totals_ref[...] + total)
    row = lax.broadcasted_iota(jnp.int32, gains_ref.shape, 0)
    gains_ref[...] = jnp.where(row == 0, gains[0], jnp.where(row == 1, gains[1], 0.0))


def attend_back(
    q, k, v, grad, raws, sums, gains, angles, place, segments, scale, full, after=()
):
    seqs, length = segments.shape
    heads = q.shape[1] // HEAD
    block = pl.BlockSpec((length, HEAD), lambda seq, head, _: (seq, head))
    gain = pl.BlockSpec((1, HEAD), lambda seq, head, _: (0, head))
    line = pl.BlockSpec((8, length), lambda seq, head, _: (0, seq))
    work = seqs * heads * length * length * HEAD
    return pl.pallas_call(
        functools.partial(attend_back_kernel, scale, min(256, length), full, len(after)),
        grid_spec=pltpu.PrefetchScalarGridSpec(
            num_scalar_prefetch=1,
            grid=(seqs, heads),
            in_specs=[
                block,
                block,
                block,
                pl.BlockSpec(
                    (grad.shape[0], grad.shape[1] // seqs, HEAD),
                    lambda seq, head, _: (0, seq, head),
                ),
                block,
                block,
                line,
                gain,
                gain,
                pl.BlockSpec((length, HEAD), lambda seq, head, _: (seq, 0)),
                pl.BlockSpec((length, 1), lambda seq, head, _: (seq, 0)),
                pl.BlockSpec((1, 1, length), lambda seq, head, _: (seq, 0, 0)),
            ]
            + [ANY] * len(after),
            out_specs=[
                block,
                block,
                block,
                line,
                pl.BlockSpec((8, HEAD), lambda seq, head, _: (seq, head)),
            ],
            scratch_shapes=[pltpu.VMEM((length, HEAD), BF)]
            + [pltpu.VMEM((length, HEAD), F32)] * 3,
        ),
        out_shape=[
            jax.ShapeDtypeStruct(q.shape, F32),
            jax.ShapeDtypeStruct(q.shape, F32),
            jax.ShapeDtypeStruct(q.shape, BF),
            jax.ShapeDtypeStruct((8, q.shape[0]), F32),
            jax.ShapeDtypeStruct((8 * seqs, q.shape[1]), F32),
        ],
        compiler_params=params(58),
        cost_estimate=cost(10 * work, q.size * 30),
        name="attend_back",
    )(
        place,
        q,
        k,
        v,
        grad,
        *raws,
        sums,
        *gains,
        angles,
        segments.reshape(-1, 1),
        segments[:, None, :],
        *after,
    )


def raw_grads_kernel(full, qs_ref, ks_ref, qr_ref, kr_ref, sums_ref, totals_ref, dq_ref, dk_ref):
    for which, scaled, raw, out in ((0, qs_ref, qr_ref, dq_ref), (1, ks_ref, kr_ref, dk_ref)):
        scale = hat_scale(sums_ref, which, full)
        total = across_lanes(totals_ref[which : which + 1, :]) / full
        out[...] = (scale * (scaled[...] - raw[...] * scale * total)).astype(BF)


def raw_grads(scaled, raws, sums, totals, full):
    tokens, wide = raws[0].shape
    rows = min(512, tokens)
    block = pl.BlockSpec((rows, HEAD), lambda i, head: (i, head))
    line = pl.BlockSpec((8, rows), lambda i, head: (0, i))
    return pl.pallas_call(
        functools.partial(raw_grads_kernel, full),
        grid=(tokens // rows, wide // HEAD),
        in_specs=[block] * 4 + [line] * 2,
        out_specs=[block] * 2,
        out_shape=[jax.ShapeDtypeStruct((tokens, wide), BF)] * 2,
        compiler_params=params(58),
        cost_estimate=cost(0, 20 * tokens * wide),
        name="raw_grads",
    )(*scaled, *raws, sums, totals)


def expert_terms(gate_act, up_act, low_grad, gate):
    sigmoid = 0.5 * jnp.tanh(0.5 * gate_act) + 0.5
    silu = gate_act * sigmoid
    inner = (silu * up_act).astype(BF).astype(F32)
    inner_grad = low_grad * gate
    gate_grad = inner_grad * up_act * (sigmoid + silu * (1.0 - sigmoid))
    return (
        (inner * gate).astype(BF),
        gate_grad.astype(BF),
        (inner_grad * silu).astype(BF),
        inner * low_grad,
    )


def low_kernel(rows, after, dy_ref, wd_ref, *refs):
    out_ref, down = refs[after:]
    many, _, hid = wd_ref.shape
    for part in range(many):
        down[:, part * hid : (part + 1) * hid] = wd_ref[part]

    def body(index, carry):
        here = pl.ds(pl.multiple_of(index * rows, rows), rows)
        out_ref[here, :] = dot(dy_ref[here, :], down[...])
        return carry

    lax.fori_loop(0, dy_ref.shape[0] // rows, body, 0)


def low_grads(dy, w_down, chunk, tokens, after=(), last=False):
    width = dy.shape[1]
    experts, _, hid = w_down.shape
    many = 2
    return pl.pallas_call(
        functools.partial(low_kernel, min(1024, tokens), len(after)),
        grid=(experts // many,),
        in_specs=[
            pl.BlockSpec(
                (tokens, width), lambda e: (chunk, 0), pipeline_mode=pl.Buffered(buffer_count=1)
            ),
            pl.BlockSpec((many, width, hid), lambda e: (e, 0, 0)),
        ]
        + [ANY] * len(after),
        out_specs=pl.BlockSpec((tokens, many * hid), lambda e: (0, e)),
        out_shape=jax.ShapeDtypeStruct((tokens, experts * hid), F32),
        scratch_shapes=[pltpu.VMEM((width, many * hid), BF)],
        compiler_params=params(58),
        cost_estimate=cost(8 * tokens * width * experts * hid, 8 * tokens * width, last),
        name="low_grads",
    )(dy, w_down, *after)


def expert_kernel(rows, after, mixed_ref, low_ref, gates_ref, wg_ref, wu_ref, *refs):
    gi_ref, gg_ref, ug_ref, dots_ref, both = refs[after:]
    step = pl.program_id(0)
    many, _, hid = wg_ref.shape
    for part in range(many):
        both[:, part * hid : (part + 1) * hid] = wg_ref[part]
        both[:, (many + part) * hid : (many + part + 1) * hid] = wu_ref[part]

    @pl.when(step == 0)
    def _():
        dots_ref[...] = jnp.zeros_like(dots_ref)

    def body(index, carry):
        here = pl.ds(pl.multiple_of(index * rows, rows), rows)
        acts = dot(mixed_ref[here, :], both[...])
        gates = gates_ref[here, :]
        totals = dots_ref[here, :]
        lane = lax.broadcasted_iota(jnp.int32, gates.shape, 1)
        spot = lax.broadcasted_iota(jnp.int32, totals.shape, 1)
        for part in range(many):
            chosen = lane == step * many + part
            gate = jnp.sum(jnp.where(chosen, gates, 0.0), axis=1, keepdims=True)
            span = slice(part * hid, (part + 1) * hid)
            other = slice((many + part) * hid, (many + part + 1) * hid)
            gi, gg, ug, terms = expert_terms(
                acts[:, span], acts[:, other], low_ref[here, span], gate
            )
            gi_ref[here, span] = gi
            gg_ref[here, span] = gg
            ug_ref[here, span] = ug
            mine = spot == step * many + part
            totals = jnp.where(mine, jnp.sum(terms, axis=1, keepdims=True), totals)
        dots_ref[here, :] = totals
        return carry

    lax.fori_loop(0, mixed_ref.shape[0] // rows, body, 0, unroll=True)


def expert_acts(mixed, low, gates, w_gate, w_up, after=(), last=False):
    tokens, width = mixed.shape
    experts, _, hid = w_gate.shape
    many = 2
    weight = pl.BlockSpec((many, width, hid), lambda e: (e, 0, 0))
    wide = pl.BlockSpec((tokens, many * hid), lambda e: (0, e))
    wide_shape = jax.ShapeDtypeStruct((tokens, experts * hid), BF)
    return pl.pallas_call(
        functools.partial(expert_kernel, min(512, tokens), len(after)),
        grid=(experts // many,),
        in_specs=[
            whole_spec(mixed.shape),
            wide,
            whole_spec(gates.shape),
            weight,
            weight,
        ]
        + [ANY] * len(after),
        out_specs=[wide, wide, wide, whole_spec((tokens, LANES))],
        out_shape=[wide_shape, wide_shape, wide_shape, jax.ShapeDtypeStruct((tokens, LANES), F32)],
        scratch_shapes=[pltpu.VMEM((width, 2 * many * hid), BF)],
        compiler_params=params(58),
        cost_estimate=cost(4 * tokens * width * experts * hid, 12 * tokens * width, last),
        name="expert_acts",
    )(mixed, low, gates, w_gate, w_up, *after)


def fill(held, weight):
    experts, _, hid = weight.shape
    for expert in range(experts):
        held[:, expert * hid : (expert + 1) * hid] = weight[expert]


def back_columns_kernel(rows, count, extra, after, table_ref, rank_ref, *refs):
    lefts, weights = refs[:count], refs[count : 2 * count]
    more = refs[2 * count : 2 * count + extra]
    refs = refs[2 * count + extra + after :]
    outs, held = refs[:-count], refs[-count:]
    step = pl.program_id(0)
    for index in range(count):
        fill(held[index], weights[index])
    places = [out.at[part] for out in outs for part in range(out.shape[0])]
    for number, out_ref in enumerate(places):

        @pl.when(step == number)
        def _(out_ref=out_ref):
            def body(index, carry):
                here = pl.ds(pl.multiple_of(index * rows, rows), rows)
                total = dot(lefts[0][here, :], held[0][...], 1, 1)
                for left, right in zip(lefts[1:], held[1:]):
                    total = total + dot(left[here, :], right[...], 1, 1)
                out_ref[here, :] = total
                return carry

            lax.fori_loop(0, out_ref.shape[0] // rows, body, 0)
            for added in more:
                own = added.shape[0]
                out_ref[pl.ds(pl.multiple_of(rank_ref[0] * own, own), own), :] += added[...]


def back_columns(
    lefts, weights, table, groups, after=(), last=False, rank=None, added=(), chunk=0
):
    rank = jnp.zeros((1,), jnp.int32) if rank is None else rank.reshape(1)
    table = table[jnp.array([k for group in groups for k in group], jnp.int32)]
    tokens = lefts[0].shape[0]
    experts, width, hid = weights[0].shape
    count, parts = len(lefts), table.shape[0]
    block = width // parts
    return pl.pallas_call(
        functools.partial(
            back_columns_kernel, min(512, tokens), count, len(added), len(after)
        ),
        grid_spec=pltpu.PrefetchScalarGridSpec(
            num_scalar_prefetch=2,
            grid=(parts,),
            in_specs=[whole_spec(left.shape) for left in lefts]
            + [pl.BlockSpec((experts, block, hid), lambda d, table, _: (0, table[d], 0))] * count
            + [
                pl.BlockSpec((tokens // parts, block), lambda d, table, _: (chunk, table[d]))
                for item in added
            ]
            + [ANY] * len(after),
            out_specs=[whole_spec((len(group), tokens, block)) for group in groups],
            scratch_shapes=[pltpu.VMEM((block, experts * hid), BF)] * count,
        ),
        out_shape=[jax.ShapeDtypeStruct((len(group), tokens, block), F32) for group in groups],
        compiler_params=params(58),
        cost_estimate=cost(
            2 * count * tokens * width * experts * hid, (4 + 4 * count) * tokens * width, last
        ),
        name="back_columns",
    )(table, rank, *lefts, *weights, *added, *after)


def back_rows_kernel(rows, count, after, table_ref, *refs):
    lefts, weights, dots_ref = refs[:count], refs[count : 2 * count], refs[2 * count]
    refs = refs[2 * count + 1 + after :]
    outs, held, turned = refs[:-2], refs[-2], refs[-1]
    outs = [out.at[part] for out in outs for part in range(out.shape[0])]
    part_rows = outs[0].shape[0]
    deep = held.shape[1] // count
    experts, _, hid = weights[0].shape
    last = pl.num_programs(0) - 1

    @pl.when(pl.program_id(0) == 0)
    def _():
        for number in range(len(outs)):
            here = pl.ds(pl.multiple_of(table_ref[number] * part_rows, part_rows), part_rows)
            there = slice(number * part_rows, (number + 1) * part_rows)
            for index in range(count):
                turned[there, index * deep : (index + 1) * deep] = lefts[index][here, :]

    @pl.when(pl.program_id(0) < last)
    def _():
        for index in range(count):
            for expert in range(experts):
                place = index * deep + expert * hid
                held[:, place : place + hid] = weights[index][expert]
        for step in range(len(outs) * part_rows // rows):
            total = dot(turned[step * rows : (step + 1) * rows, :], held[...], 1, 1)
            for part in range(rows // part_rows):
                number = step * (rows // part_rows) + part
                outs[number][...] = total[part * part_rows : (part + 1) * part_rows]

    @pl.when(pl.program_id(0) == last)
    def _():
        for number in range(len(outs)):
            here = pl.ds(pl.multiple_of(table_ref[number] * part_rows, part_rows), part_rows)
            outs[number][:, :LANES] = dots_ref[here, :]


def back_rows(lefts, weights, dots, table, groups, after=()):
    table = table[jnp.array([k for group in groups for k in group], jnp.int32)]
    tokens = lefts[0].shape[0]
    experts, width, hid = weights[0].shape
    count, parts = len(lefts), table.shape[0]
    block = min(256, width)
    part_rows = tokens // parts
    return pl.pallas_call(
        functools.partial(back_rows_kernel, min(512, tokens), count, len(after)),
        grid_spec=pltpu.PrefetchScalarGridSpec(
            num_scalar_prefetch=1,
            grid=(width // block + 1,),
            in_specs=[whole_spec(left.shape) for left in lefts]
            + [
                pl.BlockSpec(
                    (experts, block, hid),
                    lambda d, _: (0, jnp.minimum(d, width // block - 1), 0),
                )
            ]
            * count
            + [whole_spec(dots.shape)]
            + [ANY] * len(after),
            out_specs=[
                pl.BlockSpec((len(group), part_rows, block), lambda d, _: (0, 0, d))
                for group in groups
            ],
            scratch_shapes=[
                pltpu.VMEM((block, count * experts * hid), BF),
                pltpu.VMEM((tokens, count * experts * hid), BF),
            ],
        ),
        out_shape=[
            jax.ShapeDtypeStruct((len(group), part_rows, width + LANES), F32) for group in groups
        ],
        compiler_params=params(58),
        cost_estimate=cost(
            2 * count * tokens * width * experts * hid, (4 + 4 * count) * tokens * width
        ),
        name="back_rows",
    )(table, *lefts, *weights, dots, *after)


def grads_kernel(rows, chunks, after, *refs):
    lefts = refs[:chunks]
    rest = refs[chunks + after :]
    count = (len(rest) - 2 * chunks) // (chunks + 1)
    rights = [rest[c * count : (c + 1) * count] for c in range(chunks)]
    outs = rest[chunks * count : (chunks + 1) * count]
    held, turned = rest[(chunks + 1) * count : -chunks], rest[-chunks:]
    many, width, hid = outs[0].shape

    @pl.when(pl.program_id(0) == 0)
    def _():
        for chunk in range(chunks):
            wide = 256
            for start in range(0, width, wide):
                turned[chunk][start : start + wide, :] = lefts[chunk][:, start : start + wide].T

    for chunk in range(chunks):
        for index, right in enumerate(rights[chunk]):
            held[chunk][:, index * many * hid : (index + 1) * many * hid] = right[...]

    def body(index, carry):
        here = pl.ds(pl.multiple_of(index * rows, rows), rows)
        total = dot(turned[0][here, :], held[0][...])
        for chunk in range(1, chunks):
            total = total + dot(turned[chunk][here, :], held[chunk][...])
        for which, out in enumerate(outs):
            for part in range(many):
                place = (which * many + part) * hid
                out[part, here, :] = total[:, place : place + hid]
        return carry

    lax.fori_loop(0, width // rows, body, 0)


def expert_grads(lefts, rights, experts, after=()):
    chunks, count = len(rights), len(rights[0])
    tokens = rights[0][0].shape[0]
    width = lefts[0].shape[1]
    hid = rights[0][0].shape[1] // experts
    many = 2
    if len(lefts) == chunks:
        left_specs = [whole_spec(left.shape) for left in lefts]
    else:
        left_specs = [
            pl.BlockSpec(
                (tokens, width),
                lambda e, chunk=chunk: (chunk, 0),
                pipeline_mode=pl.Buffered(buffer_count=1),
            )
            for chunk in range(chunks)
        ]
        lefts = list(lefts) * chunks
    return pl.pallas_call(
        functools.partial(grads_kernel, min(512, width), chunks, len(after)),
        grid=(experts // many,),
        in_specs=left_specs
        + [ANY] * len(after)
        + [pl.BlockSpec((tokens, many * hid), lambda e: (0, e))] * (count * chunks),
        out_specs=[pl.BlockSpec((many, width, hid), lambda e: (e, 0, 0))] * count,
        out_shape=[jax.ShapeDtypeStruct((experts, width, hid), F32)] * count,
        scratch_shapes=[pltpu.VMEM((tokens, count * many * hid), BF)] * chunks
        + [pltpu.VMEM((width, tokens), BF)] * chunks,
        compiler_params=params(58),
        cost_estimate=cost(
            2 * count * chunks * tokens * width * experts * hid, 6 * count * experts * hid * width
        ),
        name="expert_grads",
    )(*lefts, *after, *[item for chunk in rights for item in chunk])


def branch_kernel(count, after, *refs):
    pieces = refs[:count]
    w_ref, x_ref, gain_ref, router_ref, kept_ref = refs[count : count + 5]
    mid_ref, mixed_ref, probs_ref, gates_ref, all_ref = refs[count + 5 + after :]
    share = pieces[0].shape[1]
    for index, piece in enumerate(pieces):
        all_ref[:, index * share : (index + 1) * share] = piece[...].astype(BF)
    middle = x_ref[...].astype(F32) + dot(all_ref[...], w_ref[...], 1, 1)
    mid_ref[...] = middle
    mid_hat = middle * norm_scale(middle)
    mixed = (mid_hat * gain_ref[...].astype(F32)).astype(BF)
    mixed_ref[...] = mixed
    logits = dot(mixed, router_ref[...])
    expo = jnp.exp(logits - jnp.max(logits, axis=1, keepdims=True))
    probs = expo / jnp.sum(expo, axis=1, keepdims=True)
    probs_ref[...] = probs
    gates_ref[...] = probs * kept_ref[...]


def branch(pieces, w_out, hidden, chunk, gain, w_router, kept, after=()):
    tokens, share = pieces[0].shape
    width, full = w_out.shape
    rows = min(256, tokens)
    steps = tokens // rows
    experts = w_router.shape[1]
    return pl.pallas_call(
        functools.partial(branch_kernel, len(pieces), len(after)),
        grid=(steps,),
        in_specs=[pl.BlockSpec((rows, share), lambda i: (i, 0))] * len(pieces)
        + [
            whole_spec(w_out.shape),
            pl.BlockSpec((rows, width), lambda i: (chunk * steps + i, 0)),
            whole_spec((1, width)),
            whole_spec(w_router.shape),
            pl.BlockSpec((rows, experts), lambda i: (chunk * steps + i, 0)),
        ]
        + [ANY] * len(after),
        out_specs=[
            pl.BlockSpec((rows, width), lambda i: (i, 0)),
            pl.BlockSpec((rows, width), lambda i: (i, 0)),
            pl.BlockSpec((rows, experts), lambda i: (i, 0)),
            pl.BlockSpec((rows, experts), lambda i: (i, 0)),
            pl.BlockSpec((rows, full), lambda i: (i, 0)),
        ],
        out_shape=[
            jax.ShapeDtypeStruct((tokens, width), F32),
            jax.ShapeDtypeStruct((tokens, width), BF),
            jax.ShapeDtypeStruct((tokens, experts), F32),
            jax.ShapeDtypeStruct((tokens, experts), F32),
            jax.ShapeDtypeStruct((tokens, full), BF),
        ],
        compiler_params=params(58),
        cost_estimate=cost(2 * tokens * width * full, 16 * tokens * width),
        name="branch",
    )(*pieces, w_out, hidden, gain.reshape(1, -1), w_router, kept, *after)


def cast_kernel(table_ref, in_ref, out_ref):
    wide = in_ref.shape[3]
    for index in range(in_ref.shape[1]):
        span = slice(index * wide, (index + 1) * wide)
        out_ref[:, span] = in_ref[0, table_ref[index]].astype(out_ref.dtype)


def cast(parts, table):
    count, blocks, rows, wide = parts.shape
    step = min(256, rows)
    per = rows // step
    return pl.pallas_call(
        cast_kernel,
        grid_spec=pltpu.PrefetchScalarGridSpec(
            num_scalar_prefetch=1,
            grid=(count, per),
            in_specs=[pl.BlockSpec((1, blocks, step, wide), lambda d, i, _: (d, 0, i, 0))],
            out_specs=pl.BlockSpec((step, blocks * wide), lambda d, i, _: (d * per + i, 0)),
        ),
        out_shape=jax.ShapeDtypeStruct((count * rows, blocks * wide), BF),
        compiler_params=params(58),
        cost_estimate=cost(0, 6 * parts.size),
        name="cast",
    )(table, parts)


def send_back_kernel(after, low_ref, w_ref, *outs):
    for number, out_ref in enumerate(outs[after:]):

        @pl.when(pl.program_id(0) == number)
        def _(out_ref=out_ref):
            out_ref[...] = dot(low_ref[...], w_ref[...]).astype(BF).astype(F32)


def send_back(low, w_out, parts, after=()):
    rows, width = low.shape
    full = w_out.shape[1]
    block = full // parts
    return pl.pallas_call(
        functools.partial(send_back_kernel, len(after)),
        grid=(parts,),
        in_specs=[whole_spec(low.shape), pl.BlockSpec((width, block), lambda k: (0, k))]
        + [ANY] * len(after),
        out_specs=[whole_spec((rows, block))] * parts,
        out_shape=[jax.ShapeDtypeStruct((rows, block), F32)] * parts,
        compiler_params=params(58),
        cost_estimate=cost(2 * rows * width * full, 2 * width * full + 8 * rows * full),
        name="send_back",
    )(low, w_out, *after)


def mid_back_kernel(counts, rank_ref, *refs):
    chunks = len(counts)
    terms, refs = refs[: sum(counts)], refs[sum(counts) :]
    by_chunk = [refs[c * 6 : (c + 1) * 6] for c in range(chunks)]
    gain_ref, in_ref, router_ref = refs[6 * chunks : 6 * chunks + 3]
    low_ref, direct_ref, sums_ref, vectors_ref = refs[6 * chunks + 3 :]
    experts = router_ref.shape[1]
    own, width = by_chunk[0][0].shape
    gain, gain_in = gain_ref[...].astype(F32), in_ref[...].astype(F32)
    gain_mid, direct_gain, router = 0.0, 0.0, 0.0
    used = 0
    for chunk in range(chunks):
        mid_ref, dy_ref, x_ref, probs_ref, kept_ref, mixed_ref = by_chunk[chunk]
        total = terms[used][0]
        for term in terms[used + 1 : used + counts[chunk]]:
            total = total + term[0]
        used += counts[chunk]
        probs = probs_ref[...]
        prob_grad = total[:, width : width + experts] * kept_ref[...]
        logit_grad = (
            probs * (prob_grad - jnp.sum(probs * prob_grad, axis=1, keepdims=True))
        ).astype(BF)
        mixed_grad = total[:, :width] + dot(logit_grad, router_ref[...], 1, 1)
        middle = mid_ref[...]
        scale = norm_scale(middle)
        hat = middle * scale
        gain_mid = gain_mid + jnp.sum(mixed_grad * hat, axis=0, keepdims=True)
        scaled = mixed_grad * gain
        grad = dy_ref[...].astype(F32) + scale * (
            scaled - hat * jnp.mean(scaled * hat, axis=1, keepdims=True)
        )
        here = slice(chunk * own, (chunk + 1) * own)
        low_ref[here, :] = grad.astype(BF)
        hidden = x_ref[...].astype(F32)
        in_scale = norm_scale(hidden)
        in_hat = hidden * in_scale
        direct = grad / (in_scale * gain_in)
        direct_ref[here, :] = direct
        sums_ref[here, :] = jnp.broadcast_to(
            jnp.sum(grad * in_hat, axis=1, keepdims=True) / in_scale, (own, LANES)
        )
        direct_gain = direct_gain + jnp.sum(direct * in_hat, axis=0, keepdims=True)
        router = router + dot(logit_grad, mixed_ref[...], 0, 0)
    vectors_ref[:experts, :] = router
    row = lax.broadcasted_iota(jnp.int32, (8, width), 0)
    vectors_ref[experts:, :] = jnp.where(
        row == 0, gain_mid, jnp.where(row == 1, direct_gain, 0.0)
    )


def mid_back(rank, shares, middle, dy, hidden, probs, kept, mixed, gain, gain_in, w_router):
    chunks = len(shares)
    own, width = shares[0][0][0].shape[1], middle[0].shape[1]
    experts = w_router.shape[1]
    parts = middle[0].shape[0] // own
    specs, arrays = [], []
    for chunk in shares:
        for array, block in chunk:
            specs.append(
                pl.BlockSpec((1,) + array.shape[1:], lambda i, _, block=block: (block, 0, 0))
            )
            arrays.append(array)
    for c in range(chunks):
        mine = pl.BlockSpec((own, width), lambda i, rank: (rank[0], 0))
        far = pl.BlockSpec((own, width), lambda i, rank, c=c: (c * parts + rank[0], 0))
        few = pl.BlockSpec((own, experts), lambda i, rank: (rank[0], 0))
        some = pl.BlockSpec((own, experts), lambda i, rank, c=c: (c * parts + rank[0], 0))
        specs += [mine, far, far, few, some, mine]
        arrays += [middle[c], dy, hidden, probs[c], kept, mixed[c]]
    rows = chunks * own
    return pl.pallas_call(
        functools.partial(mid_back_kernel, tuple(len(chunk) for chunk in shares)),
        grid_spec=pltpu.PrefetchScalarGridSpec(
            num_scalar_prefetch=1,
            grid=(1,),
            in_specs=specs
            + [whole_spec((1, width)), whole_spec((1, width)), whole_spec(w_router.shape)],
            out_specs=[
                whole_spec((rows, width)),
                whole_spec((rows, width)),
                whole_spec((rows, LANES)),
                whole_spec((experts + 8, width)),
            ],
        ),
        out_shape=[
            jax.ShapeDtypeStruct((rows, width), BF),
            jax.ShapeDtypeStruct((rows, width), F32),
            jax.ShapeDtypeStruct((rows, LANES), F32),
            jax.ShapeDtypeStruct((experts + 8, width), F32),
        ],
        compiler_params=params(58),
        cost_estimate=cost(0, 0, True),
        name="mid_back",
    )(rank.reshape(1), *arrays, gain.reshape(1, -1), gain_in.reshape(1, -1), w_router)


def outer_kernel(count, after, table_ref, columns_ref, rank_ref, left_ref, *refs):
    rights, refs = refs[:count], refs[count + after :]
    outs, held = refs[:-1], refs[-1]
    own = rights[0].shape[0]
    number = pl.program_id(0) * 2 + pl.program_id(1)

    @pl.when((number == 0) & (pl.program_id(2) == 0))
    def _():
        for index, right in enumerate(rights):
            held[index * own : (index + 1) * own, :] = right[...]

    left = left_ref[...].T
    for index, out_ref in enumerate(outs):

        @pl.when(number == index)
        def _(out_ref=out_ref):
            for part in range(out_ref.shape[0]):
                wide = out_ref.shape[2]
                place = columns_ref[(index % 2) * out_ref.shape[0] + part] * wide
                right = held[:, pl.ds(pl.multiple_of(place, LANES), wide)]
                out_ref[part] = dot(left, right)


def outer(left, rights, rank, table, columns, after=()):
    rows, width = left.shape
    count = len(rights)
    own, full = rows // count, rights[0].shape[1]
    parts, pieces = table.shape[0], columns.shape[0]
    high, wide = width // parts, full // pieces
    steps = 2 if high % (2 * LANES) == 0 else 1
    return pl.pallas_call(
        functools.partial(outer_kernel, count, len(after)),
        grid_spec=pltpu.PrefetchScalarGridSpec(
            num_scalar_prefetch=3,
            grid=(parts, 2, steps),
            in_specs=[
                pl.BlockSpec(
                    (rows, high // steps), lambda k, m, i, table, *_: (0, table[k] * steps + i)
                ),
            ]
            + [pl.BlockSpec((own, full), lambda k, m, i, t, c, rank: (rank[0], 0))] * count
            + [ANY] * len(after),
            out_specs=[
                pl.BlockSpec(
                    (pieces // 2, high // steps, wide),
                    lambda k, m, i, *_, index=index: (
                        0,
                        jnp.where(
                            k * 2 + m < index, 0, jnp.where(k * 2 + m > index, steps - 1, i)
                        ),
                        0,
                    ),
                )
                for index in range(2 * parts)
            ],
            scratch_shapes=[pltpu.VMEM((rows, full), BF)],
        ),
        out_shape=[jax.ShapeDtypeStruct((pieces // 2, high, wide), F32)] * (2 * parts),
        compiler_params=params(58),
        cost_estimate=cost(2 * width * rows * full, 4 * width * full),
        name="outer",
    )(table, columns, rank.reshape(1), left, *rights, *after)


def in_grads_kernel(count, after, table_ref, left_ref, *refs):
    rights, refs = refs[:count], refs[count + after :]
    outs, held = refs[:-1], refs[-1]
    wide = rights[0].shape[1]

    @pl.when(pl.program_id(0) == 0)
    def _():
        for index, right in enumerate(rights):
            held[:, index * wide : (index + 1) * wide] = right[...]

    for number, out_ref in enumerate(outs):

        @pl.when(pl.program_id(0) == number)
        def _(out_ref=out_ref):
            out_ref[...] = dot(left_ref[...].T, held[...])


def in_grads_of(left, rights, table, after=()):
    tokens, width = left.shape
    parts, count = table.shape[0], len(rights)
    wide = rights[0].shape[1]
    high = width // parts
    return pl.pallas_call(
        functools.partial(in_grads_kernel, count, len(after)),
        grid_spec=pltpu.PrefetchScalarGridSpec(
            num_scalar_prefetch=1,
            grid=(parts,),
            in_specs=[pl.BlockSpec((tokens, high), lambda k, table: (0, table[k]))]
            + [whole_spec(right.shape) for right in rights]
            + [ANY] * len(after),
            out_specs=[whole_spec((high, count * wide))] * parts,
            scratch_shapes=[pltpu.VMEM((tokens, count * wide), BF)],
        ),
        out_shape=[jax.ShapeDtypeStruct((high, count * wide), F32)] * parts,
        compiler_params=params(58),
        cost_estimate=cost(0, 0, True),
        name="in_grads",
    )(table, left, *rights, *after)


def plain_low(dy, w_down, chunk, tokens, after=(), last=False):
    dy = lax.slice_in_dim(dy, chunk * tokens, (chunk + 1) * tokens, axis=0)
    low = jnp.einsum("td,edh->teh", dy, w_down, preferred_element_type=F32)
    return low.reshape(tokens, -1)


def plain_acts(mixed, low, gates, w_gate, w_up, after=(), last=False):
    acts = jnp.einsum("td,edh->teh", mixed, w_gate, preferred_element_type=F32)
    ups = jnp.einsum("td,edh->teh", mixed, w_up, preferred_element_type=F32)
    gi, gg, ug, terms = expert_terms(acts, ups, low.reshape(acts.shape), gates[:, :, None])
    flat = (mixed.shape[0], -1)
    dots = jnp.pad(jnp.sum(terms, axis=2), ((0, 0), (0, LANES - gates.shape[1])))
    return gi.reshape(flat), gg.reshape(flat), ug.reshape(flat), dots


def plain_back(lefts, weights):
    experts, _, hid = weights[0].shape
    total = 0.0
    for left, weight in zip(lefts, weights):
        total = total + jnp.einsum(
            "teh,edh->td", left.reshape(-1, experts, hid), weight, preferred_element_type=F32
        )
    return total


def plain_columns(
    lefts, weights, table, groups, after=(), last=False, rank=None, added=(), chunk=0
):
    total = plain_back(lefts, weights)
    for item in added:
        own = total.shape[0] // table.shape[0]
        mine = lax.slice_in_dim(item, chunk * own, (chunk + 1) * own, axis=0)
        rows = lax.dynamic_slice_in_dim(total, rank * own, own, 0) + mine
        total = lax.dynamic_update_slice_in_dim(total, rows, rank * own, 0)
    block = total.shape[1] // table.shape[0]
    return [
        jnp.stack([lax.dynamic_slice_in_dim(total, table[k] * block, block, 1) for k in group])
        for group in groups
    ]


def plain_rows(lefts, weights, dots, table, groups, after=()):
    total = jnp.concatenate([plain_back(lefts, weights), dots], axis=1)
    block = total.shape[0] // table.shape[0]
    return [
        jnp.stack([lax.dynamic_slice_in_dim(total, table[k] * block, block, 0) for k in group])
        for group in groups
    ]


def plain_grads(lefts, rights, experts, after=()):
    left = jnp.concatenate(lefts, axis=0)
    return [
        jnp.einsum(
            "td,teh->edh",
            left,
            jnp.concatenate(parts, axis=0).reshape(left.shape[0], experts, -1),
            preferred_element_type=F32,
        )
        for parts in zip(*rights)
    ]


def bits_of(count):
    if count & (count - 1):
        raise ValueError("tensor axis")
    return [1 << bit for bit in range(count.bit_length() - 1)]


def swap(value, axis, step):
    count = lax.axis_size(axis)
    return lax.ppermute(value, axis, [(i, i ^ step) for i in range(count)])


def reduce_blocks(blocks, axis="tensor", start=1):
    blocks = list(blocks)
    live = [k for k in range(len(blocks)) if not k % start]
    for bit in bits_of(len(blocks)):
        if bit < start:
            continue
        for k in sorted((k for k in live if k & bit), reverse=True):
            blocks[k ^ bit] = blocks[k ^ bit] + swap(blocks[k], axis, bit)
        live = [k for k in live if not k & bit]
    return blocks[0]


def stage_kernel(count, parts, skip, *refs):
    terms, out = refs[:count], refs[count + skip]
    total = terms[0][...]
    for term in terms[1:]:
        total = total + term[...]
    out[...] = total


def stage(parts, terms, passes=(), after=()):
    steps = 4
    _, rows, columns = terms[0].shape
    block = pl.BlockSpec((parts, rows // steps, columns), lambda i: (0, i, 0))
    outs = pl.pallas_call(
        functools.partial(stage_kernel, len(terms), parts, len(passes) + len(after)),
        grid=(steps,),
        in_specs=[block] * len(terms) + [ANY] * (len(passes) + len(after)),
        out_specs=[block] + [ANY] * len(passes),
        out_shape=[jax.ShapeDtypeStruct((parts, rows, columns), F32)]
        + [jax.ShapeDtypeStruct(item.shape, item.dtype) for item in passes],
        input_output_aliases={len(terms) + i: 1 + i for i in range(len(passes))},
        compiler_params=params(58),
        cost_estimate=cost(0, 4 * parts * rows * columns * (len(terms) + 1)),
        name="stage",
    )(*terms, *passes, *after)
    return outs[0], outs[1:]


def tie_kernel(*refs):
    pass


def tie(values, after):
    return pl.pallas_call(
        tie_kernel,
        in_specs=[ANY] * (len(values) + len(after)),
        out_specs=[ANY] * len(values),
        out_shape=[jax.ShapeDtypeStruct(value.shape, value.dtype) for value in values],
        input_output_aliases={i: i for i in range(len(values))},
        compiler_params=params(58),
        cost_estimate=cost(0, 0, True),
        name="tie",
    )(*values, *after)


class Chain:
    groups = ((7, 3), (5, 1), (6, 2), (4, 0))

    def __init__(self, parts):
        self.first, self.second, self.six_two, self.four_zero = parts

    def send_first(self):
        self.got_first = swap(self.first, "tensor", 1)

    def send_second(self):
        self.got_second = swap(self.second, "tensor", 1)
        self.got_near = swap(self.six_two, "tensor", 2)

    def send_far(self):
        self.got_far = swap(self.four, "tensor", 4)

    def terms(self):
        return [
            (self.four_zero, 1),
            (self.got_second, 1),
            (self.got_near, 1),
            (self.got_far, 0),
        ]

    def result(self):
        return sum(array[block] for array, block in self.terms())


def odd_stage(ending, starting, passes=(), after=(), hold=False):
    if ending is not None:
        after = (*after, ending.got_far)
    passes = (*passes, starting.second)
    starting.six_two, passes = stage(
        2, (starting.six_two, starting.got_first), passes, after
    )
    starting.second = passes[-1]
    if not hold:
        starting.send_second()
    return passes[:-1]


def even_stage(middle, coming, passes=(), after=()):
    if coming is not None:
        passes = (*passes, coming.first)
    middle.four, passes = stage(
        1, (middle.four_zero, middle.got_second, middle.got_near), passes, after
    )
    middle.send_far()
    if coming is not None:
        coming.first = passes[-1]
        coming.send_first()
        passes = passes[:-1]
    return passes


def reduce_first(blocks, axis):
    return [
        item + swap(blocks[k + 1], axis, 1) if not k & 1 else item for k, item in enumerate(blocks)
    ]


def halves_order(count):
    bits = bits_of(count)
    return [
        sum(bit for bit, other in zip(bits, reversed(bits)) if m & other) for m in range(count)
    ]


def reduce_halves(low, high, axis="tensor", start=1):
    for bit in bits_of(2 * start * low.shape[0]):
        if bit < start:
            continue
        total = low + swap(high, axis, bit)
        half = total.shape[0] // 2
        low, high = total[:half], total[half:]
    return total[0]


def gather_blocks(value):
    count = lax.axis_size("tensor")
    have = {0: value}
    for bit in reversed(bits_of(count)):
        for k in sorted(have):
            have[k ^ bit] = swap(have[k], "tensor", bit)
    return [have[k] for k in range(count)]


def exchange_blocks(blocks):
    return [blocks[0]] + [swap(blocks[k], "tensor", k) for k in range(1, len(blocks))]


def small_sum(value, axis):
    for bit in bits_of(lax.axis_size(axis)):
        value = value + swap(value, axis, bit)
    return value


def on_device(
    hidden_in,
    cotangent,
    routes,
    segments,
    gain_in,
    w_query,
    w_key,
    w_value,
    w_out,
    gain_query,
    gain_key,
    gain_mid,
    w_router,
    w_gate,
    w_up,
    w_down,
):
    count = lax.axis_size("tensor")
    rank = lax.axis_index("tensor")
    dp_count = lax.axis_size("dp")
    dp_rank = lax.axis_index("dp")
    tok_rows, width = hidden_in.shape
    local_width = w_query.shape[1]
    heads_here = local_width // HEAD
    full_width = local_width * count
    share = width // count
    experts = w_gate.shape[0]
    seqs, length = segments.shape
    own = length // count
    scale = 1.0 / math.sqrt(HEAD)
    tiled = w_gate.shape[2] % LANES == 0
    acts_of = expert_acts if tiled else plain_acts
    low_of = low_grads if tiled else plain_low
    columns_of = back_columns if tiled else plain_columns
    rows_of = back_rows if tiled else plain_rows
    grads_of = expert_grads if tiled else plain_grads
    table = rank ^ jnp.arange(count, dtype=jnp.int32)
    chunks = range(seqs)

    part = width // dp_count
    w_part = lax.dynamic_slice_in_dim(w_out, dp_rank * part, part, 0).astype(F32)
    if count == 8:
        w_part = lax.all_gather(w_part, "tensor", axis=0, tiled=False)
    staged = count == 8 and seqs == 2

    in_scale = norm_scale(hidden_in.astype(F32))
    normed, query_raw, key_raw, value_low, square_sums = project(
        hidden_in, gain_in, w_query, w_key, w_value
    )
    raws = (query_raw, key_raw)
    square_sums = small_sum(square_sums, "tensor")
    angles = jnp.concatenate(
        rotary_tables(document_positions(segments).reshape(-1), HEAD), axis=1
    )
    gains_here = (gain_query.reshape(1, -1), gain_key.reshape(1, -1))
    expert_ids = jnp.arange(experts, dtype=jnp.int32)
    hits = jnp.any(routes[:, :, None] == expert_ids[None, None, :], axis=1)
    counts = hits.astype(jnp.int32)
    kept_all = hits & (jnp.cumsum(counts, axis=0, dtype=jnp.int32) - counts < CAP)
    kept_all = kept_all.astype(F32)

    query_low, key_low = [], []

    def attend_of(c, after=()):
        attended_c, query_c, key_c = attend(
            query_raw, key_raw, value_low, square_sums, gains_here, angles, segments, c, scale,
            full_width, after,
        )
        query_low.append(query_c)
        key_low.append(key_c)
        return attended_c

    pieces, low = [], []
    if staged:
        first = attend_of(0)
        near = swap(first, "tensor", 2)
        odd = [swap(first, "tensor", 1)]
        second = attend_of(1, (first,))
        near, again = tie((near, first), (odd[0], second))
        far = swap(again, "tensor", 4)
        odd.append(swap(near, "tensor", 1))
        (w_part,) = tie((w_part,), (near,))
        low.append(low_of(cotangent, w_down, 0, length, (near,)))
        low.append(low_of(cotangent, w_down, 1, length, (low[0],), True))
        w_whole = cast(lax.all_gather(w_part, "dp", axis=0, tiled=False), table)
        (far,) = tie((far,), (odd[1], low[1]))
        both = swap(far, "tensor", 2)
        odd.append(swap(far, "tensor", 1))
        both, second = tie((both, second), (odd[2],))
        odd.append(swap(both, "tensor", 1))
        even = [again, near, far, both]
        pieces.append([item for pair in zip(even, odd) for item in pair])
        near = swap(second, "tensor", 2)
        near, again = tie((near, second), (odd[3],))
        far = swap(again, "tensor", 4)
        odd = [swap(again, "tensor", 1), swap(near, "tensor", 1)]
    else:
        for c in chunks:
            pieces.append(gather_blocks(attend_of(c)))
            low.append(low_of(cotangent, w_down, c, length))
    query_low = jnp.concatenate(query_low, axis=0)
    key_low = jnp.concatenate(key_low, axis=0)
    if not staged:
        w_part = jnp.stack(gather_blocks(w_part)) if count != 8 else w_part
        w_table = jnp.arange(count, dtype=jnp.int32) if count != 8 else table
        w_whole = cast(lax.all_gather(w_part, "dp", axis=0, tiled=False), w_table)

    groups = Chain.groups if staged else tuple((k,) for k in range(count))

    def plain_reduce(parts):
        return reduce_blocks([item[0] for item in parts])

    middle, mixed, attended, probs, gates = ([] for _ in range(5))

    def forward(c, after, last=False):
        mid_c, mixed_c, probs_c, gates_c, attended_c = branch(
            pieces[c], w_whole, hidden_in, c, gain_mid, w_router, kept_all, after
        )
        middle.append(mid_c)
        mixed.append(mixed_c)
        attended.append(attended_c)
        probs.append(probs_c)
        gates.append(gates_c)
        return acts_of(mixed_c, low[c], gates[c], w_gate, w_up, (), last)

    def mixed_blocks(c, after=()):
        return rows_of(acts[c][1:3], [w_gate, w_up], acts[c][3], table, groups, after)

    def moe_of(c, after=(), last=False):
        return columns_of([acts[c][0]], [w_down], table, groups, after, last)

    def down_grads(after=()):
        return grads_of([cotangent], [a[:1] for a in acts], experts, after)[0]

    def act_grads(after=()):
        return grads_of(mixed, [a[1:3] for a in acts], experts, after)

    def rows_own(value, start=0):
        return lax.dynamic_slice_in_dim(value, start + rank * own, own, 0)

    def columns_own(value):
        return lax.dynamic_slice_in_dim(value, rank * share, share, 1)

    if staged:
        acts = [forward(0, ())]
        (far,) = tie((far,), (middle[0], odd[0], odd[1]))
        both = swap(far, "tensor", 2)
        odd.append(swap(far, "tensor", 1))
        (both,) = tie((both,), (acts[0][0], odd[2]))
        odd.append(swap(both, "tensor", 1))
        even = [again, near, far, both]
        pieces.append([item for pair in zip(even, odd) for item in pair])
        mix = [Chain(mixed_blocks(0))]
        (mix[0].first,) = tie((mix[0].first,), (odd[3],))
        mix[0].send_first()
        acts.append(forward(1, (mix[0].four_zero,), True))
        odd_stage(None, mix[0], after=(acts[1][0],))
        mix.append(Chain(mixed_blocks(1, (mix[0].six_two,))))
        even_stage(mix[0], mix[1])
        grad_down = down_grads((mix[0].four,))
        (grad_down,) = odd_stage(mix[0], mix[1], passes=(grad_down,))
    else:
        acts = []
        for c in chunks:
            acts.append(forward(c, ()))
        mixed_share = [plain_reduce(mixed_blocks(c)) for c in chunks]
        moe_share = [plain_reduce(moe_of(c)) for c in chunks]
        grad_down = down_grads()
        grad_gate, grad_up = act_grads()

    if staged:
        moe = [Chain(moe_of(0, (mix[1].six_two,)))]
        even_stage(mix[1], moe[0])
        grad_gate, grad_up = act_grads((mix[1].four,))
        grad_gate, grad_up = odd_stage(mix[1], moe[0], passes=(grad_gate, grad_up))
        mixed_terms = [item.terms() for item in mix]
    else:
        mixed_terms = [[(item[None], 0)] for item in mixed_share]

    mid_low, direct, direct_sums, vectors = mid_back(
        rank, mixed_terms, middle, cotangent, hidden_in, probs, kept_all, mixed, gain_mid,
        gain_in, w_router,
    )
    if staged:
        moe.append(Chain(moe_of(1, (mid_low,), True)))
        (mid_low,) = even_stage(moe[0], moe[1], passes=(mid_low,))
    blocks = send_back(mid_low, w_whole, count)
    attended_grad = jnp.stack(exchange_blocks(blocks))

    dp_table = dp_rank ^ jnp.arange(dp_count, dtype=jnp.int32)
    order = jnp.array(halves_order(count), jnp.int32)
    out_parts = outer(mid_low, attended, rank, dp_table, order, (blocks[0],))

    q_scaled, k_scaled, value_grad, totals, gain_parts = attend_back(
        query_low, key_low, value_low, attended_grad, raws, square_sums, gains_here, angles,
        table, segments, scale, full_width, (out_parts[0],),
    )
    if staged:
        out_high = reduce_first(out_parts[1::2], "dp")
        out_low = reduce_first(out_parts[::2], "dp")
        after = (q_scaled, out_high[0], out_high[2], out_low[0], out_low[2])
        odd_stage(moe[0], moe[1], after=after, hold=True)
    gain_parts = jnp.sum(gain_parts.reshape(seqs, 8, local_width), axis=0)
    totals = small_sum(totals, "tensor")
    query_grad, key_grad = raw_grads((q_scaled, k_scaled), raws, square_sums, totals, full_width)
    in_grads = [query_grad, key_grad, value_grad]
    weights_in = [w[None] for w in (w_query, w_key, w_value)]
    columns_in = back_columns if local_width % LANES == 0 and share % LANES == 0 else plain_columns

    def normed_blocks(c):
        part_grads = [grad[c * length : (c + 1) * length] for grad in in_grads]
        return columns_in(
            part_grads, weights_in, table, groups, rank=rank, added=(direct,), chunk=c
        )

    if staged:
        moe[1].second, moe[1].six_two = tie((moe[1].second, moe[1].six_two), (totals,))
        moe[1].send_second()
        norm = [Chain(normed_blocks(c)) for c in chunks]
        even_stage(moe[1], norm[0], after=(norm[1].four_zero,))
        grad_in = in_grads_of(normed, in_grads, dp_table, (moe[1].four,))
        grad_in = reduce_first(grad_in, "dp")
        odd_stage(moe[1], norm[0], after=(grad_in[0], grad_in[2]))
        even_stage(norm[0], norm[1])
        out_high = reduce_blocks(out_high, "dp", 2)
        odd_stage(norm[0], norm[1], after=(out_high,))
        out_low = reduce_blocks(out_low, "dp", 2)
        grad_in = reduce_blocks(grad_in, "dp", 2)
        (out_high,) = even_stage(norm[1], None, passes=(out_high,), after=(out_low, grad_in))
        grad_w_out = reduce_halves(out_low, out_high)
        normed_share = [item.result() for item in norm]
        moe_share = [item.result() for item in moe]
    else:
        normed_share = [plain_reduce(normed_blocks(c)) for c in chunks]
        out_low = reduce_blocks(out_parts[::2], "dp")
        out_high = reduce_blocks(out_parts[1::2], "dp")
        grad_in = dot(normed, jnp.concatenate(in_grads, axis=1), 0, 0)
        grad_in = reduce_blocks(
            [
                lax.dynamic_slice_in_dim(grad_in, dp_table[k] * part, part, 0)
                for k in range(dp_count)
            ],
            "dp",
        )
        grad_w_out = reduce_halves(out_low, out_high)
    output = jnp.concatenate(
        [(columns_own(middle[c]) + moe_share[c]).astype(BF) for c in chunks], axis=0
    )

    def over_dp(grad):
        return lax.psum_scatter(grad, "dp", scatter_dimension=0, tiled=True)

    grad_w_query, grad_w_key, grad_w_value = (
        grad_in[:, i * local_width : (i + 1) * local_width] for i in range(3)
    )

    normed_share = jnp.concatenate(normed_share, axis=0)
    in_hat_share = columns_own(hidden_in).astype(F32) * in_scale
    gain_share = lax.dynamic_slice_in_dim(gain_in.astype(F32), rank * share, share, 0)
    in_scaled = normed_share * gain_share
    row_sums = jnp.sum(in_scaled * in_hat_share, axis=1).reshape(seqs, length)
    mine = lax.dynamic_slice_in_dim(row_sums, rank * own, own, 1)
    mine = mine - direct_sums[:, 0].reshape(seqs, own)
    row_sums = lax.dynamic_update_slice_in_dim(row_sums, mine, rank * own, 1)
    wide = small_sum(vectors, "dp")
    direct_gain = wide[experts + 1]
    wide = lax.dynamic_slice_in_dim(wide[: experts + 1], dp_rank * part, part, 1)
    flat = [row_sums.reshape(-1), wide.reshape(-1), direct_gain]
    flat = small_sum(jnp.concatenate(flat)[None], "tensor")[0]
    row_totals = flat[:tok_rows]
    wide = flat[tok_rows : tok_rows + wide.size].reshape(wide.shape)
    direct_gain = lax.dynamic_slice_in_dim(flat[-width:], rank * share, share, 0)
    grad_input = (
        in_scale * (in_scaled - in_hat_share * (row_totals / width)[:, None])
    ).astype(BF)
    grad_gain_in = jnp.sum(normed_share * in_hat_share, axis=0)
    gains = jnp.concatenate([grad_gain_in, gain_parts[0], gain_parts[1]])
    gains = small_sum(gains[None], "dp")[0]

    return (
        output,
        grad_input,
        grad_w_query,
        grad_w_key,
        grad_w_value,
        grad_w_out,
        gains[:share] - direct_gain,
        gains[share : share + local_width],
        gains[share + local_width :],
        wide[experts],
        wide[:experts].T,
        over_dp(grad_gate),
        over_dp(grad_up),
        over_dp(grad_down),
    )


def solution(mesh):
    in_specs = (
        P("dp", None),
        P("dp", None),
        P("dp", None),
        P("dp", None),
        P(),
        P(None, "tensor"),
        P(None, "tensor"),
        P(None, "tensor"),
        P(None, "tensor"),
        P("tensor"),
        P("tensor"),
        P(),
        P(),
        P(None, None, "tensor"),
        P(None, None, "tensor"),
        P(None, None, "tensor"),
    )
    out_specs = (
        P("dp", "tensor"),
        P("dp", "tensor"),
        P("dp", "tensor"),
        P("dp", "tensor"),
        P("dp", "tensor"),
        P("dp", "tensor"),
        P("tensor"),
        P("tensor"),
        P("tensor"),
        P("dp"),
        P("dp", None),
        P("dp", None, "tensor"),
        P("dp", None, "tensor"),
        P("dp", None, "tensor"),
    )
    return jax.shard_map(
        on_device, mesh=mesh, in_specs=in_specs, out_specs=out_specs, check_vma=False
    )
```

```python
import functools
import math

import jax
import jax.numpy as jnp
from jax import lax
from jax.experimental import pallas as pl
from jax.experimental.pallas import tpu as pltpu
from jax.sharding import PartitionSpec as P

HEAD = 128
CAP = 1280
LONGEST = 512
EPSILON = 1e-05
MASKED = -1e30
LANES = 128
MIB = 1 << 20
BF = jnp.bfloat16
F32 = jnp.float32


ANY = pl.BlockSpec(memory_space=pl.ANY)


def norm_scale(values):
    return lax.rsqrt(jnp.mean(values * values, axis=-1, keepdims=True) + EPSILON)


def document_positions(segments):
    index = jnp.broadcast_to(
        jnp.arange(segments.shape[1], dtype=jnp.int32)[None, :], segments.shape
    )
    previous = jnp.concatenate([segments[:, :1] - 1, segments[:, :-1]], axis=1)
    starts = lax.cummax(jnp.where(segments != previous, index, 0), axis=1)
    return index - starts


def rotary_tables(positions, head):
    half = head // 2
    freq = 10000.0 ** (-2.0 * jnp.arange(half, dtype=F32) / head)
    angle = positions.astype(F32)[:, None] * freq[None, :]
    return (jnp.cos(angle), jnp.sin(angle))


def dot(left, right, left_dim=1, right_dim=0):
    return lax.dot_general(
        left, right, (((left_dim,), (right_dim,)), ((), ())), preferred_element_type=F32
    )


def whole_spec(shape):
    return pl.BlockSpec(
        shape, lambda *_: (0,) * len(shape), pipeline_mode=pl.Buffered(buffer_count=1)
    )


def params(mib):
    return pltpu.CompilerParams(vmem_limit_bytes=mib * MIB)


def cost(flops, moved, last=False):
    if last:
        flops, moved = 1024, 1024
    return pl.CostEstimate(flops=int(flops), bytes_accessed=int(moved), transcendentals=0)


def across_lanes(row):
    return jnp.broadcast_to(row, (LANES, row.shape[1])).T


def along_lanes(column):
    return jnp.broadcast_to(column, (column.shape[0], LANES)).T[:8]


def project_kernel(x_ref, gain_ref, wq_ref, wk_ref, wv_ref, n_ref, q_ref, k_ref, v_ref, sums_ref):
    x = x_ref[...].astype(F32)
    normed = (x * norm_scale(x) * gain_ref[...].astype(F32)).astype(BF)
    n_ref[...] = normed
    query = dot(normed, wq_ref[...])
    key = dot(normed, wk_ref[...])
    q_ref[...] = query
    k_ref[...] = key
    v_ref[...] = dot(normed, wv_ref[...]).astype(BF)
    q_sum = along_lanes(jnp.sum(query * query, axis=1, keepdims=True))
    k_sum = along_lanes(jnp.sum(key * key, axis=1, keepdims=True))
    first = lax.broadcasted_iota(jnp.int32, q_sum.shape, 0) == 0
    sums_ref[...] = jnp.where(first, q_sum, k_sum)


def project(hidden, gain, w_query, w_key, w_value):
    tokens, width = hidden.shape
    wide = w_query.shape[1]
    rows = min(256, tokens)
    out = pl.BlockSpec((rows, wide), lambda i: (i, 0))
    return pl.pallas_call(
        project_kernel,
        grid=(tokens // rows,),
        in_specs=[pl.BlockSpec((rows, width), lambda i: (i, 0)), whole_spec((1, width))]
        + [whole_spec(w_query.shape)] * 3,
        out_specs=[
            pl.BlockSpec((rows, width), lambda i: (i, 0)),
            out,
            out,
            out,
            pl.BlockSpec((8, rows), lambda i: (0, i)),
        ],
        out_shape=[
            jax.ShapeDtypeStruct((tokens, width), BF),
            jax.ShapeDtypeStruct((tokens, wide), F32),
            jax.ShapeDtypeStruct((tokens, wide), F32),
            jax.ShapeDtypeStruct((tokens, wide), BF),
            jax.ShapeDtypeStruct((8, tokens), F32),
        ],
        compiler_params=params(58),
        cost_estimate=cost(6 * tokens * width * wide, 4 * tokens * width),
        name="project",
    )(hidden, gain.reshape(1, -1), w_query, w_key, w_value)


def key_span(block, rows):
    start = max(0, block * rows - LONGEST)
    return start, (block + 1) * rows


def masked_scores(q_rows, k_rows, seg_col, seg_row, row0, key0, scale):
    scores = dot(q_rows, k_rows, 1, 1) * scale
    row = lax.broadcasted_iota(jnp.int32, scores.shape, 0) + row0
    key = lax.broadcasted_iota(jnp.int32, scores.shape, 1) + key0
    return jnp.where((seg_col == seg_row) & (row >= key), scores, MASKED)


def both_halves(angles):
    other = pltpu.roll(angles, HEAD // 2, 1)
    low = lax.broadcasted_iota(jnp.int32, angles.shape, 1) < HEAD // 2
    return jnp.where(low, angles, other), jnp.where(low, -other, angles)


def turn(values, cosine, sine):
    return values * cosine + pltpu.roll(values, HEAD // 2, 1) * sine


def hat_scale(sums_ref, which, full):
    return lax.rsqrt(across_lanes(sums_ref[which : which + 1, :]) / full + EPSILON)


def attend_kernel(
    scale,
    block,
    full,
    after,
    q_ref,
    k_ref,
    v_ref,
    sums_ref,
    gq_ref,
    gk_ref,
    angle_ref,
    col_ref,
    row_ref,
    *refs,
):
    out_ref, ql_ref, kl_ref = refs[after:]
    length = q_ref.shape[0]
    cosine, sine = both_halves(angle_ref[...])
    for raw, which, gain, low in ((q_ref, 0, gq_ref, ql_ref), (k_ref, 1, gk_ref, kl_ref)):
        hat = raw[...] * hat_scale(sums_ref, which, full)
        low[...] = turn(hat * gain[...].astype(F32), cosine, sine).astype(BF)
    for index in range(length // block):
        start, stop = key_span(index, block)
        rows = slice(index * block, (index + 1) * block)
        scores = masked_scores(
            ql_ref[rows, :],
            kl_ref[start:stop, :],
            col_ref[rows, :],
            row_ref[0, :, start:stop],
            index * block,
            start,
            scale,
        )
        expo = jnp.exp(scores - jnp.max(scores, axis=1, keepdims=True))
        weights = (expo / jnp.sum(expo, axis=1, keepdims=True)).astype(BF)
        out_ref[rows, :] = dot(weights, v_ref[start:stop, :]).astype(BF).astype(F32)


def attend(q, k, v, sums, gains, angles, segments, chunk, scale, full, after=()):
    seqs, length = segments.shape
    heads = q.shape[1] // HEAD
    block = pl.BlockSpec((length, HEAD), lambda head: (chunk, head))
    mine = pl.BlockSpec((length, HEAD), lambda head: (0, head))
    gain = pl.BlockSpec((1, HEAD), lambda head: (0, head))
    work = heads * length * length * HEAD
    return pl.pallas_call(
        functools.partial(attend_kernel, scale, min(256, length), full, len(after)),
        grid=(heads,),
        in_specs=[
            block,
            block,
            block,
            pl.BlockSpec((8, length), lambda head: (0, chunk)),
            gain,
            gain,
            pl.BlockSpec((length, HEAD), lambda head: (chunk, 0)),
            pl.BlockSpec((length, 1), lambda head: (chunk, 0)),
            pl.BlockSpec((1, 1, length), lambda head: (chunk, 0, 0)),
        ]
        + [ANY] * len(after),
        out_specs=[mine] * 3,
        out_shape=[jax.ShapeDtypeStruct((length, q.shape[1]), kind) for kind in (F32, BF, BF)],
        compiler_params=params(58),
        cost_estimate=cost(64 * work, length * heads * HEAD * 22),
        name="attend",
    )(q, k, v, sums, *gains, angles, segments.reshape(-1, 1), segments[:, None, :], *after)


def attend_back_kernel(
    scale,
    block,
    full,
    after,
    place_ref,
    q_ref,
    k_ref,
    v_ref,
    grad_ref,
    qr_ref,
    kr_ref,
    sums_ref,
    gq_ref,
    gk_ref,
    angle_ref,
    col_ref,
    row_ref,
    *refs,
):
    qs_ref, ks_ref, dv_out, totals_ref, gains_ref, g_ref, dq_ref, dk_ref, dv_ref = refs[after:]
    length = q_ref.shape[0]
    parts, part_rows, _ = grad_ref.shape
    for part in range(parts):
        here = slice(part * part_rows, (part + 1) * part_rows)
        g_ref[here, :] = grad_ref[place_ref[part]].astype(BF)
    dk_ref[...] = jnp.zeros_like(dk_ref)
    dv_ref[...] = jnp.zeros_like(dv_ref)
    for index in range(length // block):
        start, stop = key_span(index, block)
        rows = slice(index * block, (index + 1) * block)
        q_rows = q_ref[rows, :]
        g_rows = g_ref[rows, :]
        k_rows = k_ref[start:stop, :]
        scores = masked_scores(
            q_rows, k_rows, col_ref[rows, :], row_ref[0, :, start:stop], index * block, start, scale
        )
        expo = jnp.exp(scores - jnp.max(scores, axis=1, keepdims=True))
        probs = expo / jnp.sum(expo, axis=1, keepdims=True)
        weight_grad = dot(g_rows, v_ref[start:stop, :], 1, 1)
        delta = jnp.sum(probs * weight_grad, axis=1, keepdims=True)
        score_grad = (probs * (weight_grad - delta)).astype(BF)
        dv_ref[start:stop, :] += dot(probs.astype(BF), g_rows, 0, 0)
        dk_ref[start:stop, :] += dot(score_grad, q_rows, 0, 0) * scale
        dq_ref[rows, :] = dot(score_grad, k_rows) * scale
    dv_out[...] = dv_ref[...].astype(BF)
    cosine, sine = both_halves(angle_ref[...])
    sums, gains = [], []
    for grad, raw, which, gain, out in (
        (dq_ref, qr_ref, 0, gq_ref, qs_ref),
        (dk_ref, kr_ref, 1, gk_ref, ks_ref),
    ):
        norm_grad = turn(grad[...], cosine, -sine)
        hat = raw[...] * hat_scale(sums_ref, which, full)
        gains.append(jnp.sum(norm_grad * hat, axis=0, keepdims=True))
        scaled = norm_grad * gain[...].astype(F32)
        out[...] = scaled
        sums.append(along_lanes(jnp.sum(scaled * hat, axis=1, keepdims=True)))
    first = lax.broadcasted_iota(jnp.int32, sums[0].shape, 0) == 0
    total = jnp.where(first, sums[0], sums[1])
    if_first = pl.program_id(1) == 0
    totals_ref[...] = jnp.where(if_first, total, totals_ref[...] + total)
    row = lax.broadcasted_iota(jnp.int32, gains_ref.shape, 0)
    gains_ref[...] = jnp.where(row == 0, gains[0], jnp.where(row == 1, gains[1], 0.0))


def attend_back(
    q, k, v, grad, raws, sums, gains, angles, place, segments, scale, full, after=()
):
    seqs, length = segments.shape
    heads = q.shape[1] // HEAD
    block = pl.BlockSpec((length, HEAD), lambda seq, head, _: (seq, head))
    gain = pl.BlockSpec((1, HEAD), lambda seq, head, _: (0, head))
    line = pl.BlockSpec((8, length), lambda seq, head, _: (0, seq))
    work = seqs * heads * length * length * HEAD
    return pl.pallas_call(
        functools.partial(attend_back_kernel, scale, min(256, length), full, len(after)),
        grid_spec=pltpu.PrefetchScalarGridSpec(
            num_scalar_prefetch=1,
            grid=(seqs, heads),
            in_specs=[
                block,
                block,
                block,
                pl.BlockSpec(
                    (grad.shape[0], grad.shape[1] // seqs, HEAD),
                    lambda seq, head, _: (0, seq, head),
                ),
                block,
                block,
                line,
                gain,
                gain,
                pl.BlockSpec((length, HEAD), lambda seq, head, _: (seq, 0)),
                pl.BlockSpec((length, 1), lambda seq, head, _: (seq, 0)),
                pl.BlockSpec((1, 1, length), lambda seq, head, _: (seq, 0, 0)),
            ]
            + [ANY] * len(after),
            out_specs=[
                block,
                block,
                block,
                line,
                pl.BlockSpec((8, HEAD), lambda seq, head, _: (seq, head)),
            ],
            scratch_shapes=[pltpu.VMEM((length, HEAD), BF)]
            + [pltpu.VMEM((length, HEAD), F32)] * 3,
        ),
        out_shape=[
            jax.ShapeDtypeStruct(q.shape, F32),
            jax.ShapeDtypeStruct(q.shape, F32),
            jax.ShapeDtypeStruct(q.shape, BF),
            jax.ShapeDtypeStruct((8, q.shape[0]), F32),
            jax.ShapeDtypeStruct((8 * seqs, q.shape[1]), F32),
        ],
        compiler_params=params(58),
        cost_estimate=cost(10 * work, q.size * 30),
        name="attend_back",
    )(
        place,
        q,
        k,
        v,
        grad,
        *raws,
        sums,
        *gains,
        angles,
        segments.reshape(-1, 1),
        segments[:, None, :],
        *after,
    )


def raw_grads_kernel(full, qs_ref, ks_ref, qr_ref, kr_ref, sums_ref, totals_ref, dq_ref, dk_ref):
    for which, scaled, raw, out in ((0, qs_ref, qr_ref, dq_ref), (1, ks_ref, kr_ref, dk_ref)):
        scale = hat_scale(sums_ref, which, full)
        total = across_lanes(totals_ref[which : which + 1, :]) / full
        out[...] = (scale * (scaled[...] - raw[...] * scale * total)).astype(BF)


def raw_grads(scaled, raws, sums, totals, full):
    tokens, wide = raws[0].shape
    rows = min(512, tokens)
    block = pl.BlockSpec((rows, HEAD), lambda i, head: (i, head))
    line = pl.BlockSpec((8, rows), lambda i, head: (0, i))
    return pl.pallas_call(
        functools.partial(raw_grads_kernel, full),
        grid=(tokens // rows, wide // HEAD),
        in_specs=[block] * 4 + [line] * 2,
        out_specs=[block] * 2,
        out_shape=[jax.ShapeDtypeStruct((tokens, wide), BF)] * 2,
        compiler_params=params(58),
        cost_estimate=cost(0, 20 * tokens * wide),
        name="raw_grads",
    )(*scaled, *raws, sums, totals)


def expert_terms(gate_act, up_act, low_grad, gate):
    sigmoid = 0.5 * jnp.tanh(0.5 * gate_act) + 0.5
    silu = gate_act * sigmoid
    inner = (silu * up_act).astype(BF).astype(F32)
    inner_grad = low_grad * gate
    gate_grad = inner_grad * up_act * (sigmoid + silu * (1.0 - sigmoid))
    return (
        (inner * gate).astype(BF),
        gate_grad.astype(BF),
        (inner_grad * silu).astype(BF),
        inner * low_grad,
    )


def low_kernel(rows, after, dy_ref, wd_ref, *refs):
    out_ref, down = refs[after:]
    many, _, hid = wd_ref.shape
    for part in range(many):
        down[:, part * hid : (part + 1) * hid] = wd_ref[part]

    def body(index, carry):
        here = pl.ds(pl.multiple_of(index * rows, rows), rows)
        out_ref[here, :] = dot(dy_ref[here, :], down[...])
        return carry

    lax.fori_loop(0, dy_ref.shape[0] // rows, body, 0)


def low_grads(dy, w_down, chunk, tokens, after=(), last=False):
    width = dy.shape[1]
    experts, _, hid = w_down.shape
    many = 2
    return pl.pallas_call(
        functools.partial(low_kernel, min(1024, tokens), len(after)),
        grid=(experts // many,),
        in_specs=[
            pl.BlockSpec(
                (tokens, width), lambda e: (chunk, 0), pipeline_mode=pl.Buffered(buffer_count=1)
            ),
            pl.BlockSpec((many, width, hid), lambda e: (e, 0, 0)),
        ]
        + [ANY] * len(after),
        out_specs=pl.BlockSpec((tokens, many * hid), lambda e: (0, e)),
        out_shape=jax.ShapeDtypeStruct((tokens, experts * hid), F32),
        scratch_shapes=[pltpu.VMEM((width, many * hid), BF)],
        compiler_params=params(58),
        cost_estimate=cost(8 * tokens * width * experts * hid, 8 * tokens * width, last),
        name="low_grads",
    )(dy, w_down, *after)


def expert_kernel(rows, after, mixed_ref, low_ref, gates_ref, wg_ref, wu_ref, *refs):
    gi_ref, gg_ref, ug_ref, dots_ref, both = refs[after:]
    step = pl.program_id(0)
    many, _, hid = wg_ref.shape
    for part in range(many):
        both[:, part * hid : (part + 1) * hid] = wg_ref[part]
        both[:, (many + part) * hid : (many + part + 1) * hid] = wu_ref[part]

    @pl.when(step == 0)
    def _():
        dots_ref[...] = jnp.zeros_like(dots_ref)

    def body(index, carry):
        here = pl.ds(pl.multiple_of(index * rows, rows), rows)
        acts = dot(mixed_ref[here, :], both[...])
        gates = gates_ref[here, :]
        totals = dots_ref[here, :]
        lane = lax.broadcasted_iota(jnp.int32, gates.shape, 1)
        spot = lax.broadcasted_iota(jnp.int32, totals.shape, 1)
        for part in range(many):
            chosen = lane == step * many + part
            gate = jnp.sum(jnp.where(chosen, gates, 0.0), axis=1, keepdims=True)
            span = slice(part * hid, (part + 1) * hid)
            other = slice((many + part) * hid, (many + part + 1) * hid)
            gi, gg, ug, terms = expert_terms(
                acts[:, span], acts[:, other], low_ref[here, span], gate
            )
            gi_ref[here, span] = gi
            gg_ref[here, span] = gg
            ug_ref[here, span] = ug
            mine = spot == step * many + part
            totals = jnp.where(mine, jnp.sum(terms, axis=1, keepdims=True), totals)
        dots_ref[here, :] = totals
        return carry

    lax.fori_loop(0, mixed_ref.shape[0] // rows, body, 0, unroll=True)


def expert_acts(mixed, low, gates, w_gate, w_up, after=(), last=False):
    tokens, width = mixed.shape
    experts, _, hid = w_gate.shape
    many = 2
    weight = pl.BlockSpec((many, width, hid), lambda e: (e, 0, 0))
    wide = pl.BlockSpec((tokens, many * hid), lambda e: (0, e))
    wide_shape = jax.ShapeDtypeStruct((tokens, experts * hid), BF)
    return pl.pallas_call(
        functools.partial(expert_kernel, min(512, tokens), len(after)),
        grid=(experts // many,),
        in_specs=[
            whole_spec(mixed.shape),
            wide,
            whole_spec(gates.shape),
            weight,
            weight,
        ]
        + [ANY] * len(after),
        out_specs=[wide, wide, wide, whole_spec((tokens, LANES))],
        out_shape=[wide_shape, wide_shape, wide_shape, jax.ShapeDtypeStruct((tokens, LANES), F32)],
        scratch_shapes=[pltpu.VMEM((width, 2 * many * hid), BF)],
        compiler_params=params(58),
        cost_estimate=cost(4 * tokens * width * experts * hid, 12 * tokens * width, last),
        name="expert_acts",
    )(mixed, low, gates, w_gate, w_up, *after)


def fill(held, weight):
    experts, _, hid = weight.shape
    for expert in range(experts):
        held[:, expert * hid : (expert + 1) * hid] = weight[expert]


def back_columns_kernel(rows, count, extra, after, table_ref, rank_ref, *refs):
    lefts, weights = refs[:count], refs[count : 2 * count]
    more = refs[2 * count : 2 * count + extra]
    refs = refs[2 * count + extra + after :]
    outs, held = refs[:-count], refs[-count:]
    step = pl.program_id(0)
    for index in range(count):
        fill(held[index], weights[index])
    places = [out.at[part] for out in outs for part in range(out.shape[0])]
    for number, out_ref in enumerate(places):

        @pl.when(step == number)
        def _(out_ref=out_ref):
            def body(index, carry):
                here = pl.ds(pl.multiple_of(index * rows, rows), rows)
                total = dot(lefts[0][here, :], held[0][...], 1, 1)
                for left, right in zip(lefts[1:], held[1:]):
                    total = total + dot(left[here, :], right[...], 1, 1)
                out_ref[here, :] = total
                return carry

            lax.fori_loop(0, out_ref.shape[0] // rows, body, 0)
            for added in more:
                own = added.shape[0]
                out_ref[pl.ds(pl.multiple_of(rank_ref[0] * own, own), own), :] += added[...]


def back_columns(
    lefts, weights, table, groups, after=(), last=False, rank=None, added=(), chunk=0
):
    rank = jnp.zeros((1,), jnp.int32) if rank is None else rank.reshape(1)
    table = table[jnp.array([k for group in groups for k in group], jnp.int32)]
    tokens = lefts[0].shape[0]
    experts, width, hid = weights[0].shape
    count, parts = len(lefts), table.shape[0]
    block = width // parts
    return pl.pallas_call(
        functools.partial(
            back_columns_kernel, min(512, tokens), count, len(added), len(after)
        ),
        grid_spec=pltpu.PrefetchScalarGridSpec(
            num_scalar_prefetch=2,
            grid=(parts,),
            in_specs=[whole_spec(left.shape) for left in lefts]
            + [pl.BlockSpec((experts, block, hid), lambda d, table, _: (0, table[d], 0))] * count
            + [
                pl.BlockSpec((tokens // parts, block), lambda d, table, _: (chunk, table[d]))
                for item in added
            ]
            + [ANY] * len(after),
            out_specs=[whole_spec((len(group), tokens, block)) for group in groups],
            scratch_shapes=[pltpu.VMEM((block, experts * hid), BF)] * count,
        ),
        out_shape=[jax.ShapeDtypeStruct((len(group), tokens, block), F32) for group in groups],
        compiler_params=params(58),
        cost_estimate=cost(
            2 * count * tokens * width * experts * hid, (4 + 4 * count) * tokens * width, last
        ),
        name="back_columns",
    )(table, rank, *lefts, *weights, *added, *after)


def back_rows_kernel(rows, count, after, table_ref, *refs):
    lefts, weights, dots_ref = refs[:count], refs[count : 2 * count], refs[2 * count]
    refs = refs[2 * count + 1 + after :]
    outs, held, turned = refs[:-2], refs[-2], refs[-1]
    outs = [out.at[part] for out in outs for part in range(out.shape[0])]
    part_rows = outs[0].shape[0]
    deep = held.shape[1] // count
    experts, _, hid = weights[0].shape
    last = pl.num_programs(0) - 1

    @pl.when(pl.program_id(0) == 0)
    def _():
        for number in range(len(outs)):
            here = pl.ds(pl.multiple_of(table_ref[number] * part_rows, part_rows), part_rows)
            there = slice(number * part_rows, (number + 1) * part_rows)
            for index in range(count):
                turned[there, index * deep : (index + 1) * deep] = lefts[index][here, :]

    @pl.when(pl.program_id(0) < last)
    def _():
        for index in range(count):
            for expert in range(experts):
                place = index * deep + expert * hid
                held[:, place : place + hid] = weights[index][expert]
        for step in range(len(outs) * part_rows // rows):
            total = dot(turned[step * rows : (step + 1) * rows, :], held[...], 1, 1)
            for part in range(rows // part_rows):
                number = step * (rows // part_rows) + part
                outs[number][...] = total[part * part_rows : (part + 1) * part_rows]

    @pl.when(pl.program_id(0) == last)
    def _():
        for number in range(len(outs)):
            here = pl.ds(pl.multiple_of(table_ref[number] * part_rows, part_rows), part_rows)
            outs[number][:, :LANES] = dots_ref[here, :]


def back_rows(lefts, weights, dots, table, groups, after=()):
    table = table[jnp.array([k for group in groups for k in group], jnp.int32)]
    tokens = lefts[0].shape[0]
    experts, width, hid = weights[0].shape
    count, parts = len(lefts), table.shape[0]
    block = min(256, width)
    part_rows = tokens // parts
    return pl.pallas_call(
        functools.partial(back_rows_kernel, min(512, tokens), count, len(after)),
        grid_spec=pltpu.PrefetchScalarGridSpec(
            num_scalar_prefetch=1,
            grid=(width // block + 1,),
            in_specs=[whole_spec(left.shape) for left in lefts]
            + [
                pl.BlockSpec(
                    (experts, block, hid),
                    lambda d, _: (0, jnp.minimum(d, width // block - 1), 0),
                )
            ]
            * count
            + [whole_spec(dots.shape)]
            + [ANY] * len(after),
            out_specs=[
                pl.BlockSpec((len(group), part_rows, block), lambda d, _: (0, 0, d))
                for group in groups
            ],
            scratch_shapes=[
                pltpu.VMEM((block, count * experts * hid), BF),
                pltpu.VMEM((tokens, count * experts * hid), BF),
            ],
        ),
        out_shape=[
            jax.ShapeDtypeStruct((len(group), part_rows, width + LANES), F32) for group in groups
        ],
        compiler_params=params(58),
        cost_estimate=cost(
            2 * count * tokens * width * experts * hid, (4 + 4 * count) * tokens * width
        ),
        name="back_rows",
    )(table, *lefts, *weights, dots, *after)


def grads_kernel(rows, chunks, after, *refs):
    lefts = refs[:chunks]
    rest = refs[chunks + after :]
    count = (len(rest) - 2 * chunks) // (chunks + 1)
    rights = [rest[c * count : (c + 1) * count] for c in range(chunks)]
    outs = rest[chunks * count : (chunks + 1) * count]
    held, turned = rest[(chunks + 1) * count : -chunks], rest[-chunks:]
    many, width, hid = outs[0].shape

    @pl.when(pl.program_id(0) == 0)
    def _():
        for chunk in range(chunks):
            wide = 256
            for start in range(0, width, wide):
                turned[chunk][start : start + wide, :] = lefts[chunk][:, start : start + wide].T

    for chunk in range(chunks):
        for index, right in enumerate(rights[chunk]):
            held[chunk][:, index * many * hid : (index + 1) * many * hid] = right[...]

    def body(index, carry):
        here = pl.ds(pl.multiple_of(index * rows, rows), rows)
        total = dot(turned[0][here, :], held[0][...])
        for chunk in range(1, chunks):
            total = total + dot(turned[chunk][here, :], held[chunk][...])
        for which, out in enumerate(outs):
            for part in range(many):
                place = (which * many + part) * hid
                out[part, here, :] = total[:, place : place + hid]
        return carry

    lax.fori_loop(0, width // rows, body, 0)


def expert_grads(lefts, rights, experts, after=()):
    chunks, count = len(rights), len(rights[0])
    tokens = rights[0][0].shape[0]
    width = lefts[0].shape[1]
    hid = rights[0][0].shape[1] // experts
    many = 2
    if len(lefts) == chunks:
        left_specs = [whole_spec(left.shape) for left in lefts]
    else:
        left_specs = [
            pl.BlockSpec(
                (tokens, width),
                lambda e, chunk=chunk: (chunk, 0),
                pipeline_mode=pl.Buffered(buffer_count=1),
            )
            for chunk in range(chunks)
        ]
        lefts = list(lefts) * chunks
    return pl.pallas_call(
        functools.partial(grads_kernel, min(512, width), chunks, len(after)),
        grid=(experts // many,),
        in_specs=left_specs
        + [ANY] * len(after)
        + [pl.BlockSpec((tokens, many * hid), lambda e: (0, e))] * (count * chunks),
        out_specs=[pl.BlockSpec((many, width, hid), lambda e: (e, 0, 0))] * count,
        out_shape=[jax.ShapeDtypeStruct((experts, width, hid), F32)] * count,
        scratch_shapes=[pltpu.VMEM((tokens, count * many * hid), BF)] * chunks
        + [pltpu.VMEM((width, tokens), BF)] * chunks,
        compiler_params=params(58),
        cost_estimate=cost(
            2 * count * chunks * tokens * width * experts * hid, 6 * count * experts * hid * width
        ),
        name="expert_grads",
    )(*lefts, *after, *[item for chunk in rights for item in chunk])


def branch_kernel(count, after, *refs):
    pieces = refs[:count]
    w_ref, x_ref, gain_ref, router_ref, kept_ref = refs[count : count + 5]
    mid_ref, mixed_ref, probs_ref, gates_ref, all_ref = refs[count + 5 + after :]
    share = pieces[0].shape[1]
    for index, piece in enumerate(pieces):
        all_ref[:, index * share : (index + 1) * share] = piece[...].astype(BF)
    middle = x_ref[...].astype(F32) + dot(all_ref[...], w_ref[...], 1, 1)
    mid_ref[...] = middle
    mid_hat = middle * norm_scale(middle)
    mixed = (mid_hat * gain_ref[...].astype(F32)).astype(BF)
    mixed_ref[...] = mixed
    logits = dot(mixed, router_ref[...])
    expo = jnp.exp(logits - jnp.max(logits, axis=1, keepdims=True))
    probs = expo / jnp.sum(expo, axis=1, keepdims=True)
    probs_ref[...] = probs
    gates_ref[...] = probs * kept_ref[...]


def branch(pieces, w_out, hidden, chunk, gain, w_router, kept, after=()):
    tokens, share = pieces[0].shape
    width, full = w_out.shape
    rows = min(256, tokens)
    steps = tokens // rows
    experts = w_router.shape[1]
    return pl.pallas_call(
        functools.partial(branch_kernel, len(pieces), len(after)),
        grid=(steps,),
        in_specs=[pl.BlockSpec((rows, share), lambda i: (i, 0))] * len(pieces)
        + [
            whole_spec(w_out.shape),
            pl.BlockSpec((rows, width), lambda i: (chunk * steps + i, 0)),
            whole_spec((1, width)),
            whole_spec(w_router.shape),
            pl.BlockSpec((rows, experts), lambda i: (chunk * steps + i, 0)),
        ]
        + [ANY] * len(after),
        out_specs=[
            pl.BlockSpec((rows, width), lambda i: (i, 0)),
            pl.BlockSpec((rows, width), lambda i: (i, 0)),
            pl.BlockSpec((rows, experts), lambda i: (i, 0)),
            pl.BlockSpec((rows, experts), lambda i: (i, 0)),
            pl.BlockSpec((rows, full), lambda i: (i, 0)),
        ],
        out_shape=[
            jax.ShapeDtypeStruct((tokens, width), F32),
            jax.ShapeDtypeStruct((tokens, width), BF),
            jax.ShapeDtypeStruct((tokens, experts), F32),
            jax.ShapeDtypeStruct((tokens, experts), F32),
            jax.ShapeDtypeStruct((tokens, full), BF),
        ],
        compiler_params=params(58),
        cost_estimate=cost(2 * tokens * width * full, 16 * tokens * width),
        name="branch",
    )(*pieces, w_out, hidden, gain.reshape(1, -1), w_router, kept, *after)


def cast_kernel(table_ref, in_ref, out_ref):
    wide = in_ref.shape[3]
    for index in range(in_ref.shape[1]):
        span = slice(index * wide, (index + 1) * wide)
        out_ref[:, span] = in_ref[0, table_ref[index]].astype(out_ref.dtype)


def cast(parts, table):
    count, blocks, rows, wide = parts.shape
    step = min(256, rows)
    per = rows // step
    return pl.pallas_call(
        cast_kernel,
        grid_spec=pltpu.PrefetchScalarGridSpec(
            num_scalar_prefetch=1,
            grid=(count, per),
            in_specs=[pl.BlockSpec((1, blocks, step, wide), lambda d, i, _: (d, 0, i, 0))],
            out_specs=pl.BlockSpec((step, blocks * wide), lambda d, i, _: (d * per + i, 0)),
        ),
        out_shape=jax.ShapeDtypeStruct((count * rows, blocks * wide), BF),
        compiler_params=params(58),
        cost_estimate=cost(0, 6 * parts.size),
        name="cast",
    )(table, parts)


def send_back_kernel(after, low_ref, w_ref, *outs):
    for number, out_ref in enumerate(outs[after:]):

        @pl.when(pl.program_id(0) == number)
        def _(out_ref=out_ref):
            out_ref[...] = dot(low_ref[...], w_ref[...]).astype(BF).astype(F32)


def send_back(low, w_out, parts, after=()):
    rows, width = low.shape
    full = w_out.shape[1]
    block = full // parts
    return pl.pallas_call(
        functools.partial(send_back_kernel, len(after)),
        grid=(parts,),
        in_specs=[whole_spec(low.shape), pl.BlockSpec((width, block), lambda k: (0, k))]
        + [ANY] * len(after),
        out_specs=[whole_spec((rows, block))] * parts,
        out_shape=[jax.ShapeDtypeStruct((rows, block), F32)] * parts,
        compiler_params=params(58),
        cost_estimate=cost(2 * rows * width * full, 2 * width * full + 8 * rows * full),
        name="send_back",
    )(low, w_out, *after)


def mid_back_kernel(counts, rank_ref, *refs):
    chunks = len(counts)
    terms, refs = refs[: sum(counts)], refs[sum(counts) :]
    by_chunk = [refs[c * 6 : (c + 1) * 6] for c in range(chunks)]
    gain_ref, in_ref, router_ref = refs[6 * chunks : 6 * chunks + 3]
    low_ref, direct_ref, sums_ref, vectors_ref = refs[6 * chunks + 3 :]
    experts = router_ref.shape[1]
    own, width = by_chunk[0][0].shape
    gain, gain_in = gain_ref[...].astype(F32), in_ref[...].astype(F32)
    gain_mid, direct_gain, router = 0.0, 0.0, 0.0
    used = 0
    for chunk in range(chunks):
        mid_ref, dy_ref, x_ref, probs_ref, kept_ref, mixed_ref = by_chunk[chunk]
        total = terms[used][0]
        for term in terms[used + 1 : used + counts[chunk]]:
            total = total + term[0]
        used += counts[chunk]
        probs = probs_ref[...]
        prob_grad = total[:, width : width + experts] * kept_ref[...]
        logit_grad = (
            probs * (prob_grad - jnp.sum(probs * prob_grad, axis=1, keepdims=True))
        ).astype(BF)
        mixed_grad = total[:, :width] + dot(logit_grad, router_ref[...], 1, 1)
        middle = mid_ref[...]
        scale = norm_scale(middle)
        hat = middle * scale
        gain_mid = gain_mid + jnp.sum(mixed_grad * hat, axis=0, keepdims=True)
        scaled = mixed_grad * gain
        grad = dy_ref[...].astype(F32) + scale * (
            scaled - hat * jnp.mean(scaled * hat, axis=1, keepdims=True)
        )
        here = slice(chunk * own, (chunk + 1) * own)
        low_ref[here, :] = grad.astype(BF)
        hidden = x_ref[...].astype(F32)
        in_scale = norm_scale(hidden)
        in_hat = hidden * in_scale
        direct = grad / (in_scale * gain_in)
        direct_ref[here, :] = direct
        sums_ref[here, :] = jnp.broadcast_to(
            jnp.sum(grad * in_hat, axis=1, keepdims=True) / in_scale, (own, LANES)
        )
        direct_gain = direct_gain + jnp.sum(direct * in_hat, axis=0, keepdims=True)
        router = router + dot(logit_grad, mixed_ref[...], 0, 0)
    vectors_ref[:experts, :] = router
    row = lax.broadcasted_iota(jnp.int32, (8, width), 0)
    vectors_ref[experts:, :] = jnp.where(
        row == 0, gain_mid, jnp.where(row == 1, direct_gain, 0.0)
    )


def mid_back(rank, shares, middle, dy, hidden, probs, kept, mixed, gain, gain_in, w_router):
    chunks = len(shares)
    own, width = shares[0][0][0].shape[1], middle[0].shape[1]
    experts = w_router.shape[1]
    parts = middle[0].shape[0] // own
    specs, arrays = [], []
    for chunk in shares:
        for array, block in chunk:
            specs.append(
                pl.BlockSpec((1,) + array.shape[1:], lambda i, _, block=block: (block, 0, 0))
            )
            arrays.append(array)
    for c in range(chunks):
        mine = pl.BlockSpec((own, width), lambda i, rank: (rank[0], 0))
        far = pl.BlockSpec((own, width), lambda i, rank, c=c: (c * parts + rank[0], 0))
        few = pl.BlockSpec((own, experts), lambda i, rank: (rank[0], 0))
        some = pl.BlockSpec((own, experts), lambda i, rank, c=c: (c * parts + rank[0], 0))
        specs += [mine, far, far, few, some, mine]
        arrays += [middle[c], dy, hidden, probs[c], kept, mixed[c]]
    rows = chunks * own
    return pl.pallas_call(
        functools.partial(mid_back_kernel, tuple(len(chunk) for chunk in shares)),
        grid_spec=pltpu.PrefetchScalarGridSpec(
            num_scalar_prefetch=1,
            grid=(1,),
            in_specs=specs
            + [whole_spec((1, width)), whole_spec((1, width)), whole_spec(w_router.shape)],
            out_specs=[
                whole_spec((rows, width)),
                whole_spec((rows, width)),
                whole_spec((rows, LANES)),
                whole_spec((experts + 8, width)),
            ],
        ),
        out_shape=[
            jax.ShapeDtypeStruct((rows, width), BF),
            jax.ShapeDtypeStruct((rows, width), F32),
            jax.ShapeDtypeStruct((rows, LANES), F32),
            jax.ShapeDtypeStruct((experts + 8, width), F32),
        ],
        compiler_params=params(58),
        cost_estimate=cost(0, 0, True),
        name="mid_back",
    )(rank.reshape(1), *arrays, gain.reshape(1, -1), gain_in.reshape(1, -1), w_router)


def outer_kernel(count, after, table_ref, columns_ref, rank_ref, left_ref, *refs):
    rights, refs = refs[:count], refs[count + after :]
    outs, held = refs[:-1], refs[-1]
    own = rights[0].shape[0]
    number = pl.program_id(0) * 2 + pl.program_id(1)

    @pl.when((number == 0) & (pl.program_id(2) == 0))
    def _():
        for index, right in enumerate(rights):
            held[index * own : (index + 1) * own, :] = right[...]

    left = left_ref[...].T
    for index, out_ref in enumerate(outs):

        @pl.when(number == index)
        def _(out_ref=out_ref):
            for part in range(out_ref.shape[0]):
                wide = out_ref.shape[2]
                place = columns_ref[(index % 2) * out_ref.shape[0] + part] * wide
                right = held[:, pl.ds(pl.multiple_of(place, LANES), wide)]
                out_ref[part] = dot(left, right)


def outer(left, rights, rank, table, columns, after=()):
    rows, width = left.shape
    count = len(rights)
    own, full = rows // count, rights[0].shape[1]
    parts, pieces = table.shape[0], columns.shape[0]
    high, wide = width // parts, full // pieces
    steps = 2 if high % (2 * LANES) == 0 else 1
    return pl.pallas_call(
        functools.partial(outer_kernel, count, len(after)),
        grid_spec=pltpu.PrefetchScalarGridSpec(
            num_scalar_prefetch=3,
            grid=(parts, 2, steps),
            in_specs=[
                pl.BlockSpec(
                    (rows, high // steps), lambda k, m, i, table, *_: (0, table[k] * steps + i)
                ),
            ]
            + [pl.BlockSpec((own, full), lambda k, m, i, t, c, rank: (rank[0], 0))] * count
            + [ANY] * len(after),
            out_specs=[
                pl.BlockSpec(
                    (pieces // 2, high // steps, wide),
                    lambda k, m, i, *_, index=index: (
                        0,
                        jnp.where(
                            k * 2 + m < index, 0, jnp.where(k * 2 + m > index, steps - 1, i)
                        ),
                        0,
                    ),
                )
                for index in range(2 * parts)
            ],
            scratch_shapes=[pltpu.VMEM((rows, full), BF)],
        ),
        out_shape=[jax.ShapeDtypeStruct((pieces // 2, high, wide), F32)] * (2 * parts),
        compiler_params=params(58),
        cost_estimate=cost(2 * width * rows * full, 4 * width * full),
        name="outer",
    )(table, columns, rank.reshape(1), left, *rights, *after)


def in_grads_kernel(count, after, table_ref, left_ref, *refs):
    rights, refs = refs[:count], refs[count + after :]
    outs, held = refs[:-1], refs[-1]
    wide = rights[0].shape[1]

    @pl.when(pl.program_id(0) == 0)
    def _():
        for index, right in enumerate(rights):
            held[:, index * wide : (index + 1) * wide] = right[...]

    for number, out_ref in enumerate(outs):

        @pl.when(pl.program_id(0) == number)
        def _(out_ref=out_ref):
            out_ref[...] = dot(left_ref[...].T, held[...])


def in_grads_of(left, rights, table, after=()):
    tokens, width = left.shape
    parts, count = table.shape[0], len(rights)
    wide = rights[0].shape[1]
    high = width // parts
    return pl.pallas_call(
        functools.partial(in_grads_kernel, count, len(after)),
        grid_spec=pltpu.PrefetchScalarGridSpec(
            num_scalar_prefetch=1,
            grid=(parts,),
            in_specs=[pl.BlockSpec((tokens, high), lambda k, table: (0, table[k]))]
            + [whole_spec(right.shape) for right in rights]
            + [ANY] * len(after),
            out_specs=[whole_spec((high, count * wide))] * parts,
            scratch_shapes=[pltpu.VMEM((tokens, count * wide), BF)],
        ),
        out_shape=[jax.ShapeDtypeStruct((high, count * wide), F32)] * parts,
        compiler_params=params(58),
        cost_estimate=cost(0, 0, True),
        name="in_grads",
    )(table, left, *rights, *after)


def plain_low(dy, w_down, chunk, tokens, after=(), last=False):
    dy = lax.slice_in_dim(dy, chunk * tokens, (chunk + 1) * tokens, axis=0)
    low = jnp.einsum("td,edh->teh", dy, w_down, preferred_element_type=F32)
    return low.reshape(tokens, -1)


def plain_acts(mixed, low, gates, w_gate, w_up, after=(), last=False):
    acts = jnp.einsum("td,edh->teh", mixed, w_gate, preferred_element_type=F32)
    ups = jnp.einsum("td,edh->teh", mixed, w_up, preferred_element_type=F32)
    gi, gg, ug, terms = expert_terms(acts, ups, low.reshape(acts.shape), gates[:, :, None])
    flat = (mixed.shape[0], -1)
    dots = jnp.pad(jnp.sum(terms, axis=2), ((0, 0), (0, LANES - gates.shape[1])))
    return gi.reshape(flat), gg.reshape(flat), ug.reshape(flat), dots


def plain_back(lefts, weights):
    experts, _, hid = weights[0].shape
    total = 0.0
    for left, weight in zip(lefts, weights):
        total = total + jnp.einsum(
            "teh,edh->td", left.reshape(-1, experts, hid), weight, preferred_element_type=F32
        )
    return total


def plain_columns(
    lefts, weights, table, groups, after=(), last=False, rank=None, added=(), chunk=0
):
    total = plain_back(lefts, weights)
    for item in added:
        own = total.shape[0] // table.shape[0]
        mine = lax.slice_in_dim(item, chunk * own, (chunk + 1) * own, axis=0)
        rows = lax.dynamic_slice_in_dim(total, rank * own, own, 0) + mine
        total = lax.dynamic_update_slice_in_dim(total, rows, rank * own, 0)
    block = total.shape[1] // table.shape[0]
    return [
        jnp.stack([lax.dynamic_slice_in_dim(total, table[k] * block, block, 1) for k in group])
        for group in groups
    ]


def plain_rows(lefts, weights, dots, table, groups, after=()):
    total = jnp.concatenate([plain_back(lefts, weights), dots], axis=1)
    block = total.shape[0] // table.shape[0]
    return [
        jnp.stack([lax.dynamic_slice_in_dim(total, table[k] * block, block, 0) for k in group])
        for group in groups
    ]


def plain_grads(lefts, rights, experts, after=()):
    left = jnp.concatenate(lefts, axis=0)
    return [
        jnp.einsum(
            "td,teh->edh",
            left,
            jnp.concatenate(parts, axis=0).reshape(left.shape[0], experts, -1),
            preferred_element_type=F32,
        )
        for parts in zip(*rights)
    ]


def bits_of(count):
    if count & (count - 1):
        raise ValueError("tensor axis")
    return [1 << bit for bit in range(count.bit_length() - 1)]


def swap(value, axis, step):
    count = lax.axis_size(axis)
    return lax.ppermute(value, axis, [(i, i ^ step) for i in range(count)])


def reduce_blocks(blocks, axis="tensor", start=1):
    blocks = list(blocks)
    live = [k for k in range(len(blocks)) if not k % start]
    for bit in bits_of(len(blocks)):
        if bit < start:
            continue
        for k in sorted((k for k in live if k & bit), reverse=True):
            blocks[k ^ bit] = blocks[k ^ bit] + swap(blocks[k], axis, bit)
        live = [k for k in live if not k & bit]
    return blocks[0]


def stage_kernel(count, parts, skip, *refs):
    terms, out = refs[:count], refs[count + skip]
    total = terms[0][...]
    for term in terms[1:]:
        total = total + term[...]
    out[...] = total


def stage(parts, terms, passes=(), after=()):
    steps = 4
    _, rows, columns = terms[0].shape
    block = pl.BlockSpec((parts, rows // steps, columns), lambda i: (0, i, 0))
    outs = pl.pallas_call(
        functools.partial(stage_kernel, len(terms), parts, len(passes) + len(after)),
        grid=(steps,),
        in_specs=[block] * len(terms) + [ANY] * (len(passes) + len(after)),
        out_specs=[block] + [ANY] * len(passes),
        out_shape=[jax.ShapeDtypeStruct((parts, rows, columns), F32)]
        + [jax.ShapeDtypeStruct(item.shape, item.dtype) for item in passes],
        input_output_aliases={len(terms) + i: 1 + i for i in range(len(passes))},
        compiler_params=params(58),
        cost_estimate=cost(0, 4 * parts * rows * columns * (len(terms) + 1)),
        name="stage",
    )(*terms, *passes, *after)
    return outs[0], outs[1:]


def tie_kernel(*refs):
    pass


def tie(values, after):
    return pl.pallas_call(
        tie_kernel,
        in_specs=[ANY] * (len(values) + len(after)),
        out_specs=[ANY] * len(values),
        out_shape=[jax.ShapeDtypeStruct(value.shape, value.dtype) for value in values],
        input_output_aliases={i: i for i in range(len(values))},
        compiler_params=params(58),
        cost_estimate=cost(0, 0, True),
        name="tie",
    )(*values, *after)


class Chain:
    groups = ((7, 3), (5, 1), (6, 2), (4, 0))

    def __init__(self, parts):
        self.first, self.second, self.six_two, self.four_zero = parts

    def send_first(self):
        self.got_first = swap(self.first, "tensor", 1)

    def send_second(self):
        self.got_second = swap(self.second, "tensor", 1)
        self.got_near = swap(self.six_two, "tensor", 2)

    def send_far(self):
        self.got_far = swap(self.four, "tensor", 4)

    def terms(self):
        return [
            (self.four_zero, 1),
            (self.got_second, 1),
            (self.got_near, 1),
            (self.got_far, 0),
        ]

    def result(self):
        return sum(array[block] for array, block in self.terms())


def odd_stage(ending, starting, passes=(), after=(), hold=False):
    if ending is not None:
        after = (*after, ending.got_far)
    passes = (*passes, starting.second)
    starting.six_two, passes = stage(
        2, (starting.six_two, starting.got_first), passes, after
    )
    starting.second = passes[-1]
    if not hold:
        starting.send_second()
    return passes[:-1]


def even_stage(middle, coming, passes=(), after=()):
    if coming is not None:
        passes = (*passes, coming.first)
    middle.four, passes = stage(
        1, (middle.four_zero, middle.got_second, middle.got_near), passes, after
    )
    middle.send_far()
    if coming is not None:
        coming.first = passes[-1]
        coming.send_first()
        passes = passes[:-1]
    return passes


def reduce_first(blocks, axis):
    return [
        item + swap(blocks[k + 1], axis, 1) if not k & 1 else item for k, item in enumerate(blocks)
    ]


def halves_order(count):
    bits = bits_of(count)
    return [
        sum(bit for bit, other in zip(bits, reversed(bits)) if m & other) for m in range(count)
    ]


def reduce_halves(low, high, axis="tensor", start=1):
    for bit in bits_of(2 * start * low.shape[0]):
        if bit < start:
            continue
        total = low + swap(high, axis, bit)
        half = total.shape[0] // 2
        low, high = total[:half], total[half:]
    return total[0]


def gather_blocks(value):
    count = lax.axis_size("tensor")
    have = {0: value}
    for bit in reversed(bits_of(count)):
        for k in sorted(have):
            have[k ^ bit] = swap(have[k], "tensor", bit)
    return [have[k] for k in range(count)]


def exchange_blocks(blocks):
    return [blocks[0]] + [swap(blocks[k], "tensor", k) for k in range(1, len(blocks))]


def small_sum(value, axis):
    for bit in bits_of(lax.axis_size(axis)):
        value = value + swap(value, axis, bit)
    return value


def on_device(
    hidden_in,
    cotangent,
    routes,
    segments,
    gain_in,
    w_query,
    w_key,
    w_value,
    w_out,
    gain_query,
    gain_key,
    gain_mid,
    w_router,
    w_gate,
    w_up,
    w_down,
):
    count = lax.axis_size("tensor")
    rank = lax.axis_index("tensor")
    dp_count = lax.axis_size("dp")
    dp_rank = lax.axis_index("dp")
    tok_rows, width = hidden_in.shape
    local_width = w_query.shape[1]
    heads_here = local_width // HEAD
    full_width = local_width * count
    share = width // count
    experts = w_gate.shape[0]
    seqs, length = segments.shape
    own = length // count
    scale = 1.0 / math.sqrt(HEAD)
    tiled = w_gate.shape[2] % LANES == 0
    acts_of = expert_acts if tiled else plain_acts
    low_of = low_grads if tiled else plain_low
    columns_of = back_columns if tiled else plain_columns
    rows_of = back_rows if tiled else plain_rows
    grads_of = expert_grads if tiled else plain_grads
    table = rank ^ jnp.arange(count, dtype=jnp.int32)
    chunks = range(seqs)

    part = width // dp_count
    w_part = lax.dynamic_slice_in_dim(w_out, dp_rank * part, part, 0).astype(F32)
    if count == 8:
        w_part = lax.all_gather(w_part, "tensor", axis=0, tiled=False)
    staged = count == 8 and seqs == 2

    in_scale = norm_scale(hidden_in.astype(F32))
    normed, query_raw, key_raw, value_low, square_sums = project(
        hidden_in, gain_in, w_query, w_key, w_value
    )
    raws = (query_raw, key_raw)
    square_sums = small_sum(square_sums, "tensor")
    angles = jnp.concatenate(
        rotary_tables(document_positions(segments).reshape(-1), HEAD), axis=1
    )
    gains_here = (gain_query.reshape(1, -1), gain_key.reshape(1, -1))
    expert_ids = jnp.arange(experts, dtype=jnp.int32)
    hits = jnp.any(routes[:, :, None] == expert_ids[None, None, :], axis=1)
    counts = hits.astype(jnp.int32)
    kept_all = hits & (jnp.cumsum(counts, axis=0, dtype=jnp.int32) - counts < CAP)
    kept_all = kept_all.astype(F32)

    query_low, key_low = [], []

    def attend_of(c, after=()):
        attended_c, query_c, key_c = attend(
            query_raw, key_raw, value_low, square_sums, gains_here, angles, segments, c, scale,
            full_width, after,
        )
        query_low.append(query_c)
        key_low.append(key_c)
        return attended_c

    pieces, low = [], []
    if staged:
        first = attend_of(0)
        near = swap(first, "tensor", 2)
        odd = [swap(first, "tensor", 1)]
        second = attend_of(1, (first,))
        near, again = tie((near, first), (odd[0], second))
        far = swap(again, "tensor", 4)
        odd.append(swap(near, "tensor", 1))
        (w_part,) = tie((w_part,), (near,))
        low.append(low_of(cotangent, w_down, 0, length, (near,)))
        low.append(low_of(cotangent, w_down, 1, length, (low[0],), True))
        w_whole = cast(lax.all_gather(w_part, "dp", axis=0, tiled=False), table)
        (far,) = tie((far,), (odd[1], low[1]))
        both = swap(far, "tensor", 2)
        odd.append(swap(far, "tensor", 1))
        both, second = tie((both, second), (odd[2],))
        odd.append(swap(both, "tensor", 1))
        even = [again, near, far, both]
        pieces.append([item for pair in zip(even, odd) for item in pair])
        near = swap(second, "tensor", 2)
        near, again = tie((near, second), (odd[3],))
        far = swap(again, "tensor", 4)
        odd = [swap(again, "tensor", 1), swap(near, "tensor", 1)]
    else:
        for c in chunks:
            pieces.append(gather_blocks(attend_of(c)))
            low.append(low_of(cotangent, w_down, c, length))
    query_low = jnp.concatenate(query_low, axis=0)
    key_low = jnp.concatenate(key_low, axis=0)
    if not staged:
        w_part = jnp.stack(gather_blocks(w_part)) if count != 8 else w_part
        w_table = jnp.arange(count, dtype=jnp.int32) if count != 8 else table
        w_whole = cast(lax.all_gather(w_part, "dp", axis=0, tiled=False), w_table)

    groups = Chain.groups if staged else tuple((k,) for k in range(count))

    def plain_reduce(parts):
        return reduce_blocks([item[0] for item in parts])

    middle, mixed, attended, probs, gates = ([] for _ in range(5))

    def forward(c, after, last=False):
        mid_c, mixed_c, probs_c, gates_c, attended_c = branch(
            pieces[c], w_whole, hidden_in, c, gain_mid, w_router, kept_all, after
        )
        middle.append(mid_c)
        mixed.append(mixed_c)
        attended.append(attended_c)
        probs.append(probs_c)
        gates.append(gates_c)
        return acts_of(mixed_c, low[c], gates[c], w_gate, w_up, (), last)

    def mixed_blocks(c, after=()):
        return rows_of(acts[c][1:3], [w_gate, w_up], acts[c][3], table, groups, after)

    def moe_of(c, after=(), last=False):
        return columns_of([acts[c][0]], [w_down], table, groups, after, last)

    def down_grads(after=()):
        return grads_of([cotangent], [a[:1] for a in acts], experts, after)[0]

    def act_grads(after=()):
        return grads_of(mixed, [a[1:3] for a in acts], experts, after)

    def rows_own(value, start=0):
        return lax.dynamic_slice_in_dim(value, start + rank * own, own, 0)

    def columns_own(value):
        return lax.dynamic_slice_in_dim(value, rank * share, share, 1)

    if staged:
        acts = [forward(0, ())]
        (far,) = tie((far,), (middle[0], odd[0]))
        both = swap(far, "tensor", 2)
        odd.append(swap(far, "tensor", 1))
        (both,) = tie((both,), (acts[0][0], odd[1], odd[2]))
        odd.append(swap(both, "tensor", 1))
        even = [again, near, far, both]
        pieces.append([item for pair in zip(even, odd) for item in pair])
        mix = [Chain(mixed_blocks(0))]
        (mix[0].first,) = tie((mix[0].first,), (odd[3],))
        mix[0].send_first()
        acts.append(forward(1, (mix[0].four_zero,), True))
        odd_stage(None, mix[0], after=(acts[1][0],))
        mix.append(Chain(mixed_blocks(1, (mix[0].six_two,))))
        even_stage(mix[0], mix[1])
        grad_down = down_grads((mix[0].four,))
        (grad_down,) = odd_stage(mix[0], mix[1], passes=(grad_down,))
    else:
        acts = []
        for c in chunks:
            acts.append(forward(c, ()))
        mixed_share = [plain_reduce(mixed_blocks(c)) for c in chunks]
        moe_share = [plain_reduce(moe_of(c)) for c in chunks]
        grad_down = down_grads()
        grad_gate, grad_up = act_grads()

    if staged:
        moe = [Chain(moe_of(0, (mix[1].six_two,)))]
        even_stage(mix[1], moe[0])
        grad_gate, grad_up = act_grads((mix[1].four,))
        grad_gate, grad_up = odd_stage(mix[1], moe[0], passes=(grad_gate, grad_up))
        mixed_terms = [item.terms() for item in mix]
    else:
        mixed_terms = [[(item[None], 0)] for item in mixed_share]

    mid_low, direct, direct_sums, vectors = mid_back(
        rank, mixed_terms, middle, cotangent, hidden_in, probs, kept_all, mixed, gain_mid,
        gain_in, w_router,
    )
    if staged:
        moe.append(Chain(moe_of(1, (mid_low,), True)))
        (mid_low,) = even_stage(moe[0], moe[1], passes=(mid_low,))
    blocks = send_back(mid_low, w_whole, count)
    attended_grad = jnp.stack(exchange_blocks(blocks))

    dp_table = dp_rank ^ jnp.arange(dp_count, dtype=jnp.int32)
    order = jnp.array(halves_order(count), jnp.int32)
    out_parts = outer(mid_low, attended, rank, dp_table, order, (blocks[0],))

    q_scaled, k_scaled, value_grad, totals, gain_parts = attend_back(
        query_low, key_low, value_low, attended_grad, raws, square_sums, gains_here, angles,
        table, segments, scale, full_width, (out_parts[0],),
    )
    if staged:
        odd_stage(moe[0], moe[1], after=(q_scaled,), hold=True)
    gain_parts = jnp.sum(gain_parts.reshape(seqs, 8, local_width), axis=0)
    totals = small_sum(totals, "tensor")
    query_grad, key_grad = raw_grads((q_scaled, k_scaled), raws, square_sums, totals, full_width)
    in_grads = [query_grad, key_grad, value_grad]
    weights_in = [w[None] for w in (w_query, w_key, w_value)]
    columns_in = back_columns if local_width % LANES == 0 and share % LANES == 0 else plain_columns

    def normed_blocks(c):
        part_grads = [grad[c * length : (c + 1) * length] for grad in in_grads]
        return columns_in(
            part_grads, weights_in, table, groups, rank=rank, added=(direct,), chunk=c
        )

    if staged:
        moe[1].second, moe[1].six_two = tie((moe[1].second, moe[1].six_two), (totals,))
        moe[1].send_second()
        norm = [Chain(normed_blocks(c)) for c in chunks]
        even_stage(moe[1], norm[0], after=(norm[1].four_zero,))
        grad_in = in_grads_of(normed, in_grads, dp_table, (moe[1].four,))
        odd_stage(moe[1], norm[0], after=(grad_in[0],))
        even_stage(norm[0], norm[1])
        out_high = reduce_blocks(out_parts[1::2], "dp")
        odd_stage(norm[0], norm[1], after=(out_high,))
        out_low = reduce_blocks(out_parts[::2], "dp")
        grad_in = reduce_blocks(grad_in, "dp")
        (out_high,) = even_stage(norm[1], None, passes=(out_high,), after=(out_low, grad_in))
        grad_w_out = reduce_halves(out_low, out_high)
        normed_share = [item.result() for item in norm]
        moe_share = [item.result() for item in moe]
    else:
        normed_share = [plain_reduce(normed_blocks(c)) for c in chunks]
        out_low = reduce_blocks(out_parts[::2], "dp")
        out_high = reduce_blocks(out_parts[1::2], "dp")
        grad_in = dot(normed, jnp.concatenate(in_grads, axis=1), 0, 0)
        grad_in = reduce_blocks(
            [
                lax.dynamic_slice_in_dim(grad_in, dp_table[k] * part, part, 0)
                for k in range(dp_count)
            ],
            "dp",
        )
        grad_w_out = reduce_halves(out_low, out_high)
    output = jnp.concatenate(
        [(columns_own(middle[c]) + moe_share[c]).astype(BF) for c in chunks], axis=0
    )

    def over_dp(grad):
        return lax.psum_scatter(grad, "dp", scatter_dimension=0, tiled=True)

    grad_w_query, grad_w_key, grad_w_value = (
        grad_in[:, i * local_width : (i + 1) * local_width] for i in range(3)
    )

    normed_share = jnp.concatenate(normed_share, axis=0)
    in_hat_share = columns_own(hidden_in).astype(F32) * in_scale
    gain_share = lax.dynamic_slice_in_dim(gain_in.astype(F32), rank * share, share, 0)
    in_scaled = normed_share * gain_share
    row_sums = jnp.sum(in_scaled * in_hat_share, axis=1).reshape(seqs, length)
    mine = lax.dynamic_slice_in_dim(row_sums, rank * own, own, 1)
    mine = mine - direct_sums[:, 0].reshape(seqs, own)
    row_sums = lax.dynamic_update_slice_in_dim(row_sums, mine, rank * own, 1)
    wide = small_sum(vectors, "dp")
    direct_gain = wide[experts + 1]
    wide = lax.dynamic_slice_in_dim(wide[: experts + 1], dp_rank * part, part, 1)
    flat = [row_sums.reshape(-1), wide.reshape(-1), direct_gain]
    flat = small_sum(jnp.concatenate(flat)[None], "tensor")[0]
    row_totals = flat[:tok_rows]
    wide = flat[tok_rows : tok_rows + wide.size].reshape(wide.shape)
    direct_gain = lax.dynamic_slice_in_dim(flat[-width:], rank * share, share, 0)
    grad_input = (
        in_scale * (in_scaled - in_hat_share * (row_totals / width)[:, None])
    ).astype(BF)
    grad_gain_in = jnp.sum(normed_share * in_hat_share, axis=0)
    gains = jnp.concatenate([grad_gain_in, gain_parts[0], gain_parts[1]])
    gains = small_sum(gains[None], "dp")[0]

    return (
        output,
        grad_input,
        grad_w_query,
        grad_w_key,
        grad_w_value,
        grad_w_out,
        gains[:share] - direct_gain,
        gains[share : share + local_width],
        gains[share + local_width :],
        wide[experts],
        wide[:experts].T,
        over_dp(grad_gate),
        over_dp(grad_up),
        over_dp(grad_down),
    )


def solution(mesh):
    in_specs = (
        P("dp", None),
        P("dp", None),
        P("dp", None),
        P("dp", None),
        P(),
        P(None, "tensor"),
        P(None, "tensor"),
        P(None, "tensor"),
        P(None, "tensor"),
        P("tensor"),
        P("tensor"),
        P(),
        P(),
        P(None, None, "tensor"),
        P(None, None, "tensor"),
        P(None, None, "tensor"),
    )
    out_specs = (
        P("dp", "tensor"),
        P("dp", "tensor"),
        P("dp", "tensor"),
        P("dp", "tensor"),
        P("dp", "tensor"),
        P("dp", "tensor"),
        P("tensor"),
        P("tensor"),
        P("tensor"),
        P("dp"),
        P("dp", None),
        P("dp", None, "tensor"),
        P("dp", None, "tensor"),
        P("dp", None, "tensor"),
    )
    return jax.shard_map(
        on_device, mesh=mesh, in_specs=in_specs, out_specs=out_specs, check_vma=False
    )
```
